128 devices in a mesh: dp: 16 (over z, x), fsdp: 8 (over y, core).
Axes of the slice: x: 4, y: 4, z: 4, core: 2. Of those that a mesh axis runs over, the one named last changes fastest.
Arguments:
- feats: bfloat16 [256, 1024, 96], P(('dp', 'fsdp')), may hold values from -6 to 6
- targets: float32 [256, 1024], P(('dp', 'fsdp')), may hold values from -36 to 36
- lag_mask: int32 [256, 84], P(('dp', 'fsdp')), may hold values 0 or 1
- date_mask: int32 [256, 12], P(('dp', 'fsdp')), may hold values 0 or 1
- freq_ids: int32 [256], P(('dp', 'fsdp')), may hold values from 0 to 2
- dataset_ids: int32 [256], P(('dp', 'fsdp')), may hold values from 0 to 7
- w_in: bfloat16 [13824], P(('dp', 'fsdp')), may hold values from -0.625 to 0.625
- w_qkv: bfloat16 [62208], P(('dp', 'fsdp')), may hold values from -0.5 to 0.5
- w_out: bfloat16 [20736], P(('dp', 'fsdp')), may hold values from -2 to 2
- w_gu: bfloat16 [147456], P(('dp', 'fsdp')), may hold values from -0.5 to 0.5
- w_down: bfloat16 [73728], P(('dp', 'fsdp')), may hold values from -0.25 to 0.25
- gains: bfloat16 [2, 144], P(None, 'dp'), may hold values from 0.5 to 1.5
- running: float32 [8], replicated, may hold values from 0.5 to 4
- d_out: bfloat16 [256, 1024, 144], P(('dp', 'fsdp')), may hold values from -6 to 6
Outputs:
- out: bfloat16 [256, 1024, 144], P(('dp', 'fsdp'))
- grad_feats: bfloat16 [256, 1024, 96], P(('dp', 'fsdp'))
- grad_w_in: float32 [13824], P(('dp', 'fsdp'))
- grad_w_qkv: float32 [62208], P(('dp', 'fsdp'))
- grad_w_out: float32 [20736], P(('dp', 'fsdp'))
- grad_w_gu: float32 [147456], P(('dp', 'fsdp'))
- grad_w_down: float32 [73728], P(('dp', 'fsdp'))
- grad_gains: float32 [2, 144], P(None, 'dp')
- running_next: float32 [8], replicated
The draws below stay inside these ranges and needn't reach their ends.
All inputs are finite; a program needn't handle non-finite values. Where the reference program divides by a largest or mean magnitude, that divisor is 1e-20 or more. No bound on the sum of `lag_mask` or of `date_mask` on one device may be relied on, other than what follows from the above.
Results may differ from the reference program's by a relative error of at most 0.014.
Values may be sent and summed in bfloat16 or wider, within the bound.
A program may use at most 256 MiB of HBM per device.

```python
import jax
import jax.numpy as jnp
from jax import lax

D = 144
H = 9
HD = 16
FF = 512
NLAG = 84
NDATE = 12
F = 96
NSET = 8
LEN = 1024
SERIES = 256


def draw_targets(key, part):
    key = jax.random.fold_in(key, 7)
    rows = jnp.arange(SERIES, dtype=jnp.float32)[:, None]
    cols = jnp.arange(LEN, dtype=jnp.float32)[None, :]
    level = (1.0 + 2.0 * rows / max(SERIES - 1, 1)) * (1.0 + 2.0 * cols / max(LEN - 1, 1))
    base = jnp.clip(jax.random.normal(key, (SERIES, LEN), jnp.float32), -4.0, 4.0)
    return base * level


def place_ends(values, key, low, high):
    spot = [jax.random.randint(jax.random.fold_in(key, axis), (), 0, length) for axis, length in enumerate(values.shape)]
    widest = values.shape.index(max(values.shape))
    next_to = spot[:widest] + [(spot[widest] + 1) % values.shape[widest]] + spot[widest + 1:]
    return values.at[tuple(spot)].set(low).at[tuple(next_to)].set(high)


def steps_of(key, extent, pieces, smallest, largest):
    factor_of, own = 1.0, jax.random.fold_in(key, 6)
    for axis_at, shards_of in pieces:
        steps = jnp.exp(jax.random.uniform(jax.random.fold_in(own, axis_at), (shards_of,), jnp.float32, smallest / len(pieces), largest / len(pieces)))
        factor_of = factor_of * jnp.repeat(steps, extent[axis_at] // shards_of).reshape([-1 if axis == axis_at else 1 for axis in range(len(extent))])
    return factor_of


def scatter_about(key, dims, spread, bound, split=(), kind=jnp.bfloat16):
    entries = spread * jax.random.normal(key, dims, jnp.float32)
    if split:
        entries = entries * steps_of(key, dims, split, -0.22, 0.18)
    return jnp.clip(entries, -bound, bound).astype(kind)


def setup_inputs(seed: int = 0) -> dict:
    key_list = jax.random.split(jax.random.key(seed), 15)
    return {
        "feats": scatter_about(key_list[0], (SERIES, LEN, F), 1.0, 6.0, ((0, 128),)),
        "targets": draw_targets(jax.random.fold_in(key_list[14], 71), 0),
        "lag_mask": place_ends((jax.random.randint(key_list[2], (SERIES, NLAG), 0, 4) < 3).astype(jnp.int32), jax.random.fold_in(key_list[2], 1), 0, 1),
        "date_mask": place_ends((jax.random.randint(key_list[3], (SERIES, NDATE), 0, 4) < 3).astype(jnp.int32), jax.random.fold_in(key_list[3], 1), 0, 1),
        "freq_ids": place_ends(jax.random.randint(key_list[4], (SERIES,), 0, 3), jax.random.fold_in(key_list[4], 1), 0, 2).astype(jnp.int32),
        "dataset_ids": place_ends(jax.random.randint(key_list[5], (SERIES,), 0, NSET), jax.random.fold_in(key_list[5], 1), 0, NSET - 1).astype(jnp.int32),
        "w_in": scatter_about(key_list[6], (F * D,), F ** -0.5, 0.625, ((0, 128),)),
        "w_qkv": scatter_about(key_list[7], (3 * D * D,), D ** -0.5, 0.5, ((0, 128),)),
        "w_out": scatter_about(key_list[8], (D * D,), (D // 16) ** -0.5, 2.0, ((0, 128),)),
        "w_gu": scatter_about(key_list[9], (2 * D * FF,), D ** -0.5, 0.5, ((0, 128),)),
        "w_down": scatter_about(key_list[10], (FF * D,), FF ** -0.5, 0.25, ((0, 128),)),
        "gains": jnp.clip(1.0 + 0.1 * jax.random.normal(key_list[11], (2, D), jnp.float32), 0.5, 1.5).astype(jnp.bfloat16),
        "running": jnp.clip(jax.random.uniform(key_list[12], (NSET,), jnp.float32, 0.5, 4.0), 0.5, 4.0),
        "d_out": scatter_about(key_list[13], (SERIES, LEN, D), 1.0, 6.0, ((0, 128),)),
    }


norm_eps = 1e-05
scale_eps = 1e-05
momentum = 0.75
rope_base = 10000.0
series_block = 4
highest = lax.Precision.HIGHEST

@jax.custom_vjp
def low(v):
    return lax.optimization_barrier(v.astype(jnp.bfloat16)).astype(jnp.float32)

@jax.custom_vjp
def low_back(v):
    return v

def low_keep(v):
    return (low(v), None)

def low_pass(kept, grad):
    return (grad,)

def back_keep(v):
    return (v, None)

def back_low(kept, grad):
    return (low(grad),)
low.defvjp(low_keep, low_pass)
low_back.defvjp(back_keep, back_low)

def matmul(left, right):
    return jnp.einsum('...i,ij->...j', left, right, precision=highest)

def normalize(value):
    return value * lax.rsqrt(lax.optimization_barrier(jnp.mean(value * value, axis=-1, keepdims=True)) + norm_eps)

def rope_angles(start, count, head_size):
    spots = (start + jnp.arange(count, dtype=jnp.int32)).astype(jnp.float32)
    freqs = rope_base ** (-jnp.arange(head_size // 2, dtype=jnp.float32) * 2.0 / head_size)
    angle = spots[:, None] * freqs[None, :]
    return (jnp.cos(angle), jnp.sin(angle))

def rotate(value, cos_part, sin_part):
    half = value.shape[-1] // 2
    front = value[..., :half]
    back = value[..., half:]
    cos_wide = cos_part[:, None, :]
    sin_wide = sin_part[:, None, :]
    return jnp.concatenate([front * cos_wide - back * sin_wide, back * cos_wide + front * sin_wide], axis=-1)

def series_attention(query, keys, values):
    length = query.shape[0]
    scores = jnp.einsum('qhd,khd->hqk', query, keys, precision=highest) * query.shape[-1] ** (-0.5)
    scores = low_back(scores)
    spots = jnp.arange(length, dtype=jnp.int32)
    allowed = spots[None, :] <= spots[:, None]
    scores = jnp.where(allowed[None], scores, -1e+30)
    total = jax.nn.logsumexp(scores, axis=-1, keepdims=True)
    weights = low(jnp.exp(scores - total))
    return jnp.einsum('hqk,khd->qhd', weights, values, precision=highest)

def attend_item(item):
    return series_attention(item[0], item[1], item[2])

def reference(feats, targets, lag_mask, date_mask, freq_ids, dataset_ids, w_in, w_qkv, w_out, w_gu, w_down, gains, running, d_out):
    scale = lax.optimization_barrier(jnp.mean(jnp.abs(targets), axis=1)) + scale_eps
    shift_start = freq_ids * (NDATE // 3)
    keep = date_mask * (jnp.arange(NDATE, dtype=jnp.int32)[None, :] >= shift_start[:, None]).astype(jnp.int32)
    factors = jnp.concatenate([lag_mask.astype(jnp.float32) / scale[:, None], keep.astype(jnp.float32)], axis=1)
    attend = jax.checkpoint(attend_item)
    mats = (w_in.astype(jnp.float32), w_qkv.astype(jnp.float32), w_out.astype(jnp.float32), w_gu.astype(jnp.float32), w_down.astype(jnp.float32), gains.astype(jnp.float32))
    blocks = SERIES // series_block
    feats_blocks = feats.reshape(blocks, series_block, LEN, F)
    factor_blocks = factors.reshape(blocks, series_block, F)
    cot_blocks = d_out.reshape(blocks, series_block, LEN, D)

    def step(carry, item):
        inputs_block, factor_block, cot_block = item

        def layer(inputs, mat_in, mat_qkv, mat_out, mat_gu, mat_down, gain_pair):
            series, length, _ = inputs.shape
            cos_part, sin_part = rope_angles(0, length, HD)
            lifted = low(inputs * factor_block[:, None, :])
            first = low_back(matmul(lifted, mat_in.reshape(F, D)))
            normed = low(normalize(first) * gain_pair[0])
            joint = low_back(matmul(normed, mat_qkv.reshape(D, 3 * D)))
            query = low(rotate(joint[..., :D].reshape(series, length, H, HD), cos_part, sin_part))
            keys = low(rotate(joint[..., D:2 * D].reshape(series, length, H, HD), cos_part, sin_part))
            values = low(joint[..., 2 * D:].reshape(series, length, H, HD))
            mixed = lax.map(attend, (query, keys, values))
            mixed = low_back(low(mixed.reshape(series, length, D)))
            branch = low_back(matmul(mixed, mat_out.reshape(D, D)))
            middle = first + branch
            second = low(normalize(middle) * gain_pair[1])
            both = low_back(matmul(second, mat_gu.reshape(D, 2 * FF)))
            hidden = low(jax.nn.silu(both[..., :FF]) * both[..., FF:])
            return middle + low_back(matmul(hidden, mat_down.reshape(FF, D)))
        result, pullback = jax.vjp(layer, inputs_block.astype(jnp.float32), *mats)
        grads = pullback(cot_block.astype(jnp.float32))
        carry = tuple((c + g for c, g in zip(carry, grads[1:])))
        return (carry, (result.astype(jnp.bfloat16), grads[0].astype(jnp.bfloat16)))
    start = tuple((jnp.zeros_like(m) for m in mats))
    sums, (results, input_grads) = lax.scan(step, start, (feats_blocks, factor_blocks, cot_blocks))
    member = (dataset_ids[:, None] == jnp.arange(NSET, dtype=jnp.int32)[None, :]).astype(jnp.float32)
    set_sums = lax.optimization_barrier(jnp.sum(member * scale[:, None], axis=0))
    set_counts = lax.optimization_barrier(jnp.sum(member, axis=0))
    batch_mean = set_sums / jnp.maximum(set_counts, 1.0)
    running_next = jnp.where(set_counts > 0.5, momentum * running + (1.0 - momentum) * batch_mean, running)
    return (results.reshape(SERIES, LEN, D), input_grads.reshape(SERIES, LEN, F), sums[0], sums[1], sums[2], sums[3], sums[4], sums[5], running_next)
```

```python
import functools
import jax
import jax.numpy as jnp
import numpy as np
from jax import lax
from jax.experimental import pallas as pl
from jax.experimental.pallas import tpu as pltpu

D, H, HD, FF, NDATE, F, NSET, LEN = 144, 9, 16, 512, 12, 96, 8, 1024
EPS = 1e-05
TOK = 256
QT = 256
f32, bf16 = jnp.float32, jnp.bfloat16


def dot(a, b, ca=1, cb=0):
    return lax.dot_general(a, b, (((ca,), (cb,)), ((), ())), preferred_element_type=f32)


def rope_tables():
    freqs = np.float32(10000.0) ** (-np.arange(HD // 2, dtype=np.float32) * np.float32(2.0) / np.float32(HD))
    angle = np.arange(LEN, dtype=np.float32)[None, :] * freqs.astype(np.float32)[:, None]
    return np.cos(angle.astype(np.float64)).astype(np.float32), np.sin(angle.astype(np.float64)).astype(np.float32)


def main_kernel(feats, dout, fac, gains, cosr, sinr, win, wqkv, wout, wgu, wdown,
                out, gfeats, g_in, g_qkv, g_out, g_gu, g_down, g_gain,
                winT, wqkvT, woutT, wguT, wdownT,
                lifted, first, inv1, normed, q, k, v, prob, rl, osum, mixed, second, hidden, both,
                gmid, gbranch, gmixed, gjoint, gfirst):
    s = pl.program_id(0)

    @pl.when(s == 0)
    def _():
        for src, dst in ((win, winT), (wqkv, wqkvT), (wout, woutT), (wgu, wguT), (wdown, wdownT)):
            dst[...] = src[...].astype(f32).T.astype(bf16)
        for ref in (g_in, g_qkv, g_out, g_gu, g_down, g_gain):
            ref[...] = jnp.zeros_like(ref)

    gain0 = gains[:, 0:1]
    gain1 = gains[:, 1:2]
    factor = fac[0]

    @pl.loop(0, LEN // TOK)
    def _(i):
        t = pl.ds(pl.multiple_of(i * TOK, TOK), TOK)
        lift = (feats[0, :, t].astype(f32) * factor).astype(bf16)
        lifted[:, t] = lift
        x = dot(winT[...], lift)
        first[:, t] = x
        r = lax.rsqrt(jnp.mean(x * x, axis=0, keepdims=True) + EPS)
        inv1[:, t] = r
        n = (x * r * gain0).astype(bf16)
        normed[:, t] = n
        joint = dot(wqkvT[...], n).reshape(3, H, HD, TOK)
        c, sn = cosr[:, t][None], sinr[:, t][None]
        for which, ref, scale in ((0, q, 0.25), (1, k, 1.0)):
            a, b = joint[which, :, :8], joint[which, :, 8:]
            ref[:, :, t] = (jnp.concatenate([a * c - b * sn, b * c + a * sn], axis=1) * scale).astype(bf16)
        v[:, :, t] = joint[2].astype(bf16)

    diag = lax.broadcasted_iota(jnp.int32, (QT, QT), 0) <= lax.broadcasted_iota(jnp.int32, (QT, QT), 1)

    @pl.loop(0, H)
    def _(h):
        kt = k[h].astype(f32).T.astype(bf16)
        vh = v[h]
        for j in range(LEN // QT):
            n = (j + 1) * QT
            cols = pl.ds(j * QT, QT)
            sc = dot(kt[:n], q[h, :, cols])
            last = jnp.where(diag, sc[n - QT:], -1e30)
            top = jnp.max(last, axis=0, keepdims=True)
            if j:
                top = jnp.maximum(top, jnp.max(sc[:n - QT], axis=0, keepdims=True))
                p0 = jnp.exp(sc[:n - QT] - top)
            p1 = jnp.exp(last - top)
            total = jnp.sum(p1, axis=0, keepdims=True)
            if j:
                total = total + jnp.sum(p0, axis=0, keepdims=True)
                prob[h, : n - QT, cols] = p0.astype(bf16)
            prob[h, n - QT : n, cols] = p1.astype(bf16)
            o = dot(vh[:, :n], prob[h, :n, cols])
            inv = 1.0 / total
            rl[h, :, cols] = inv
            o = o * inv
            osum[h, :, cols] = o
            mixed[h, :, cols] = o.astype(bf16)

    @pl.loop(0, LEN // TOK)
    def _(i):
        t = pl.ds(pl.multiple_of(i * TOK, TOK), TOK)
        mid = first[:, t] + dot(woutT[...], mixed[:, :, t].reshape(D, TOK))
        r = lax.rsqrt(jnp.mean(mid * mid, axis=0, keepdims=True) + EPS)
        sec = (mid * r * gain1).astype(bf16)
        second[:, t] = sec
        g = dout[0, :, t]
        C = 128
        for f in range(0, FF, C):
            gate = dot(wguT[f : f + C], sec)
            up = dot(wguT[FF + f : FF + f + C], sec)
            gh = dot(wdown[f : f + C], g)
            sig = 1.0 / (1.0 + jnp.exp(-gate))
            silu = gate * sig
            hidden[f : f + C, t] = (silu * up).astype(bf16)
            both[FF + f : FF + f + C, t] = (gh * silu).astype(bf16)
            both[f : f + C, t] = (gh * up * (sig + silu * (1.0 - sig))).astype(bf16)
        out[0, :, t] = (mid + dot(wdownT[...], hidden[:, t])).astype(bf16)
        c = dot(wgu[...], both[:, t])
        cg = c * gain1
        inner = jnp.mean(cg * mid, axis=0, keepdims=True)
        gain_part = c * mid * r
        g_gain[1] += gain_part[:, :128] + gain_part[:, 128:]
        gm = g.astype(f32) + r * cg - mid * (r * r * r * inner)
        gmid[:, t] = gm
        gb = gm.astype(bf16)
        gbranch[:, t] = gb
        gmixed[:, :, t] = dot(wout[...], gb).reshape(H, HD, TOK)

    g_down[...] += dot(hidden[...], dout[0], 1, 1)
    g_gu[...] += dot(second[...], both[...], 1, 1)
    g_out[...] += dot(mixed[...].reshape(D, LEN), gbranch[...], 1, 1)

    @pl.loop(0, H)
    def _(h):
        do = (gmixed[h] * rl[h]).astype(bf16)
        delta = jnp.sum(do.astype(f32) * osum[h], axis=0, keepdims=True)
        vt = v[h].astype(f32).T.astype(bf16)
        kh = k[h]
        dk = jnp.zeros((HD, LEN), f32)
        dv = jnp.zeros((HD, LEN), f32)
        dqs = []
        for j in range(LEN // QT):
            n = (j + 1) * QT
            cols = slice(j * QT, n)
            dp = dot(vt[:n], do[:, cols])
            p = prob[h, :n, cols]
            ds = (p.astype(f32) * (dp - delta[:, cols])).astype(bf16)
            dqs.append(dot(kh[:, :n], ds))
            pad = lambda a: a if n == LEN else jnp.concatenate([a, jnp.zeros((HD, LEN - n), f32)], axis=1)
            dk += pad(dot(q[h, :, cols], ds, 1, 1))
            dv += pad(dot(do[:, cols], p, 1, 1))
        dq = jnp.concatenate(dqs, axis=1) * 0.25
        c, sn = cosr[...], sinr[...]
        for which, val in ((0, dq), (1, dk)):
            a, b = val[:8], val[8:]
            gjoint[which, h] = jnp.concatenate([a * c + b * sn, b * c - a * sn], axis=0).astype(bf16)
        gjoint[2, h] = dv.astype(bf16)

    @pl.loop(0, LEN // TOK)
    def _(i):
        t = pl.ds(pl.multiple_of(i * TOK, TOK), TOK)
        c = dot(wqkv[...], gjoint[:, :, :, t].reshape(3 * D, TOK))
        x, r = first[:, t], inv1[:, t]
        cg = c * gain0
        inner = jnp.mean(cg * x, axis=0, keepdims=True)
        gain_part = c * x * r
        g_gain[0] += gain_part[:, :128] + gain_part[:, 128:]
        gf = (gmid[:, t] + r * cg - x * (r * r * r * inner)).astype(bf16)
        gfirst[:, t] = gf
        gfeats[0, :, t] = (dot(win[...], gf) * factor).astype(bf16)

    g_qkv[...] += dot(normed[...], gjoint[...].reshape(3 * D, LEN), 1, 1)
    g_in[...] += dot(lifted[...], gfirst[...], 1, 1)


def run_main(feats_t, dout_t, fac, gains_t, mats):
    cos, sin = rope_tables()
    S = feats_t.shape[0]
    full = lambda *shape: pl.BlockSpec(shape, lambda s: (0,) * len(shape))
    per = lambda *shape: pl.BlockSpec((1,) + shape, lambda s: (s,) + (0,) * len(shape))
    sd = jax.ShapeDtypeStruct
    V = pltpu.VMEM
    return pl.pallas_call(
        main_kernel,
        grid=(S,),
        in_specs=[per(F, LEN), per(D, LEN), per(F, 1), full(D, 2), full(8, LEN), full(8, LEN),
                  full(F, D), full(D, 3 * D), full(D, D), full(D, 2 * FF), full(FF, D)],
        out_specs=[per(D, LEN), per(F, LEN), full(F, D), full(D, 3 * D), full(D, D), full(D, 2 * FF), full(FF, D),
                   full(2, D, 128)],
        out_shape=[sd((S, D, LEN), bf16), sd((S, F, LEN), bf16), sd((F, D), f32), sd((D, 3 * D), f32), sd((D, D), f32),
                   sd((D, 2 * FF), f32), sd((FF, D), f32), sd((2, D, 128), f32)],
        scratch_shapes=[
            V((D, F), bf16), V((3 * D, D), bf16), V((D, D), bf16), V((2 * FF, D), bf16), V((D, FF), bf16),
            V((F, LEN), bf16), V((D, LEN), f32), V((1, LEN), f32), V((D, LEN), bf16),
            V((H, HD, LEN), bf16), V((H, HD, LEN), bf16), V((H, HD, LEN), bf16),
            V((H, LEN, LEN), bf16), V((H, 1, LEN), f32), V((H, HD, LEN), f32), V((H, HD, LEN), bf16),
            V((D, LEN), bf16), V((FF, LEN), bf16), V((2 * FF, LEN), bf16),
            V((D, LEN), f32), V((D, LEN), bf16), V((H, HD, LEN), f32), V((3, H, HD, LEN), bf16), V((D, LEN), bf16),
        ],
        compiler_params=pltpu.CompilerParams(vmem_limit_bytes=60 * 2**20, dimension_semantics=("arbitrary",)),
    )(feats_t, dout_t, fac, gains_t, jnp.asarray(cos), jnp.asarray(sin), *mats)


SIZES = (108, 486, 162, 1152, 576)
SHAPES = ((F, D), (D, 3 * D), (D, D), (D, 2 * FF), (FF, D))
BOTH = ("dp", "fsdp")


def body(feats, targets, lag_mask, date_mask, freq_ids, dataset_ids, w_in, w_qkv, w_out, w_gu, w_down, gains, running, d_out):
    packed = jnp.concatenate([w_in, w_qkv, w_out, w_gu, w_down, gains.reshape(-1)])
    gathered = lax.all_gather(packed, BOTH, axis=0, tiled=False)
    mats, at = [], 0
    for size, shape in zip(SIZES, SHAPES):
        mats.append(gathered[:, at : at + size].reshape(shape))
        at += size
    gain_full = gathered[::8, at:].reshape(16, 2, 9).transpose(1, 0, 2).reshape(2, D).astype(f32)
    scale = jnp.mean(jnp.abs(targets), axis=1) + 1e-5
    keep = date_mask * (jnp.arange(NDATE, dtype=jnp.int32)[None, :] >= (freq_ids * (NDATE // 3))[:, None]).astype(jnp.int32)
    fac = jnp.concatenate([lag_mask.astype(f32) / scale[:, None], keep.astype(f32)], axis=1)
    member = (dataset_ids[:, None] == jnp.arange(NSET, dtype=jnp.int32)[None, :]).astype(f32)
    stats = jnp.concatenate([jnp.sum(member * scale[:, None], axis=0), jnp.sum(member, axis=0)])
    res = run_main(jnp.swapaxes(feats, 1, 2), jnp.swapaxes(d_out, 1, 2), fac[:, :, None], gain_full.T, mats)
    gain_grad = res[7].sum(-1).reshape(2, 16, 9).transpose(1, 0, 2).reshape(16, 1, 18)
    parts = [g.reshape(128, size) for g, size in zip(res[2:7], SIZES)]
    parts += [jnp.broadcast_to(gain_grad, (16, 8, 18)).reshape(128, 18), jnp.broadcast_to(stats[None], (128, 16))]
    own = lax.psum_scatter(jnp.concatenate(parts, axis=1), BOTH, scatter_dimension=0, tiled=True).reshape(-1)
    outs, at = [], 0
    for size in SIZES:
        outs.append(own[at : at + size])
        at += size
    grad_gains = own[at : at + 18].reshape(2, 9)
    set_sums, set_counts = own[at + 18 : at + 26], own[at + 26 : at + 34]
    batch_mean = set_sums / jnp.maximum(set_counts, 1.0)
    running_next = jnp.where(set_counts > 0.5, 0.75 * running + 0.25 * batch_mean, running)
    return (jnp.swapaxes(res[0], 1, 2), jnp.swapaxes(res[1], 1, 2), *outs, grad_gains, running_next)


def solution(mesh):
    P = jax.sharding.PartitionSpec
    flat, rows, cube = P(BOTH), P(BOTH, None), P(BOTH, None, None)
    return jax.shard_map(
        body,
        mesh=mesh,
        in_specs=(cube, rows, rows, rows, flat, flat, flat, flat, flat, flat, flat, P(None, "dp"), P(), cube),
        out_specs=(cube, cube, flat, flat, flat, flat, flat, P(None, "dp"), P()),
        check_vma=False,
    )
```

```python
import functools

import jax
import jax.numpy as jnp
import numpy as np
from jax import lax
from jax.experimental import pallas as pl
from jax.experimental.pallas import tpu as pltpu
from jax.sharding import PartitionSpec as P

D, H, HD, FF, NDATE, NLAG, F, NSET, LEN = 144, 9, 16, 512, 12, 84, 96, 8, 1024
EPS = 1e-05
TOK = 256
QT = 256
CH = 128
f32, bf16 = jnp.float32, jnp.bfloat16
MESH = pl.DeviceIdType.MESH
BOTH = ("dp", "fsdp")

A_ROWS, B_ROWS = 8, 16
SPECS = {
    "in": (D, 108, 4, 3, "a", 0),
    "qkv": (3 * D, 486, 8, 9, "a", 1),
    "gu": (2 * FF, 1152, 8, 9, "b", 0),
    "down": (D, 576, 2, 8, "b", 9),
    "out": (D, 162, 8, 9, "b", 14),
}
ROWS = {"in": F, "qkv": D, "gu": D, "down": FF, "out": D}


def dot(a, b, ca=1, cb=0, **kw):
    return lax.dot_general(a, b, (((ca,), (cb,)), ((), ())), preferred_element_type=f32, **kw)


def lane_tiles(width):
    return [(t // 128, t, min(128, width - t)) for t in range(0, width, 128)]


def pieces(piece, source, count):
    cuts = []
    for i in range(count):
        at, left, parts = i * piece, piece, []
        while left:
            c, o = divmod(at, source)
            n = min(left, source - o)
            parts.append((c, o, n))
            at, left = at + n, left - n
        cuts.append(parts)
    return cuts


def spot(c):
    return (c % 2) * 64 + c // 2


def join(parts):
    return parts[0] if len(parts) == 1 else jnp.concatenate(parts, axis=1)


def unpack(flat, rows, name, dst):
    cols, chunk, gc, gr, _, base = SPECS[name]
    groups, kept = 128 // gc, {}

    def owner(c):
        if c not in kept:
            kept[c] = join(
                [flat[pl.ds(spot(c) * rows + base + t, groups, stride=gc // 2 * rows), :] for t, _, _ in lane_tiles(chunk)]
            )
        return kept[c]

    for i, parts in enumerate(pieces(cols, chunk, gr)):
        row = join([owner(c)[:, o : o + n] for c, o, n in parts])
        for t, at, width in lane_tiles(cols):
            dst[t, pl.ds(i, groups, stride=gr), :width] = row[:, at : at + width]


def pack(src, name, flat, rows):
    cols, chunk, gc, gr, _, base = SPECS[name]
    groups, kept = 128 // gc, {}

    def line(i):
        if i not in kept:
            kept[i] = join([src[t, pl.ds(i, groups, stride=gr), :] for t, _, _ in lane_tiles(cols)])
        return kept[i]

    for c, parts in enumerate(pieces(chunk, cols, gc)):
        run = [line(i)[:, o : o + n] for i, o, n in parts]
        run = join(run + ([jnp.zeros((groups, -chunk % 128), f32)] if chunk % 128 else []))
        for t, at, _ in lane_tiles(chunk):
            flat[pl.ds(spot(c) * rows + base + t, groups, stride=gc // 2 * rows), :] = run[:, at : at + 128]


def place():
    fs = lax.axis_index("fsdp")
    return lax.axis_index("dp"), fs // 2, fs % 2


def partners():
    dp, y, core = place()
    across = lambda o: (lax.rem(dp + o, 16), 2 * y + core)
    along = lambda o: (dp, 2 * lax.rem(y + o, 4) + core)
    return across, along, (dp, 2 * y + 1 - core)


def enter():
    across, along, sibling = partners()
    barrier = pltpu.get_barrier_semaphore()

    @pl.loop(1, 16)
    def _(o):
        pl.semaphore_signal(barrier, inc=1, device_id=across(o), device_id_type=MESH)

    for o in (1, 2, 3):
        pl.semaphore_signal(barrier, inc=1, device_id=along(o), device_id_type=MESH)
    pl.semaphore_signal(barrier, inc=1, device_id=sibling, device_id_type=MESH)
    pl.semaphore_wait(barrier, 19)


def send(src, dst, sems, k, to):
    pltpu.make_async_remote_copy(
        src_ref=src, dst_ref=dst, send_sem=sems.at[0, k], recv_sem=sems.at[1, k], device_id=to, device_id_type=MESH
    ).start()


def wait(ref, sem):
    pltpu.make_async_copy(ref, ref, sem).wait()


class Gather:
    def __init__(self, own, everyone, sems):
        self.own, self.all, self.sems = own, everyone, sems

    def first(self):
        dp, y, core = place()
        _, along, _ = partners()
        for o in (1, 2, 3):
            send(self.own, self.all.at[core, dp, y], self.sems, 0, along(o))
        self.all[core, dp, y] = self.own[...]

    def second(self):
        dp, y, core = place()
        across, _, _ = partners()
        wait(self.all.at[core, dp, pl.ds(0, 3)], self.sems.at[1, 0])
        wait(self.all.at[core, dp, pl.ds(0, 3)], self.sems.at[0, 0])
        line = self.all.at[core, dp]

        @pl.loop(1, 16)
        def _(o):
            send(line, line, self.sems, 1, across(o))

    def third(self):
        _, _, core = place()
        _, _, sibling = partners()
        wait(self.all.at[core, pl.ds(0, 15)], self.sems.at[1, 1])
        wait(self.all.at[core, pl.ds(0, 15)], self.sems.at[0, 1])
        send(self.all.at[core], self.all.at[core], self.sems, 2, sibling)

    def last(self):
        _, _, core = place()
        wait(self.all.at[core], self.sems.at[1, 2])
        wait(self.all.at[core], self.sems.at[0, 2])


class Reduce:
    def __init__(self, parts, half, row, line, sems):
        self.parts, self.half, self.row, self.line, self.sems = parts, half, row, line, sems

    def first(self):
        _, _, core = place()
        _, _, sibling = partners()
        send(self.parts.at[1 - core], self.half, self.sems, 0, sibling)

    def second(self):
        dp, y, core = place()
        across, _, _ = partners()
        wait(self.half, self.sems.at[1, 0])
        wait(self.half, self.sems.at[0, 0])
        self.half[...] = (self.half[...].astype(f32) + self.parts[core].astype(f32)).astype(self.half.dtype)

        @pl.loop(1, 16)
        def _(o):
            send(self.half.at[lax.rem(dp + o, 16)], self.row.at[dp], self.sems, 1, across(o))

        self.row[dp] = self.half[dp]

    def third(self):
        dp, y, core = place()
        _, along, _ = partners()
        wait(self.row.at[pl.ds(0, 15)], self.sems.at[1, 1])
        wait(self.row.at[pl.ds(0, 15)], self.sems.at[0, 1])
        mine = jnp.sum(self.row[...].astype(f32), axis=0).astype(self.row.dtype)
        self.half[0] = mine
        for o in (1, 2, 3):
            send(self.half.at[0, lax.rem(y + o, 4)], self.line.at[y], self.sems, 2, along(o))
        self.line[y] = self.half[0, y]

    def last(self):
        wait(self.line.at[pl.ds(0, 3)], self.sems.at[1, 2])
        wait(self.line.at[pl.ds(0, 3)], self.sems.at[0, 2])
        return jnp.sum(self.line[...].astype(f32), axis=0)


def rope_tables():
    freqs = np.float32(10000.0) ** (-np.arange(HD // 2, dtype=np.float32) * np.float32(2.0) / np.float32(HD))
    angle = np.arange(LEN, dtype=np.float32)[None, :] * freqs.astype(np.float32)[:, None]
    return np.cos(angle.astype(np.float64)).astype(np.float32), np.sin(angle.astype(np.float64)).astype(np.float32)


def own_tiles(w_in, w_qkv, w_out, w_gu, w_down, gains, tile_a, tile_b, wide):
    tile_a[...] = jnp.zeros_like(tile_a)
    wide[...] = jnp.zeros_like(wide)
    for name, ref in (("in", w_in), ("qkv", w_qkv), ("out", w_out), ("gu", w_gu), ("down", w_down)):
        _, chunk, _, _, which, base = SPECS[name]
        for t, at, width in lane_tiles(chunk):
            (tile_a if which == "a" else wide)[base + t, :width] = ref[pl.ds(at, width)].astype(f32)
    tile_a[0:1, 108:117] = gains[0:1, :].astype(f32)
    tile_a[0:1, 117:126] = gains[1:2, :].astype(f32)
    tile_b[...] = wide[...].astype(bf16)


def gain_columns(flat, out):
    rows = flat[pl.ds(0, 16, stride=4 * A_ROWS), :]
    r = lax.broadcasted_iota(jnp.int32, (D, 16), 0) // 9
    spread = dot((r == lax.broadcasted_iota(jnp.int32, (D, 16), 1)).astype(f32), rows)
    lane = lax.broadcasted_iota(jnp.int32, (D, 128), 1)
    e = lax.rem(lax.broadcasted_iota(jnp.int32, (D, 128), 0), 9)
    for i in (0, 1):
        out[:, i : i + 1] = jnp.sum(jnp.where(lane == e + 108 + 9 * i, spread, 0.0), axis=1, keepdims=True)


def gain_rows(partial, flat):
    pos = lax.broadcasted_iota(jnp.int32, (128, D), 0)
    r = lax.broadcasted_iota(jnp.int32, (128, D), 1) // 9
    pick = (lax.rem(pos, 64) // 4 == r).astype(f32)
    lane = lax.broadcasted_iota(jnp.int32, (D, 128), 1)
    e = lax.rem(lax.broadcasted_iota(jnp.int32, (D, 128), 0), 9)
    cols = jnp.zeros((D, 128), f32)
    for i in (0, 1):
        cols += jnp.where(lane == e + 108 + 9 * i, jnp.sum(partial[i], axis=1, keepdims=True), 0.0)
    spread = dot(pick, cols, precision=lax.Precision.HIGHEST)
    flat[pl.ds(0, 128, stride=A_ROWS), :] += spread


def series_scalars(targets, lag_mask, date_mask, freq, sets, factor, stats):
    scale = jnp.sum(jnp.abs(targets[...]), axis=1, keepdims=True) / LEN + 1e-5
    lag = lag_mask[...].astype(f32) / scale
    second = lax.broadcasted_iota(jnp.int32, (2, NDATE), 0) == 1
    start = jnp.where(second, freq[1], freq[0]) * (NDATE // 3)
    keep = jnp.where(lax.broadcasted_iota(jnp.int32, (2, NDATE), 1) >= start, date_mask[...], 0).astype(f32)
    both = jnp.concatenate([lag, keep], axis=1)
    both = jnp.concatenate([both, jnp.zeros((2, 32), f32)], axis=1)
    both = jnp.concatenate([both, jnp.zeros((6, 128), f32)], axis=0)
    factor[...] = both.T
    lane = lax.broadcasted_iota(jnp.int32, (1, 128), 1)
    row = jnp.zeros((1, 128), f32)
    for s in (0, 1):
        row += jnp.where(lane == sets[s], scale[s : s + 1], 0.0) + jnp.where(lane == sets[s] + NSET, 1.0, 0.0)
    stats[...] = row


def gather_kernel(w_in, w_qkv, w_out, w_gu, w_down, gains, win, wqkv, wout, wgu, wdown, winT, wqkvT, woutT, wguT, wdownT, gain_cols,
                  tile_a, tile_b, wide, all_a, all_b, flat_a, flat_b, *rest):
    mats, (sem_a, sem_b) = rest[:5], rest[5:]
    own_tiles(w_in, w_qkv, w_out, w_gu, w_down, gains, tile_a, tile_b, wide)
    enter()
    a, b = Gather(tile_a, all_a, sem_a), Gather(tile_b, all_b, sem_b)
    a.first()
    b.first()
    a.second()
    b.second()
    a.third()
    b.third()
    a.last()
    flat_a[...] = all_a[...].reshape(128 * A_ROWS, 128)
    gain_columns(flat_a, gain_cols)

    def emit(name, flat, rows, mat, out, outT):
        unpack(flat, rows, name, mat)
        for t, at, width in lane_tiles(SPECS[name][0]):
            val = mat[t][:, :width]
            out[:, at : at + width] = val.astype(bf16)
            outT[at : at + width, :] = val.T.astype(bf16)

    emit("in", flat_a, A_ROWS, mats[0], win, winT)
    emit("qkv", flat_a, A_ROWS, mats[1], wqkv, wqkvT)
    b.last()
    flat_b[...] = all_b[...].astype(f32).reshape(128 * B_ROWS, 128)
    emit("out", flat_b, B_ROWS, mats[2], wout, woutT)
    emit("gu", flat_b, B_ROWS, mats[3], wgu, wguT)
    emit("down", flat_b, B_ROWS, mats[4], wdown, wdownT)


VM = pl.BlockSpec(memory_space=pltpu.VMEM)
SM = pl.BlockSpec(memory_space=pltpu.SMEM)


def tiled(name):
    return (-(-SPECS[name][0] // 128), ROWS[name], 128)


NAMES = ("in", "qkv", "out", "gu", "down")


def gather_all(w_in, w_qkv, w_out, w_gu, w_down, gains):
    sd, V = jax.ShapeDtypeStruct, pltpu.VMEM
    shapes = [(ROWS[n], SPECS[n][0]) for n in NAMES]
    return pl.pallas_call(
        gather_kernel,
        in_specs=[VM] * 6,
        out_specs=[VM] * 11,
        out_shape=[sd(s, bf16) for s in shapes] + [sd(s[::-1], bf16) for s in shapes] + [sd((D, 2), f32)],
        scratch_shapes=[V((A_ROWS, 128), f32), V((B_ROWS, 128), bf16), V((B_ROWS, 128), f32),
                        V((2, 16, 4, A_ROWS, 128), f32), V((2, 16, 4, B_ROWS, 128), bf16),
                        V((128 * A_ROWS, 128), f32), V((128 * B_ROWS, 128), f32)]
        + [V(tiled(n), f32) for n in NAMES]
        + [pltpu.SemaphoreType.DMA((2, 3))] * 2,
        compiler_params=pltpu.CompilerParams(collective_id=0, has_side_effects=True, vmem_limit_bytes=40 * 2**20),
    )(w_in, w_qkv, w_out, w_gu, w_down, gains)


def reduce_kernel(g_in, g_qkv, g_out, g_gu, g_down, g_gain, stats, running,
                  o_in, o_qkv, o_out, o_gu, o_down, o_gain, o_running,
                  flat_a, flat_b, parts_a, parts_b, half_a, half_b, row_a, row_b, line_a, line_b, total_b, sem_a, sem_b):
    flat_a[...] = jnp.zeros_like(flat_a)
    flat_b[...] = jnp.zeros_like(flat_b)
    pack(g_out, "out", flat_b, B_ROWS)
    pack(g_gu, "gu", flat_b, B_ROWS)
    pack(g_down, "down", flat_b, B_ROWS)
    parts_b[...] = flat_b[...].reshape(parts_b.shape).astype(bf16)
    pack(g_in, "in", flat_a, A_ROWS)
    pack(g_qkv, "qkv", flat_a, A_ROWS)
    gain_rows(g_gain, flat_a)
    flat_a[pl.ds(5, 128, stride=A_ROWS), :] = jnp.broadcast_to(stats[...], (128, 128))
    parts_a[...] = flat_a[...].reshape(parts_a.shape)
    enter()
    a, b = Reduce(parts_a, half_a, row_a, line_a, sem_a), Reduce(parts_b, half_b, row_b, line_b, sem_b)
    for step in ("first", "second", "third"):
        getattr(a, step)()
        getattr(b, step)()
    tot_a = a.last()
    total_b[...] = b.last()
    finish(tot_a, total_b, running, o_in, o_qkv, o_out, o_gu, o_down, o_gain, o_running)


def finish(tot_a, total_b, running, o_in, o_qkv, o_out, o_gu, o_down, o_gain, o_running):
    for name, ref in (("in", o_in), ("qkv", o_qkv), ("out", o_out), ("gu", o_gu), ("down", o_down)):
        _, chunk, _, _, which, base = SPECS[name]
        for t, at, width in lane_tiles(chunk):
            ref[pl.ds(at, width)] = tot_a[base + t, :width] if which == "a" else total_b[base + t, :width]
    o_gain[0:1, :] = tot_a[0:1, 108:117]
    o_gain[1:2, :] = tot_a[0:1, 117:126]
    sums, counts = tot_a[5, :NSET], tot_a[5, NSET : 2 * NSET]
    old = running[...]
    o_running[...] = jnp.where(counts > 0.5, 0.75 * old + 0.25 * (sums / jnp.maximum(counts, 1.0)), old)


def reduce_all(grads, g_gain, stats, running):
    sd, V = jax.ShapeDtypeStruct, pltpu.VMEM
    return pl.pallas_call(
        reduce_kernel,
        in_specs=[VM] * 8,
        out_specs=[VM] * 7,
        out_shape=[sd((SPECS[n][1],), f32) for n in NAMES] + [sd((2, 9), f32), sd((NSET,), f32)],
        scratch_shapes=[V((128 * A_ROWS, 128), f32), V((128 * B_ROWS, 128), f32),
                        V((2, 16, 4, A_ROWS, 128), f32), V((2, 16, 4, B_ROWS, 128), bf16),
                        V((16, 4, A_ROWS, 128), f32), V((16, 4, B_ROWS, 128), bf16),
                        V((16, 4, A_ROWS, 128), f32), V((16, 4, B_ROWS, 128), bf16),
                        V((4, A_ROWS, 128), f32), V((4, B_ROWS, 128), bf16), V((B_ROWS, 128), f32)]
        + [pltpu.SemaphoreType.DMA((2, 3))] * 2,
        compiler_params=pltpu.CompilerParams(collective_id=1, has_side_effects=True, vmem_limit_bytes=40 * 2**20),
    )(*grads, g_gain, stats, running)


def fold(op, a):
    return op(a.reshape(a.shape[0] // 8, 8, a.shape[1]), axis=0)


def weave(gens):
    gens = list(gens)
    while gens:
        for g in list(gens):
            try:
                next(g)
            except StopIteration:
                gens.remove(g)


def attend(hh, count, q, k, v, prob, sbuf, rl, osum, mixed):
    diag = lambda c0: (lax.broadcasted_iota(jnp.int32, (CH, QT), 0) + c0) <= lax.broadcasted_iota(jnp.int32, (CH, QT), 1)
    kts = [k[hh * count + u].astype(f32).T.astype(bf16) for u in range(count)]
    tasks = [(u, j) for j in range(LEN // QT - 1, -1, -1) for u in range(count)]
    tops, invs = {}, {}

    def score(i):
        u, j = tasks[i]
        n, best = (j + 1) * QT, []
        for c in range(0, n, CH):
            s = dot(kts[u][c : c + CH], q[hh * count + u, :, j * QT : j * QT + QT])
            if c + CH > n - QT:
                s = jnp.where(diag(c - (n - QT)), s, -1e30)
            sbuf[i % 2, c : c + CH] = s
            best.append(fold(jnp.max, s))
            yield
        tops[i] = jnp.max(functools.reduce(jnp.maximum, best), axis=0, keepdims=True)

    def exponent(i):
        u, j = tasks[i]
        n, sums = (j + 1) * QT, []
        for c in range(0, n, CH):
            p = jnp.exp(sbuf[i % 2, c : c + CH] - tops[i])
            sums.append(fold(jnp.sum, p))
            prob[j][hh * count + u, c : c + CH] = p.astype(bf16)
            yield
        invs[i] = 1.0 / jnp.sum(functools.reduce(jnp.add, sums), axis=0, keepdims=True)

    def mix(i):
        u, j = tasks[i]
        h, n, cols = hh * count + u, (j + 1) * QT, pl.ds(j * QT, QT)
        o = dot(v[h][:, :n], prob[j][h]) * invs[i]
        rl[h, :, cols] = invs[i]
        osum[h, :, cols] = o
        mixed[h, :, cols] = o.astype(bf16)

    last = len(tasks)
    for i in range(last + 2):
        if 0 <= i - 2:
            mix(i - 2)
        weave(([score(i)] if i < last else []) + ([exponent(i - 1)] if 0 <= i - 1 < last else []))


def main_kernel(feats, dout, targets, lag_mask, date_mask, freq, sets, gains, cosr, sinr,
                win, wqkv, wout, wgu, wdown, winT, wqkvT, woutT, wguT, wdownT,
                out, gfeats, g_in, g_qkv, g_out, g_gu, g_down, g_gain, stats,
                factor, lifted, first, inv1, normed, q, k, v, p0, p1, p2, p3, sbuf, rl, osum, mixed, second, hidden, both,
                gmid, gbranch, gmixed, gjoint, gfirst):
    s = pl.program_id(0)
    prob = (p0, p1, p2, p3)

    @pl.when(s == 0)
    def _():
        for ref in (g_in, g_qkv, g_out, g_gu, g_down, g_gain):
            ref[...] = jnp.zeros_like(ref)
        series_scalars(targets, lag_mask, date_mask, freq, sets, factor, stats)

    def add_to(ref, val):
        for t, at, width in lane_tiles(val.shape[1]):
            ref[t, :, :width] += val[:, at : at + width]

    gain0 = gains[:, 0:1]
    gain1 = gains[:, 1:2]
    fac = jnp.where(s == 0, factor[:F, 0:1], factor[:F, 1:2])

    @pl.loop(0, LEN // TOK)
    def _(i):
        t = pl.ds(pl.multiple_of(i * TOK, TOK), TOK)
        lift = (feats[0, :, t].astype(f32) * fac).astype(bf16)
        lifted[:, t] = lift
        x = dot(winT[...], lift)
        first[:, t] = x
        r = lax.rsqrt(jnp.mean(x * x, axis=0, keepdims=True) + EPS)
        inv1[:, t] = r
        n = (x * r * gain0).astype(bf16)
        normed[:, t] = n
        joint = dot(wqkvT[...], n).reshape(3, H, HD, TOK)
        c, sn = cosr[:, t][None], sinr[:, t][None]
        for which, ref, scale in ((0, q, 0.25), (1, k, 1.0)):
            a, b = joint[which, :, :8], joint[which, :, 8:]
            ref[:, :, t] = (jnp.concatenate([a * c - b * sn, b * c + a * sn], axis=1) * scale).astype(bf16)
        v[:, :, t] = joint[2].astype(bf16)

    @pl.loop(0, H // 3)
    def _(hh):
        attend(hh, 3, q, k, v, prob, sbuf, rl, osum, mixed)

    @pl.loop(0, LEN // TOK)
    def _(i):
        t = pl.ds(pl.multiple_of(i * TOK, TOK), TOK)
        mid = first[:, t] + dot(woutT[...], mixed[:, :, t].reshape(D, TOK))
        r = lax.rsqrt(jnp.mean(mid * mid, axis=0, keepdims=True) + EPS)
        sec = (mid * r * gain1).astype(bf16)
        second[:, t] = sec
        g = dout[0, :, t]
        for f in range(0, FF, 128):
            gate = dot(wguT[f : f + 128], sec)
            up = dot(wguT[FF + f : FF + f + 128], sec)
            gh = dot(wdown[f : f + 128], g)
            sig = 1.0 / (1.0 + jnp.exp(-gate))
            silu = gate * sig
            hidden[f : f + 128, t] = (silu * up).astype(bf16)
            both[FF + f : FF + f + 128, t] = (gh * silu).astype(bf16)
            both[f : f + 128, t] = (gh * up * (sig + silu * (1.0 - sig))).astype(bf16)
        out[0, :, t] = (mid + dot(wdownT[...], hidden[:, t])).astype(bf16)
        c = dot(wgu[...], both[:, t])
        cg = c * gain1
        inner = jnp.mean(cg * mid, axis=0, keepdims=True)
        gain_part = c * mid * r
        g_gain[1] += gain_part[:, :128] + gain_part[:, 128:]
        gm = g.astype(f32) + r * cg - mid * (r * r * r * inner)
        gmid[:, t] = gm
        gb = gm.astype(bf16)
        gbranch[:, t] = gb
        gmixed[:, :, t] = dot(wout[...], gb).reshape(H, HD, TOK)

    add_to(g_down, dot(hidden[...], dout[0], 1, 1))
    add_to(g_gu, dot(second[...], both[...], 1, 1))
    add_to(g_out, dot(mixed[...].reshape(D, LEN), gbranch[...], 1, 1))

    @pl.loop(0, H)
    def _(h):
        do = (gmixed[h] * rl[h]).astype(bf16)
        delta = jnp.sum(do.astype(f32) * osum[h], axis=0, keepdims=True)
        vt = v[h].astype(f32).T.astype(bf16)
        kh = k[h]
        dk = jnp.zeros((HD, LEN), f32)
        dv = jnp.zeros((HD, LEN), f32)
        dqs = []
        for j in range(LEN // QT):
            n = (j + 1) * QT
            cols = slice(j * QT, n)
            dp = dot(vt[:n], do[:, cols])
            p = prob[j][h]
            ds = (p.astype(f32) * (dp - delta[:, cols])).astype(bf16)
            dqs.append(dot(kh[:, :n], ds))
            pad = lambda a: a if n == LEN else jnp.concatenate([a, jnp.zeros((HD, LEN - n), f32)], axis=1)
            dk += pad(dot(q[h, :, cols], ds, 1, 1))
            dv += pad(dot(do[:, cols], p, 1, 1))
        dq = jnp.concatenate(dqs, axis=1) * 0.25
        c, sn = cosr[...], sinr[...]
        for which, val in ((0, dq), (1, dk)):
            a, b = val[:8], val[8:]
            gjoint[which, h] = jnp.concatenate([a * c + b * sn, b * c - a * sn], axis=0).astype(bf16)
        gjoint[2, h] = dv.astype(bf16)

    @pl.loop(0, LEN // TOK)
    def _(i):
        t = pl.ds(pl.multiple_of(i * TOK, TOK), TOK)
        c = dot(wqkv[...], gjoint[:, :, :, t].reshape(3 * D, TOK))
        x, r = first[:, t], inv1[:, t]
        cg = c * gain0
        inner = jnp.mean(cg * x, axis=0, keepdims=True)
        gain_part = c * x * r
        g_gain[0] += gain_part[:, :128] + gain_part[:, 128:]
        gf = (gmid[:, t] + r * cg - x * (r * r * r * inner)).astype(bf16)
        gfirst[:, t] = gf
        gfeats[0, :, t] = (dot(win[...], gf) * fac).astype(bf16)

    add_to(g_qkv, dot(normed[...], gjoint[...].reshape(3 * D, LEN), 1, 1))
    add_to(g_in, dot(lifted[...], gfirst[...], 1, 1))


def run_main(feats_t, dout_t, targets, lag_mask, date_mask, freq_ids, dataset_ids, gain_cols, mats):
    cos, sin = rope_tables()
    S = feats_t.shape[0]
    full = lambda *shape: pl.BlockSpec(shape, lambda s: (0,) * len(shape))
    per = lambda *shape: pl.BlockSpec((1,) + shape, lambda s: (s,) + (0,) * len(shape))
    sd = jax.ShapeDtypeStruct
    V = pltpu.VMEM
    shapes = [(ROWS[n], SPECS[n][0]) for n in NAMES]
    return pl.pallas_call(
        main_kernel,
        grid=(S,),
        in_specs=[per(F, LEN), per(D, LEN), full(2, LEN), full(2, NLAG), full(2, NDATE), SM, SM, full(D, 2), full(8, LEN), full(8, LEN)]
        + [full(*s) for s in shapes]
        + [full(*s[::-1]) for s in shapes],
        out_specs=[per(D, LEN), per(F, LEN)] + [full(*tiled(n)) for n in NAMES] + [full(2, D, 128), full(1, 128)],
        out_shape=[sd((S, D, LEN), bf16), sd((S, F, LEN), bf16)] + [sd(tiled(n), f32) for n in NAMES] + [sd((2, D, 128), f32), sd((1, 128), f32)],
        scratch_shapes=[
            V((128, 8), f32),
            V((F, LEN), bf16), V((D, LEN), f32), V((1, LEN), f32), V((D, LEN), bf16),
            V((H, HD, LEN), bf16), V((H, HD, LEN), bf16), V((H, HD, LEN), bf16),
            *[V((H, (j + 1) * QT, QT), bf16) for j in range(4)],
            V((2, LEN, QT), f32), V((H, 1, LEN), f32), V((H, HD, LEN), f32), V((H, HD, LEN), bf16),
            V((D, LEN), bf16), V((FF, LEN), bf16), V((2 * FF, LEN), bf16),
            V((D, LEN), f32), V((D, LEN), bf16), V((H, HD, LEN), f32), V((3, H, HD, LEN), bf16), V((D, LEN), bf16),
        ],
        compiler_params=pltpu.CompilerParams(vmem_limit_bytes=60 * 2**20, dimension_semantics=("arbitrary",)),
    )(feats_t, dout_t, targets, lag_mask, date_mask, freq_ids, dataset_ids, gain_cols, jnp.asarray(cos), jnp.asarray(sin), *mats)


def body(feats, targets, lag_mask, date_mask, freq_ids, dataset_ids, w_in, w_qkv, w_out, w_gu, w_down, gains, running, d_out):
    *mats, gain_cols = gather_all(w_in, w_qkv, w_out, w_gu, w_down, gains)
    out, gfeats, *grads, g_gain, stats = run_main(
        jnp.swapaxes(feats, 1, 2), jnp.swapaxes(d_out, 1, 2), targets, lag_mask, date_mask, freq_ids, dataset_ids, gain_cols, mats
    )
    owned = reduce_all(grads, g_gain, stats, running)
    return (jnp.swapaxes(out, 1, 2), jnp.swapaxes(gfeats, 1, 2), *owned)


def solution(mesh):
    flat, rows, cube = P(BOTH), P(BOTH, None), P(BOTH, None, None)
    return jax.shard_map(
        body,
        mesh=mesh,
        in_specs=(cube, rows, rows, rows, flat, flat, flat, flat, flat, flat, flat, P(None, "dp"), P(), cube),
        out_specs=(cube, cube, flat, flat, flat, flat, flat, P(None, "dp"), P()),
        check_vma=False,
    )
```

```python
import functools

import jax
import jax.numpy as jnp
import numpy as np
from jax import lax
from jax.experimental import pallas as pl
from jax.experimental.pallas import tpu as pltpu
from jax.sharding import PartitionSpec as P

D, H, HD, FF, NDATE, NLAG, F, NSET, LEN = 144, 9, 16, 512, 12, 84, 96, 8, 1024
EPS = 1e-05
TOK = 256
QT = 256
CH = 128
f32, bf16 = jnp.float32, jnp.bfloat16
MESH = pl.DeviceIdType.MESH
BOTH = ("dp", "fsdp")

A_ROWS, B_ROWS = 8, 16
SPECS = {
    "in": (D, 108, 4, 3, "a", 0),
    "qkv": (3 * D, 486, 8, 9, "a", 1),
    "gu": (2 * FF, 1152, 8, 9, "b", 0),
    "down": (D, 576, 2, 8, "b", 9),
    "out": (D, 162, 8, 9, "b", 14),
}
ROWS = {"in": F, "qkv": D, "gu": D, "down": FF, "out": D}


def dot(a, b, ca=1, cb=0, **kw):
    return lax.dot_general(a, b, (((ca,), (cb,)), ((), ())), preferred_element_type=f32, **kw)


def lane_tiles(width):
    return [(t // 128, t, min(128, width - t)) for t in range(0, width, 128)]


def pieces(piece, source, count):
    cuts = []
    for i in range(count):
        at, left, parts = i * piece, piece, []
        while left:
            c, o = divmod(at, source)
            n = min(left, source - o)
            parts.append((c, o, n))
            at, left = at + n, left - n
        cuts.append(parts)
    return cuts


def spot(c):
    return (c % 2) * 64 + c // 2


def join(parts):
    return parts[0] if len(parts) == 1 else jnp.concatenate(parts, axis=1)


def unpack(flat, rows, name, dst):
    cols, chunk, gc, gr, _, base = SPECS[name]
    groups, kept = 128 // gc, {}

    def owner(c):
        if c not in kept:
            kept[c] = join(
                [flat[pl.ds(spot(c) * rows + base + t, groups, stride=gc // 2 * rows), :] for t, _, _ in lane_tiles(chunk)]
            )
        return kept[c]

    for i, parts in enumerate(pieces(cols, chunk, gr)):
        row = join([owner(c)[:, o : o + n] for c, o, n in parts])
        for t, at, width in lane_tiles(cols):
            dst[t, pl.ds(i, groups, stride=gr), :width] = row[:, at : at + width]


def pack(src, name, flat, rows):
    cols, chunk, gc, gr, _, base = SPECS[name]
    groups, kept = 128 // gc, {}

    def line(i):
        if i not in kept:
            kept[i] = join([src[t, pl.ds(i, groups, stride=gr), :] for t, _, _ in lane_tiles(cols)])
        return kept[i]

    for c, parts in enumerate(pieces(chunk, cols, gc)):
        run = [line(i)[:, o : o + n] for i, o, n in parts]
        run = join(run + ([jnp.zeros((groups, -chunk % 128), f32)] if chunk % 128 else []))
        for t, at, _ in lane_tiles(chunk):
            flat[pl.ds(spot(c) * rows + base + t, groups, stride=gc // 2 * rows), :] = run[:, at : at + 128]


def place():
    fs = lax.axis_index("fsdp")
    return lax.axis_index("dp"), fs // 2, fs % 2


def partners():
    dp, y, core = place()
    across = lambda o: (lax.rem(dp + o, 16), 2 * y + core)
    along = lambda o: (dp, 2 * lax.rem(y + o, 4) + core)
    return across, along, (dp, 2 * y + 1 - core)


def enter():
    across, along, sibling = partners()
    barrier = pltpu.get_barrier_semaphore()

    @pl.loop(1, 16)
    def _(o):
        pl.semaphore_signal(barrier, inc=1, device_id=across(o), device_id_type=MESH)

    for o in (1, 2, 3):
        pl.semaphore_signal(barrier, inc=1, device_id=along(o), device_id_type=MESH)
    pl.semaphore_signal(barrier, inc=1, device_id=sibling, device_id_type=MESH)
    pl.semaphore_wait(barrier, 19)


def send(src, dst, sems, k, to):
    pltpu.make_async_remote_copy(
        src_ref=src, dst_ref=dst, send_sem=sems.at[0, k], recv_sem=sems.at[1, k], device_id=to, device_id_type=MESH
    ).start()


def wait(ref, sem):
    pltpu.make_async_copy(ref, ref, sem).wait()


class Gather:
    def __init__(self, own, everyone, sems):
        self.own, self.all, self.sems = own, everyone, sems

    def first(self):
        dp, y, core = place()
        _, along, _ = partners()
        for o in (1, 2, 3):
            send(self.own, self.all.at[core, dp, y], self.sems, 0, along(o))
        self.all[core, dp, y] = self.own[...]

    def second(self):
        dp, y, core = place()
        across, _, _ = partners()
        wait(self.all.at[core, dp, pl.ds(0, 3)], self.sems.at[1, 0])
        wait(self.all.at[core, dp, pl.ds(0, 3)], self.sems.at[0, 0])
        line = self.all.at[core, dp]

        @pl.loop(1, 16)
        def _(o):
            send(line, line, self.sems, 1, across(o))

    def third(self):
        _, _, core = place()
        _, _, sibling = partners()
        wait(self.all.at[core, pl.ds(0, 15)], self.sems.at[1, 1])
        wait(self.all.at[core, pl.ds(0, 15)], self.sems.at[0, 1])
        send(self.all.at[core], self.all.at[core], self.sems, 2, sibling)

    def last(self):
        _, _, core = place()
        wait(self.all.at[core], self.sems.at[1, 2])
        wait(self.all.at[core], self.sems.at[0, 2])


class Reduce:
    def __init__(self, parts, half, row, line, sems):
        self.parts, self.half, self.row, self.line, self.sems = parts, half, row, line, sems

    def first(self):
        _, _, core = place()
        _, _, sibling = partners()
        send(self.parts.at[1 - core], self.half, self.sems, 0, sibling)

    def second(self):
        dp, y, core = place()
        across, _, _ = partners()
        wait(self.half, self.sems.at[1, 0])
        wait(self.half, self.sems.at[0, 0])
        self.half[...] = (self.half[...].astype(f32) + self.parts[core].astype(f32)).astype(self.half.dtype)

        @pl.loop(1, 16)
        def _(o):
            send(self.half.at[lax.rem(dp + o, 16)], self.row.at[dp], self.sems, 1, across(o))

        self.row[dp] = self.half[dp]

    def third(self):
        dp, y, core = place()
        _, along, _ = partners()
        wait(self.row.at[pl.ds(0, 15)], self.sems.at[1, 1])
        wait(self.row.at[pl.ds(0, 15)], self.sems.at[0, 1])
        mine = jnp.sum(self.row[...].astype(f32), axis=0).astype(self.row.dtype)
        self.half[0] = mine
        for o in (1, 2, 3):
            send(self.half.at[0, lax.rem(y + o, 4)], self.line.at[y], self.sems, 2, along(o))
        self.line[y] = self.half[0, y]

    def last(self):
        wait(self.line.at[pl.ds(0, 3)], self.sems.at[1, 2])
        wait(self.line.at[pl.ds(0, 3)], self.sems.at[0, 2])
        return jnp.sum(self.line[...].astype(f32), axis=0)


def rope_tables():
    freqs = np.float32(10000.0) ** (-np.arange(HD // 2, dtype=np.float32) * np.float32(2.0) / np.float32(HD))
    angle = np.arange(LEN, dtype=np.float32)[None, :] * freqs.astype(np.float32)[:, None]
    return np.cos(angle.astype(np.float64)).astype(np.float32), np.sin(angle.astype(np.float64)).astype(np.float32)


def own_tiles(w_in, w_qkv, w_out, w_gu, w_down, gains, tile_a, tile_b, wide):
    tile_a[...] = jnp.zeros_like(tile_a)
    wide[...] = jnp.zeros_like(wide)
    for name, ref in (("in", w_in), ("qkv", w_qkv), ("out", w_out), ("gu", w_gu), ("down", w_down)):
        _, chunk, _, _, which, base = SPECS[name]
        for t, at, width in lane_tiles(chunk):
            (tile_a if which == "a" else wide)[base + t, :width] = ref[pl.ds(at, width)].astype(f32)
    tile_a[0:1, 108:117] = gains[0:1, :].astype(f32)
    tile_a[0:1, 117:126] = gains[1:2, :].astype(f32)
    tile_b[...] = wide[...].astype(bf16)


def gain_columns(flat, out):
    rows = flat[pl.ds(0, 16, stride=4 * A_ROWS), :]
    r = lax.broadcasted_iota(jnp.int32, (D, 16), 0) // 9
    spread = dot((r == lax.broadcasted_iota(jnp.int32, (D, 16), 1)).astype(f32), rows)
    lane = lax.broadcasted_iota(jnp.int32, (D, 128), 1)
    e = lax.rem(lax.broadcasted_iota(jnp.int32, (D, 128), 0), 9)
    for i in (0, 1):
        out[:, i : i + 1] = jnp.sum(jnp.where(lane == e + 108 + 9 * i, spread, 0.0), axis=1, keepdims=True)


def gain_rows(partial, flat):
    pos = lax.broadcasted_iota(jnp.int32, (128, D), 0)
    r = lax.broadcasted_iota(jnp.int32, (128, D), 1) // 9
    pick = (lax.rem(pos, 64) // 4 == r).astype(f32)
    lane = lax.broadcasted_iota(jnp.int32, (D, 128), 1)
    e = lax.rem(lax.broadcasted_iota(jnp.int32, (D, 128), 0), 9)
    cols = jnp.zeros((D, 128), f32)
    for i in (0, 1):
        cols += jnp.where(lane == e + 108 + 9 * i, jnp.sum(partial[i], axis=1, keepdims=True), 0.0)
    spread = dot(pick, cols, precision=lax.Precision.HIGHEST)
    flat[pl.ds(0, 128, stride=A_ROWS), :] += spread


def series_scalars(targets, lag_mask, date_mask, freq, sets, factor, stats):
    scale = jnp.sum(jnp.abs(targets[...]), axis=1, keepdims=True) / LEN + 1e-5
    lag = lag_mask[...].astype(f32) / scale
    second = lax.broadcasted_iota(jnp.int32, (2, NDATE), 0) == 1
    start = jnp.where(second, freq[1], freq[0]) * (NDATE // 3)
    keep = jnp.where(lax.broadcasted_iota(jnp.int32, (2, NDATE), 1) >= start, date_mask[...], 0).astype(f32)
    both = jnp.concatenate([lag, keep], axis=1)
    both = jnp.concatenate([both, jnp.zeros((2, 32), f32)], axis=1)
    both = jnp.concatenate([both, jnp.zeros((6, 128), f32)], axis=0)
    factor[...] = both.T
    lane = lax.broadcasted_iota(jnp.int32, (1, 128), 1)
    row = jnp.zeros((1, 128), f32)
    for s in (0, 1):
        row += jnp.where(lane == sets[s], scale[s : s + 1], 0.0) + jnp.where(lane == sets[s] + NSET, 1.0, 0.0)
    stats[...] = row

def fold(op, a):
    return op(a.reshape(a.shape[0] // 8, 8, a.shape[1]), axis=0)


def weave(gens):
    gens = list(gens)
    while gens:
        for g in list(gens):
            try:
                next(g)
            except StopIteration:
                gens.remove(g)


VM = pl.BlockSpec(memory_space=pltpu.VMEM)
SM = pl.BlockSpec(memory_space=pltpu.SMEM)
HB = pl.BlockSpec(memory_space=pl.ANY)
NAMES = ("in", "qkv", "out", "gu", "down")


def tiled(name):
    return (-(-SPECS[name][0] // 128), ROWS[name], 128)


def attend(s, hh, count, q, k, v, prob, sbuf, rl, osum, mixed):
    diag = lambda c0: (lax.broadcasted_iota(jnp.int32, (CH, QT), 0) + c0) <= lax.broadcasted_iota(jnp.int32, (CH, QT), 1)
    kts = [k[s, hh * count + u].astype(f32).T.astype(bf16) for u in range(count)]
    tasks = [(u, j) for j in range(LEN // QT - 1, -1, -1) for u in range(count)]
    tops, invs = {}, {}

    def score(i):
        u, j = tasks[i]
        n, best = (j + 1) * QT, []
        for c in range(0, n, CH):
            x = dot(kts[u][c : c + CH], q[s, hh * count + u, :, j * QT : j * QT + QT])
            if c + CH > n - QT:
                x = jnp.where(diag(c - (n - QT)), x, -1e30)
            sbuf[i % 2, c : c + CH] = x
            best.append(fold(jnp.max, x))
            yield
        tops[i] = jnp.max(functools.reduce(jnp.maximum, best), axis=0, keepdims=True)

    def exponent(i):
        u, j = tasks[i]
        n, sums = (j + 1) * QT, []
        for c in range(0, n, CH):
            p = jnp.exp(sbuf[i % 2, c : c + CH] - tops[i])
            sums.append(fold(jnp.sum, p))
            prob[j][s, hh * count + u, c : c + CH] = p.astype(bf16)
            yield
        invs[i] = 1.0 / jnp.sum(functools.reduce(jnp.add, sums), axis=0, keepdims=True)

    def mix(i):
        u, j = tasks[i]
        h, n, cols = hh * count + u, (j + 1) * QT, pl.ds(j * QT, QT)
        o = dot(v[s, h][:, :n], prob[j][s, h]) * invs[i]
        rl[s, h, :, cols] = invs[i]
        osum[s, h, :, cols] = o
        mixed[s, h, :, cols] = o.astype(bf16)

    last = len(tasks)
    for i in range(last + 2):
        if 0 <= i - 2:
            mix(i - 2)
        weave(([score(i)] if i < last else []) + ([exponent(i - 1)] if 0 <= i - 1 < last else []))


def attend_back(s, h, q, k, v, prob, rl, osum, gmixed, cosr, sinr, gjoint):
    do = (gmixed[s, h] * rl[s, h]).astype(bf16)
    delta = jnp.sum(do.astype(f32) * osum[s, h], axis=0, keepdims=True)
    vt = v[s, h].astype(f32).T.astype(bf16)
    kh = k[s, h]
    dk = jnp.zeros((HD, LEN), f32)
    dv = jnp.zeros((HD, LEN), f32)
    dqs = []
    for j in range(LEN // QT):
        n = (j + 1) * QT
        cols = slice(j * QT, n)
        dp = dot(vt[:n], do[:, cols])
        p = prob[j][s, h]
        ds = (p.astype(f32) * (dp - delta[:, cols])).astype(bf16)
        dqs.append(dot(kh[:, :n], ds))
        pad = lambda a: a if n == LEN else jnp.concatenate([a, jnp.zeros((HD, LEN - n), f32)], axis=1)
        dk += pad(dot(q[s, h, :, cols], ds, 1, 1))
        dv += pad(dot(do[:, cols], p, 1, 1))
    dq = jnp.concatenate(dqs, axis=1) * 0.25
    c, sn = cosr[...], sinr[...]
    for which, val in ((0, dq), (1, dk)):
        a, b = val[:8], val[8:]
        gjoint[s, which, h] = jnp.concatenate([a * c + b * sn, b * c - a * sn], axis=0).astype(bf16)
    gjoint[s, 2, h] = dv.astype(bf16)


def layer_kernel(
    feats_h, targets_h, lag_h, date_h, freq, sets, w_in_h, w_qkv_h, w_out_h, w_gu_h, w_down_h, gains_h, dout_h, cos_h, sin_h,
    out_h, gfeats_h, tot_a, tot_b,
    feats, dout, targets, lag_mask, date_mask, w_in, w_qkv, w_out, w_gu, w_down, gains_own, cosr, sinr, out, gfeats,
    tile_a, tile_b, all_a, all_b, flat_a, flat_b, half_a, half_b, row_a, row_b, line_a, line_b,
    m_in, m_qkv, m_out, m_gu, m_down, win, wqkv, wout, wgu, wdown, winT, wqkvT, woutT, wguT, wdownT,
    gains, g_gain, factor, stats, lifted, first, inv1, normed, q, k, v, p0, p1, p2, p3, sbuf, rl, osum, mixed, second, hidden, both,
    gmid, gbranch, gmixed, gjoint, gfirst, sem_a, sem_b, sem_c, sem_d, sem_l,
):
    prob = (p0, p1, p2, p3)
    loads = [
        pltpu.make_async_copy(src, dst, sem_l.at[i])
        for i, (src, dst) in enumerate(
            (
                (w_in_h, w_in), (w_qkv_h, w_qkv), (w_out_h, w_out), (w_gu_h, w_gu), (w_down_h, w_down), (gains_h, gains_own),
                (feats_h, feats), (targets_h, targets), (lag_h, lag_mask), (date_h, date_mask), (cos_h, cosr), (sin_h, sinr), (dout_h, dout),
            )
        )
    ]
    for load in loads:
        load.start()
    for load in loads[:6]:
        load.wait()
    own_tiles(w_in, w_qkv, w_out, w_gu, w_down, gains_own, tile_a, tile_b, flat_b.at[pl.ds(0, B_ROWS)])
    enter()
    a, b = Gather(tile_a, all_a, sem_a), Gather(tile_b, all_b, sem_b)
    a.first()
    b.first()
    for load in loads[6:12]:
        load.wait()
    series_scalars(targets, lag_mask, date_mask, freq, sets, factor, stats)
    g_gain[...] = jnp.zeros_like(g_gain)
    for s in (0, 1):
        lifted[s] = (feats[s].astype(f32) * factor[:F, s : s + 1]).astype(bf16)
    a.second()
    a.third()
    b.second()
    a.last()
    flat_a[...] = all_a[...].reshape(128 * A_ROWS, 128)
    gain_columns(flat_a, gains)

    def emit(name, flat, rows, mat, out, outT):
        unpack(flat, rows, name, mat)
        for t, at, width in lane_tiles(SPECS[name][0]):
            val = mat[t][:, :width]
            out[:, at : at + width] = val.astype(bf16)
            outT[at : at + width, :] = val.T.astype(bf16)
        mat[...] = jnp.zeros_like(mat)

    emit("in", flat_a, A_ROWS, m_in, win, winT)
    emit("qkv", flat_a, A_ROWS, m_qkv, wqkv, wqkvT)

    def add_to(ref, val):
        for t, at, width in lane_tiles(val.shape[1]):
            ref[t, :, :width] += val[:, at : at + width]

    gain0 = gains[:, 0:1]
    gain1 = gains[:, 1:2]

    @pl.loop(0, 2)
    def _(s):
        @pl.loop(0, LEN // TOK)
        def _(i):
            t = pl.ds(pl.multiple_of(i * TOK, TOK), TOK)
            x = dot(winT[...], lifted[s, :, t])
            first[s, :, t] = x
            r = lax.rsqrt(jnp.mean(x * x, axis=0, keepdims=True) + EPS)
            inv1[s, :, t] = r
            n = (x * r * gain0).astype(bf16)
            normed[s, :, t] = n
            joint = dot(wqkvT[...], n).reshape(3, H, HD, TOK)
            c, sn = cosr[:, t][None], sinr[:, t][None]
            for which, ref, scale in ((0, q, 0.25), (1, k, 1.0)):
                u, w = joint[which, :, :8], joint[which, :, 8:]
                ref[s, :, :, t] = (jnp.concatenate([u * c - w * sn, w * c + u * sn], axis=1) * scale).astype(bf16)
            v[s, :, :, t] = joint[2].astype(bf16)

    @pl.loop(0, H // 3)
    def _(hh):
        attend(0, hh, 3, q, k, v, prob, sbuf, rl, osum, mixed)

    b.third()

    @pl.loop(0, H // 3)
    def _(hh):
        attend(1, hh, 3, q, k, v, prob, sbuf, rl, osum, mixed)

    b.last()
    flat_b[...] = all_b[...].astype(f32).reshape(128 * B_ROWS, 128)
    emit("out", flat_b, B_ROWS, m_out, wout, woutT)
    emit("gu", flat_b, B_ROWS, m_gu, wgu, wguT)
    emit("down", flat_b, B_ROWS, m_down, wdown, wdownT)
    loads[12].wait()

    @pl.loop(0, 2)
    def _(s):
        @pl.loop(0, LEN // TOK)
        def _(i):
            t = pl.ds(pl.multiple_of(i * TOK, TOK), TOK)
            mid = first[s, :, t] + dot(woutT[...], mixed[s, :, :, t].reshape(D, TOK))
            r = lax.rsqrt(jnp.mean(mid * mid, axis=0, keepdims=True) + EPS)
            sec = (mid * r * gain1).astype(bf16)
            second[:, t] = sec
            g = dout[s, :, t]
            for f in range(0, FF, 128):
                gate = dot(wguT[f : f + 128], sec)
                up = dot(wguT[FF + f : FF + f + 128], sec)
                gh = dot(wdown[f : f + 128], g)
                sig = 1.0 / (1.0 + jnp.exp(-gate))
                silu = gate * sig
                hidden[f : f + 128, t] = (silu * up).astype(bf16)
                both[FF + f : FF + f + 128, t] = (gh * silu).astype(bf16)
                both[f : f + 128, t] = (gh * up * (sig + silu * (1.0 - sig))).astype(bf16)
            out[s, :, t] = (mid + dot(wdownT[...], hidden[:, t])).astype(bf16)
            c = dot(wgu[...], both[:, t])
            cg = c * gain1
            inner = jnp.mean(cg * mid, axis=0, keepdims=True)
            gain_part = c * mid * r
            g_gain[1] += gain_part[:, :128] + gain_part[:, 128:]
            gm = g.astype(f32) + r * cg - mid * (r * r * r * inner)
            gmid[s, :, t] = gm
            gb = gm.astype(bf16)
            gbranch[:, t] = gb
            gmixed[s, :, :, t] = dot(wout[...], gb).reshape(H, HD, TOK)

        add_to(m_down, dot(hidden[...], dout[s], 1, 1))
        add_to(m_gu, dot(second[...], both[...], 1, 1))
        add_to(m_out, dot(mixed[s].reshape(D, LEN), gbranch[...], 1, 1))

    store_out = pltpu.make_async_copy(out, out_h, sem_l.at[13])
    store_out.start()
    flat_b[...] = jnp.zeros_like(flat_b)
    pack(m_out, "out", flat_b, B_ROWS)
    pack(m_gu, "gu", flat_b, B_ROWS)
    pack(m_down, "down", flat_b, B_ROWS)
    all_b[...] = flat_b[...].reshape(all_b.shape).astype(bf16)
    a, b = Reduce(all_a, half_a, row_a, line_a, sem_c), Reduce(all_b, half_b, row_b, line_b, sem_d)
    b.first()

    @pl.loop(0, H)
    def _(h):
        attend_back(0, h, q, k, v, prob, rl, osum, gmixed, cosr, sinr, gjoint)

    b.second()

    @pl.loop(0, H)
    def _(h):
        attend_back(1, h, q, k, v, prob, rl, osum, gmixed, cosr, sinr, gjoint)

    b.third()

    @pl.loop(0, 2)
    def _(s):
        add_to(m_qkv, dot(normed[s], gjoint[s].reshape(3 * D, LEN), 1, 1))
        fac = jnp.where(s == 0, factor[:F, 0:1], factor[:F, 1:2])

        @pl.loop(0, LEN // TOK)
        def _(i):
            t = pl.ds(pl.multiple_of(i * TOK, TOK), TOK)
            c = dot(wqkv[...], gjoint[s, :, :, :, t].reshape(3 * D, TOK))
            x, r = first[s, :, t], inv1[s, :, t]
            cg = c * gain0
            inner = jnp.mean(cg * x, axis=0, keepdims=True)
            gain_part = c * x * r
            g_gain[0] += gain_part[:, :128] + gain_part[:, 128:]
            gf = (gmid[s, :, t] + r * cg - x * (r * r * r * inner)).astype(bf16)
            gfirst[:, t] = gf
            gfeats[s, :, t] = (dot(win[...], gf) * fac).astype(bf16)

        add_to(m_in, dot(lifted[s], gfirst[...], 1, 1))

    store_gfeats = pltpu.make_async_copy(gfeats, gfeats_h, sem_l.at[14])
    store_gfeats.start()
    flat_a[...] = jnp.zeros_like(flat_a)
    pack(m_in, "in", flat_a, A_ROWS)
    pack(m_qkv, "qkv", flat_a, A_ROWS)
    gain_rows(g_gain, flat_a)
    flat_a[pl.ds(5, 128, stride=A_ROWS), :] = jnp.broadcast_to(stats[...], (128, 128))
    all_a[...] = flat_a[...].reshape(all_a.shape)
    a.first()
    a.second()
    tot_b[...] = b.last()
    a.third()
    tot_a[...] = a.last()
    store_out.wait()
    store_gfeats.wait()


def run_layer(feats_t, targets, lag_mask, date_mask, freq_ids, dataset_ids, weights, gains, dout_t):
    cos, sin = rope_tables()
    sd, V = jax.ShapeDtypeStruct, pltpu.VMEM
    shapes = [(ROWS[n], SPECS[n][0]) for n in NAMES]
    return pl.pallas_call(
        layer_kernel,
        in_specs=[HB] * 4 + [SM] * 2 + [HB] * 9,
        out_specs=[HB, HB, VM, VM],
        out_shape=[sd((2, D, LEN), bf16), sd((2, F, LEN), bf16), sd((A_ROWS, 128), f32), sd((B_ROWS, 128), f32)],
        scratch_shapes=[
            V((2, F, LEN), bf16), V((2, D, LEN), bf16), V((2, LEN), f32), V((2, NLAG), jnp.int32), V((2, NDATE), jnp.int32),
            *[V((SPECS[n][1],), bf16) for n in NAMES], V((2, 9), bf16), V((8, LEN), f32), V((8, LEN), f32),
            V((2, D, LEN), bf16), V((2, F, LEN), bf16),
            V((A_ROWS, 128), f32), V((B_ROWS, 128), bf16),
            V((2, 16, 4, A_ROWS, 128), f32), V((2, 16, 4, B_ROWS, 128), bf16),
            V((128 * A_ROWS, 128), f32), V((128 * B_ROWS, 128), f32),
            V((16, 4, A_ROWS, 128), f32), V((16, 4, B_ROWS, 128), bf16),
            V((16, 4, A_ROWS, 128), f32), V((16, 4, B_ROWS, 128), bf16),
            V((4, A_ROWS, 128), f32), V((4, B_ROWS, 128), bf16),
            *[V(tiled(n), f32) for n in NAMES], *[V(s, bf16) for s in shapes], *[V(s[::-1], bf16) for s in shapes],
            V((D, 2), f32), V((2, D, 128), f32), V((128, 8), f32), V((1, 128), f32),
            V((2, F, LEN), bf16), V((2, D, LEN), f32), V((2, 1, LEN), f32), V((2, D, LEN), bf16),
            V((2, H, HD, LEN), bf16), V((2, H, HD, LEN), bf16), V((2, H, HD, LEN), bf16),
            *[V((2, H, (j + 1) * QT, QT), bf16) for j in range(4)],
            V((2, LEN, QT), f32), V((2, H, 1, LEN), f32), V((2, H, HD, LEN), f32), V((2, H, HD, LEN), bf16),
            V((D, LEN), bf16), V((FF, LEN), bf16), V((2 * FF, LEN), bf16),
            V((2, D, LEN), f32), V((D, LEN), bf16), V((2, H, HD, LEN), f32), V((2, 3, H, HD, LEN), bf16), V((D, LEN), bf16),
            *[pltpu.SemaphoreType.DMA((2, 3))] * 4, pltpu.SemaphoreType.DMA((15,)),
        ],
        compiler_params=pltpu.CompilerParams(collective_id=0, has_side_effects=True, vmem_limit_bytes=63 * 2**20),
    )(feats_t, targets, lag_mask, date_mask, freq_ids, dataset_ids, *weights, gains, dout_t, jnp.asarray(cos), jnp.asarray(sin))


def finish_kernel(out_h, gfeats_h, tot_a_h, tot_b_h, running_h, out, gfeats, o_in, o_qkv, o_out, o_gu, o_down, o_gain, o_running,
                  tot_a, tot_b, running, sems):
    pairs = ((out_h, out), (gfeats_h, gfeats), (tot_a_h, tot_a), (tot_b_h, tot_b), (running_h, running))
    copies = [pltpu.make_async_copy(src, dst, sems.at[i]) for i, (src, dst) in enumerate(pairs)]
    for copy in copies:
        copy.start()
    for copy in copies[2:]:
        copy.wait()
    for name, ref in (("in", o_in), ("qkv", o_qkv), ("out", o_out), ("gu", o_gu), ("down", o_down)):
        _, chunk, _, _, which, base = SPECS[name]
        for t, at, width in lane_tiles(chunk):
            ref[pl.ds(at, width)] = (tot_a if which == "a" else tot_b)[base + t, :width]
    o_gain[0:1, :] = tot_a[0:1, 108:117]
    o_gain[1:2, :] = tot_a[0:1, 117:126]
    sums, counts = tot_a[5, :NSET], tot_a[5, NSET : 2 * NSET]
    old = running[...]
    o_running[...] = jnp.where(counts > 0.5, 0.75 * old + 0.25 * (sums / jnp.maximum(counts, 1.0)), old)
    for copy in copies[:2]:
        copy.wait()


def hand_out(out, gfeats, tot_a, tot_b, running):
    sd, V = jax.ShapeDtypeStruct, pltpu.VMEM
    return pl.pallas_call(
        finish_kernel,
        in_specs=[HB] * 5,
        out_specs=[HB, HB] + [VM] * 7,
        out_shape=[sd((2, D, LEN), bf16), sd((2, F, LEN), bf16)]
        + [sd((SPECS[n][1],), f32) for n in NAMES] + [sd((2, 9), f32), sd((NSET,), f32)],
        scratch_shapes=[V((A_ROWS, 128), f32), V((B_ROWS, 128), f32), V((NSET,), f32), pltpu.SemaphoreType.DMA((5,))],
        compiler_params=pltpu.CompilerParams(vmem_limit_bytes=60 * 2**20),
    )(out, gfeats, tot_a, tot_b, running)


def body(feats, targets, lag_mask, date_mask, freq_ids, dataset_ids, w_in, w_qkv, w_out, w_gu, w_down, gains, running, d_out):
    done = run_layer(
        jnp.swapaxes(feats, 1, 2), targets, lag_mask, date_mask, freq_ids, dataset_ids,
        (w_in, w_qkv, w_out, w_gu, w_down), gains, jnp.swapaxes(d_out, 1, 2),
    )
    out, gfeats, *rest = hand_out(*done, running)
    return (jnp.swapaxes(out, 1, 2), jnp.swapaxes(gfeats, 1, 2), *rest)


def solution(mesh):
    flat, rows, cube = P(BOTH), P(BOTH, None), P(BOTH, None, None)
    return jax.shard_map(
        body,
        mesh=mesh,
        in_specs=(cube, rows, rows, rows, flat, flat, flat, flat, flat, flat, flat, P(None, "dp"), P(), cube),
        out_specs=(cube, cube, flat, flat, flat, flat, flat, P(None, "dp"), P()),
        check_vma=False,
    )
```

```python
import functools

import jax
import jax.numpy as jnp
import numpy as np
from jax import lax
from jax.experimental import pallas as pl
from jax.experimental.pallas import tpu as pltpu
from jax.sharding import PartitionSpec as P

D, H, HD, FF, NDATE, NLAG, F, NSET, LEN = 144, 9, 16, 512, 12, 84, 96, 8, 1024
EPS = 1e-05
TOK = 256
QT = 256
CH = 128
GROUP = 3
f32, bf16 = jnp.float32, jnp.bfloat16
MESH = pl.DeviceIdType.MESH
BOTH = ("dp", "fsdp")

A_ROWS, B_ROWS = 8, 16
SPECS = {
    "in": (D, 108, 4, 3, "a", 0),
    "qkv": (3 * D, 486, 8, 9, "a", 1),
    "gu": (2 * FF, 1152, 8, 9, "b", 0),
    "down": (D, 576, 2, 8, "b", 9),
    "out": (D, 162, 8, 9, "b", 14),
}
ROWS = {"in": F, "qkv": D, "gu": D, "down": FF, "out": D}


def dot(a, b, ca=1, cb=0, **kw):
    return lax.dot_general(a, b, (((ca,), (cb,)), ((), ())), preferred_element_type=f32, **kw)


def lane_tiles(width):
    return [(t // 128, t, min(128, width - t)) for t in range(0, width, 128)]


def pieces(piece, source, count):
    cuts = []
    for i in range(count):
        at, left, parts = i * piece, piece, []
        while left:
            c, o = divmod(at, source)
            n = min(left, source - o)
            parts.append((c, o, n))
            at, left = at + n, left - n
        cuts.append(parts)
    return cuts


def spot(c):
    return (c % 2) * 64 + c // 2


def join(parts):
    return parts[0] if len(parts) == 1 else jnp.concatenate(parts, axis=1)


def unpack(flat, rows, name, dst):
    cols, chunk, gc, gr, _, base = SPECS[name]
    groups, kept = 128 // gc, {}

    def owner(c):
        if c not in kept:
            kept[c] = join(
                [flat[pl.ds(spot(c) * rows + base + t, groups, stride=gc // 2 * rows), :] for t, _, _ in lane_tiles(chunk)]
            )
        return kept[c]

    for i, parts in enumerate(pieces(cols, chunk, gr)):
        row = join([owner(c)[:, o : o + n] for c, o, n in parts])
        for t, at, width in lane_tiles(cols):
            dst[t, pl.ds(i, groups, stride=gr), :width] = row[:, at : at + width]


def pack(src, name, flat, rows):
    cols, chunk, gc, gr, _, base = SPECS[name]
    groups, kept = 128 // gc, {}

    def line(i):
        if i not in kept:
            kept[i] = join([src[t, pl.ds(i, groups, stride=gr), :] for t, _, _ in lane_tiles(cols)])
        return kept[i]

    for c, parts in enumerate(pieces(chunk, cols, gc)):
        run = [line(i)[:, o : o + n] for i, o, n in parts]
        run = join(run + ([jnp.zeros((groups, -chunk % 128), f32)] if chunk % 128 else []))
        for t, at, _ in lane_tiles(chunk):
            flat[pl.ds(spot(c) * rows + base + t, groups, stride=gc // 2 * rows), :] = run[:, at : at + 128]


def place():
    fs = lax.axis_index("fsdp")
    return lax.axis_index("dp"), fs // 2, fs % 2


def partners():
    dp, y, core = place()
    across = lambda o: (lax.rem(dp + o, 16), 2 * y + core)
    along = lambda o: (dp, 2 * lax.rem(y + o, 4) + core)
    return across, along, (dp, 2 * y + 1 - core)


def enter():
    across, along, sibling = partners()
    barrier = pltpu.get_barrier_semaphore()

    @pl.loop(1, 16)
    def _(o):
        pl.semaphore_signal(barrier, inc=1, device_id=across(o), device_id_type=MESH)

    for o in (1, 2, 3):
        pl.semaphore_signal(barrier, inc=1, device_id=along(o), device_id_type=MESH)
    pl.semaphore_signal(barrier, inc=1, device_id=sibling, device_id_type=MESH)
    pl.semaphore_wait(barrier, 19)


def send(src, dst, sems, k, to):
    pltpu.make_async_remote_copy(
        src_ref=src, dst_ref=dst, send_sem=sems.at[0, k], recv_sem=sems.at[1, k], device_id=to, device_id_type=MESH
    ).start()


def wait(ref, sem):
    pltpu.make_async_copy(ref, ref, sem).wait()


class Gather:
    def __init__(self, own, everyone, sems):
        self.own, self.all, self.sems = own, everyone, sems

    def first(self):
        dp, y, core = place()
        _, along, _ = partners()
        for o in (1, 2, 3):
            send(self.own, self.all.at[core, dp, y], self.sems, 0, along(o))
        self.all[core, dp, y] = self.own[...]

    def second(self):
        dp, y, core = place()
        across, _, _ = partners()
        wait(self.all.at[core, dp, pl.ds(0, 3)], self.sems.at[1, 0])
        wait(self.all.at[core, dp, pl.ds(0, 3)], self.sems.at[0, 0])
        line = self.all.at[core, dp]

        @pl.loop(1, 16)
        def _(o):
            send(line, line, self.sems, 1, across(o))

    def third(self):
        _, _, core = place()
        _, _, sibling = partners()
        wait(self.all.at[core, pl.ds(0, 15)], self.sems.at[1, 1])
        wait(self.all.at[core, pl.ds(0, 15)], self.sems.at[0, 1])
        send(self.all.at[core], self.all.at[core], self.sems, 2, sibling)

    def last(self):
        _, _, core = place()
        wait(self.all.at[core], self.sems.at[1, 2])
        wait(self.all.at[core], self.sems.at[0, 2])


class Reduce:
    def __init__(self, parts, half, row, line, sems):
        self.parts, self.half, self.row, self.line, self.sems = parts, half, row, line, sems

    def first(self):
        _, _, core = place()
        _, _, sibling = partners()
        send(self.parts.at[1 - core], self.half, self.sems, 0, sibling)

    def second(self):
        dp, y, core = place()
        across, _, _ = partners()
        wait(self.half, self.sems.at[1, 0])
        wait(self.half, self.sems.at[0, 0])
        self.half[...] = (self.half[...].astype(f32) + self.parts[core].astype(f32)).astype(self.half.dtype)

        @pl.loop(1, 16)
        def _(o):
            send(self.half.at[lax.rem(dp + o, 16)], self.row.at[dp], self.sems, 1, across(o))

        self.row[dp] = self.half[dp]

    def third(self):
        dp, y, core = place()
        _, along, _ = partners()
        wait(self.row.at[pl.ds(0, 15)], self.sems.at[1, 1])
        wait(self.row.at[pl.ds(0, 15)], self.sems.at[0, 1])
        mine = jnp.sum(self.row[...].astype(f32), axis=0).astype(self.row.dtype)
        self.half[0] = mine
        for o in (1, 2, 3):
            send(self.half.at[0, lax.rem(y + o, 4)], self.line.at[y], self.sems, 2, along(o))
        self.line[y] = self.half[0, y]

    def last(self):
        wait(self.line.at[pl.ds(0, 3)], self.sems.at[1, 2])
        wait(self.line.at[pl.ds(0, 3)], self.sems.at[0, 2])
        return jnp.sum(self.line[...].astype(f32), axis=0)


def rope_tables():
    freqs = np.float32(10000.0) ** (-np.arange(HD // 2, dtype=np.float32) * np.float32(2.0) / np.float32(HD))
    angle = np.arange(LEN, dtype=np.float32)[None, :] * freqs.astype(np.float32)[:, None]
    return np.cos(angle.astype(np.float64)).astype(np.float32), np.sin(angle.astype(np.float64)).astype(np.float32)


def own_tiles(w_in, w_qkv, w_out, w_gu, w_down, gains, tile_a, tile_b, wide):
    tile_a[...] = jnp.zeros_like(tile_a)
    wide[...] = jnp.zeros_like(wide)
    for name, ref in (("in", w_in), ("qkv", w_qkv), ("out", w_out), ("gu", w_gu), ("down", w_down)):
        _, chunk, _, _, which, base = SPECS[name]
        for t, at, width in lane_tiles(chunk):
            (tile_a if which == "a" else wide)[base + t, :width] = ref[pl.ds(at, width)].astype(f32)
    tile_a[0:1, 108:117] = gains[0:1, :].astype(f32)
    tile_a[0:1, 117:126] = gains[1:2, :].astype(f32)
    tile_b[...] = wide[...].astype(bf16)


def gain_columns(flat, out):
    rows = flat[pl.ds(0, 16, stride=4 * A_ROWS), :]
    r = lax.broadcasted_iota(jnp.int32, (D, 16), 0) // 9
    spread = dot((r == lax.broadcasted_iota(jnp.int32, (D, 16), 1)).astype(f32), rows)
    lane = lax.broadcasted_iota(jnp.int32, (D, 128), 1)
    e = lax.rem(lax.broadcasted_iota(jnp.int32, (D, 128), 0), 9)
    for i in (0, 1):
        out[:, i : i + 1] = jnp.sum(jnp.where(lane == e + 108 + 9 * i, spread, 0.0), axis=1, keepdims=True)


def gain_rows(partial, flat):
    pos = lax.broadcasted_iota(jnp.int32, (128, D), 0)
    r = lax.broadcasted_iota(jnp.int32, (128, D), 1) // 9
    pick = (lax.rem(pos, 64) // 4 == r).astype(f32)
    lane = lax.broadcasted_iota(jnp.int32, (D, 128), 1)
    e = lax.rem(lax.broadcasted_iota(jnp.int32, (D, 128), 0), 9)
    cols = jnp.zeros((D, 128), f32)
    for i in (0, 1):
        cols += jnp.where(lane == e + 108 + 9 * i, jnp.sum(partial[i], axis=1, keepdims=True), 0.0)
    spread = dot(pick, cols, precision=lax.Precision.HIGHEST)
    flat[pl.ds(0, 128, stride=A_ROWS), :] += spread


def series_scalars(targets, lag_mask, date_mask, freq, sets, factor, stats):
    scale = jnp.sum(jnp.abs(targets[...]), axis=1, keepdims=True) / LEN + 1e-5
    lag = lag_mask[...].astype(f32) / scale
    second = lax.broadcasted_iota(jnp.int32, (2, NDATE), 0) == 1
    start = jnp.where(second, freq[1], freq[0]) * (NDATE // 3)
    keep = jnp.where(lax.broadcasted_iota(jnp.int32, (2, NDATE), 1) >= start, date_mask[...], 0).astype(f32)
    both = jnp.concatenate([lag, keep], axis=1)
    both = jnp.concatenate([both, jnp.zeros((2, 32), f32)], axis=1)
    both = jnp.concatenate([both, jnp.zeros((6, 128), f32)], axis=0)
    factor[...] = both.T
    lane = lax.broadcasted_iota(jnp.int32, (1, 128), 1)
    row = jnp.zeros((1, 128), f32)
    for s in (0, 1):
        row += jnp.where(lane == sets[s], scale[s : s + 1], 0.0) + jnp.where(lane == sets[s] + NSET, 1.0, 0.0)
    stats[...] = row

def fold(op, a):
    return op(a.reshape(a.shape[0] // 8, 8, a.shape[1]), axis=0)


def weave(gens):
    gens = list(gens)
    while gens:
        for g in list(gens):
            try:
                next(g)
            except StopIteration:
                gens.remove(g)


VM = pl.BlockSpec(memory_space=pltpu.VMEM)
SM = pl.BlockSpec(memory_space=pltpu.SMEM)
HB = pl.BlockSpec(memory_space=pl.ANY)
NAMES = ("in", "qkv", "out", "gu", "down")


def tiled(name):
    return (-(-SPECS[name][0] // 128), ROWS[name], 128)


def attend(s, hh, q, k, v, prob, sbuf, rl, osum, mixed):
    diag = lambda c0: (lax.broadcasted_iota(jnp.int32, (CH, QT), 0) + c0) <= lax.broadcasted_iota(jnp.int32, (CH, QT), 1)
    heads = [hh * GROUP + u for u in range(GROUP)]
    kts = [k[s, h].astype(f32).T.astype(bf16) for h in heads]
    ones = (lax.broadcasted_iota(jnp.int32, (HD, LEN), 0) == 0).astype(f32).astype(bf16)
    vs = [jnp.concatenate([v[s, h], ones], axis=0) for h in heads]
    tasks = [(u, j) for j in range(LEN // QT - 1, -1, -1) for u in range(GROUP)]
    tops = {}

    def score(i):
        u, j = tasks[i]
        n, best = (j + 1) * QT, None
        for c in range(0, n, CH):
            x = dot(kts[u][c : c + CH], q[s, heads[u], :, j * QT : j * QT + QT])
            if c + CH > n - QT:
                x = jnp.where(diag(c - (n - QT)), x, -1e30)
            sbuf[i % 2, c : c + CH] = x
            top = fold(jnp.max, x)
            best = top if best is None else jnp.maximum(best, top)
            yield
        tops[i] = jnp.max(best, axis=0, keepdims=True)

    def exponent(i):
        u, j = tasks[i]
        for c in range(0, (j + 1) * QT, CH):
            prob[j][s, heads[u], c : c + CH] = jnp.exp(sbuf[i % 2, c : c + CH] - tops[i]).astype(bf16)
            yield

    def mix(i):
        u, j = tasks[i]
        h, n, cols = heads[u], (j + 1) * QT, pl.ds(j * QT, QT)
        o = dot(vs[u][:, :n], prob[j][s, h])
        inv = 1.0 / o[HD : HD + 1]
        o = o[:HD] * inv
        rl[s, h, :, cols] = inv
        osum[s, h, :, cols] = o
        mixed[s, h, :, cols] = o.astype(bf16)

    last = len(tasks)
    for i in range(last + 3):
        if 0 <= i - 3:
            mix(i - 3)
        weave(([score(i)] if i < last else []) + ([exponent(i - 1)] if 0 <= i - 1 < last else []))


def attend_back(s, hh, q, k, v, prob, rl, osum, gmixed, cosr, sinr, gjoint, dsb, dq, dk, dv):
    heads = [hh * GROUP + u for u in range(GROUP)]
    dos, deltas, vts = [], [], []
    for h in heads:
        do = (gmixed[s, h] * rl[s, h]).astype(bf16)
        dos.append(do)
        deltas.append(jnp.sum(do.astype(f32) * osum[s, h], axis=0, keepdims=True))
        vts.append(v[s, h].astype(f32).T.astype(bf16))
    dk[...] = jnp.zeros_like(dk)
    dv[...] = jnp.zeros_like(dv)
    tasks = [(u, j) for j in range(LEN // QT - 1, -1, -1) for u in range(GROUP)]

    def spread(i):
        u, j = tasks[i]
        n = (j + 1) * QT
        cols = slice(j * QT, n)
        for c in range(0, n, QT):
            dp = dot(vts[u][c : c + QT], dos[u][:, cols]) - deltas[u][:, cols]
            dsb[i % 2, c : c + QT] = (prob[j][s, heads[u], c : c + QT].astype(f32) * dp).astype(bf16)
            yield

    def to_query(i):
        u, j = tasks[i]
        n = (j + 1) * QT
        dq[u, :, j * QT : n] = dot(k[s, heads[u]][:, :n], dsb[i % 2, :n])
        yield

    def to_keys(i):
        u, j = tasks[i]
        for c in range(0, (j + 1) * QT, QT):
            dk[u, :, c : c + QT] += dot(q[s, heads[u], :, j * QT : j * QT + QT], dsb[i % 2, c : c + QT], 1, 1)
            yield

    def to_values(i):
        u, j = tasks[i]
        for c in range(0, (j + 1) * QT, QT):
            dv[u, :, c : c + QT] += dot(dos[u][:, j * QT : j * QT + QT], prob[j][s, heads[u], c : c + QT], 1, 1)
            yield

    last = len(tasks)
    for i in range(last + 1):
        weave(([spread(i)] if i < last else []) + ([to_query(i - 1), to_keys(i - 1), to_values(i - 1)] if i else []))
    c, sn = cosr[...], sinr[...]
    for u, h in enumerate(heads):
        for which, val in ((0, dq[u] * 0.25), (1, dk[u])):
            a, b = val[:8], val[8:]
            gjoint[s, which, h] = jnp.concatenate([a * c + b * sn, b * c - a * sn], axis=0).astype(bf16)
        gjoint[s, 2, h] = dv[u].astype(bf16)


def layer_kernel(
    feats_h, targets_h, lag_h, date_h, freq, sets, w_in_h, w_qkv_h, w_out_h, w_gu_h, w_down_h, gains_h, dout_h, cos_h, sin_h,
    out_h, gfeats_h, tot_a, tot_b,
    feats, dout, targets, lag_mask, date_mask, w_in, w_qkv, w_out, w_gu, w_down, gains_own, cosr, sinr, out, gfeats,
    tile_a, tile_b, all_a, all_b, flat_a, flat_b, half_a, half_b, row_a, row_b, line_a, line_b,
    m_in, m_qkv, m_out, m_gu, m_down, win, wqkv, wout, wgu, wdown, winT, wqkvT, woutT, wguT, wdownT,
    gains, g_gain, factor, stats, lifted, first, inv1, normed, q, k, v, p0, p1, p2, p3, sbuf, rl, osum, mixed, second, hidden, both,
    gmid, gbranch, gmixed, gjoint, gfirst, dsb, dq, dk, dv, sem_a, sem_b, sem_c, sem_d, sem_l,
):
    prob = (p0, p1, p2, p3)
    loads = [
        pltpu.make_async_copy(src, dst, sem_l.at[i])
        for i, (src, dst) in enumerate(
            (
                (w_in_h, w_in), (w_qkv_h, w_qkv), (w_out_h, w_out), (w_gu_h, w_gu), (w_down_h, w_down), (gains_h, gains_own),
                (feats_h, feats), (targets_h, targets), (lag_h, lag_mask), (date_h, date_mask), (cos_h, cosr), (sin_h, sinr), (dout_h, dout),
            )
        )
    ]
    for load in loads:
        load.start()
    for load in loads[:6]:
        load.wait()
    own_tiles(w_in, w_qkv, w_out, w_gu, w_down, gains_own, tile_a, tile_b, flat_b.at[pl.ds(0, B_ROWS)])
    enter()
    a, b = Gather(tile_a, all_a, sem_a), Gather(tile_b, all_b, sem_b)
    a.first()
    b.first()
    for load in loads[6:12]:
        load.wait()
    series_scalars(targets, lag_mask, date_mask, freq, sets, factor, stats)
    g_gain[...] = jnp.zeros_like(g_gain)
    for s in (0, 1):
        lifted[s] = (feats[s].astype(f32) * factor[:F, s : s + 1]).astype(bf16)
    a.second()
    a.third()
    b.second()
    a.last()
    flat_a[...] = all_a[...].reshape(128 * A_ROWS, 128)
    gain_columns(flat_a, gains)

    def emit(name, flat, rows, mat, out, outT):
        unpack(flat, rows, name, mat)
        for t, at, width in lane_tiles(SPECS[name][0]):
            val = mat[t][:, :width]
            out[:, at : at + width] = val.astype(bf16)
            outT[at : at + width, :] = val.T.astype(bf16)
        mat[...] = jnp.zeros_like(mat)

    emit("in", flat_a, A_ROWS, m_in, win, winT)
    emit("qkv", flat_a, A_ROWS, m_qkv, wqkv, wqkvT)

    def add_to(ref, val):
        for t, at, width in lane_tiles(val.shape[1]):
            ref[t, :, :width] += val[:, at : at + width]

    gain0 = gains[:, 0:1]
    gain1 = gains[:, 1:2]

    @pl.loop(0, 2)
    def _(s):
        @pl.loop(0, LEN // TOK)
        def _(i):
            t = pl.ds(pl.multiple_of(i * TOK, TOK), TOK)
            x = dot(winT[...], lifted[s, :, t])
            first[s, :, t] = x
            r = lax.rsqrt(jnp.mean(x * x, axis=0, keepdims=True) + EPS)
            inv1[s, :, t] = r
            n = (x * r * gain0).astype(bf16)
            normed[s, :, t] = n
            joint = dot(wqkvT[...], n).reshape(3, H, HD, TOK)
            c, sn = cosr[:, t][None], sinr[:, t][None]
            for which, ref, scale in ((0, q, 0.25), (1, k, 1.0)):
                u, w = joint[which, :, :8], joint[which, :, 8:]
                ref[s, :, :, t] = (jnp.concatenate([u * c - w * sn, w * c + u * sn], axis=1) * scale).astype(bf16)
            v[s, :, :, t] = joint[2].astype(bf16)

    @pl.loop(0, H // GROUP)
    def _(hh):
        attend(0, hh, q, k, v, prob, sbuf, rl, osum, mixed)

    b.third()

    @pl.loop(0, H // GROUP)
    def _(hh):
        attend(1, hh, q, k, v, prob, sbuf, rl, osum, mixed)

    b.last()
    flat_b[...] = all_b[...].astype(f32).reshape(128 * B_ROWS, 128)
    emit("out", flat_b, B_ROWS, m_out, wout, woutT)
    emit("gu", flat_b, B_ROWS, m_gu, wgu, wguT)
    emit("down", flat_b, B_ROWS, m_down, wdown, wdownT)
    loads[12].wait()

    @pl.loop(0, 2)
    def _(s):
        @pl.loop(0, LEN // TOK)
        def _(i):
            t = pl.ds(pl.multiple_of(i * TOK, TOK), TOK)
            mid = first[s, :, t] + dot(woutT[...], mixed[s, :, :, t].reshape(D, TOK))
            r = lax.rsqrt(jnp.mean(mid * mid, axis=0, keepdims=True) + EPS)
            sec = (mid * r * gain1).astype(bf16)
            second[:, t] = sec
            g = dout[s, :, t]
            for f in range(0, FF, 128):
                gate = dot(wguT[f : f + 128], sec)
                up = dot(wguT[FF + f : FF + f + 128], sec)
                gh = dot(wdown[f : f + 128], g)
                sig = 1.0 / (1.0 + jnp.exp(-gate))
                silu = gate * sig
                hidden[f : f + 128, t] = (silu * up).astype(bf16)
                both[FF + f : FF + f + 128, t] = (gh * silu).astype(bf16)
                both[f : f + 128, t] = (gh * up * (sig + silu * (1.0 - sig))).astype(bf16)
            out[s, :, t] = (mid + dot(wdownT[...], hidden[:, t])).astype(bf16)
            c = dot(wgu[...], both[:, t])
            cg = c * gain1
            inner = jnp.mean(cg * mid, axis=0, keepdims=True)
            gain_part = c * mid * r
            g_gain[1] += gain_part[:, :128] + gain_part[:, 128:]
            gm = g.astype(f32) + r * cg - mid * (r * r * r * inner)
            gmid[s, :, t] = gm
            gb = gm.astype(bf16)
            gbranch[:, t] = gb
            gmixed[s, :, :, t] = dot(wout[...], gb).reshape(H, HD, TOK)

        add_to(m_down, dot(hidden[...], dout[s], 1, 1))
        add_to(m_gu, dot(second[...], both[...], 1, 1))
        add_to(m_out, dot(mixed[s].reshape(D, LEN), gbranch[...], 1, 1))

    store_out = pltpu.make_async_copy(out, out_h, sem_l.at[13])
    store_out.start()
    flat_b[...] = jnp.zeros_like(flat_b)
    pack(m_out, "out", flat_b, B_ROWS)
    pack(m_gu, "gu", flat_b, B_ROWS)
    pack(m_down, "down", flat_b, B_ROWS)
    all_b[...] = flat_b[...].reshape(all_b.shape).astype(bf16)
    a, b = Reduce(all_a, half_a, row_a, line_a, sem_c), Reduce(all_b, half_b, row_b, line_b, sem_d)
    b.first()

    @pl.loop(0, H // GROUP)
    def _(hh):
        attend_back(0, hh, q, k, v, prob, rl, osum, gmixed, cosr, sinr, gjoint, dsb, dq, dk, dv)

    b.second()

    @pl.loop(0, H // GROUP)
    def _(hh):
        attend_back(1, hh, q, k, v, prob, rl, osum, gmixed, cosr, sinr, gjoint, dsb, dq, dk, dv)

    b.third()

    @pl.loop(0, 2)
    def _(s):
        add_to(m_qkv, dot(normed[s], gjoint[s].reshape(3 * D, LEN), 1, 1))
        fac = jnp.where(s == 0, factor[:F, 0:1], factor[:F, 1:2])

        @pl.loop(0, LEN // TOK)
        def _(i):
            t = pl.ds(pl.multiple_of(i * TOK, TOK), TOK)
            c = dot(wqkv[...], gjoint[s, :, :, :, t].reshape(3 * D, TOK))
            x, r = first[s, :, t], inv1[s, :, t]
            cg = c * gain0
            inner = jnp.mean(cg * x, axis=0, keepdims=True)
            gain_part = c * x * r
            g_gain[0] += gain_part[:, :128] + gain_part[:, 128:]
            gf = (gmid[s, :, t] + r * cg - x * (r * r * r * inner)).astype(bf16)
            gfirst[:, t] = gf
            gfeats[s, :, t] = (dot(win[...], gf) * fac).astype(bf16)

        add_to(m_in, dot(lifted[s], gfirst[...], 1, 1))

    store_gfeats = pltpu.make_async_copy(gfeats, gfeats_h, sem_l.at[14])
    store_gfeats.start()
    flat_a[...] = jnp.zeros_like(flat_a)
    pack(m_in, "in", flat_a, A_ROWS)
    pack(m_qkv, "qkv", flat_a, A_ROWS)
    gain_rows(g_gain, flat_a)
    flat_a[pl.ds(5, 128, stride=A_ROWS), :] = jnp.broadcast_to(stats[...], (128, 128))
    all_a[...] = flat_a[...].reshape(all_a.shape)
    a.first()
    a.second()
    tot_b[...] = b.last()
    a.third()
    tot_a[...] = a.last()
    store_out.wait()
    store_gfeats.wait()


def run_layer(feats_t, targets, lag_mask, date_mask, freq_ids, dataset_ids, weights, gains, dout_t):
    cos, sin = rope_tables()
    sd, V = jax.ShapeDtypeStruct, pltpu.VMEM
    shapes = [(ROWS[n], SPECS[n][0]) for n in NAMES]
    return pl.pallas_call(
        layer_kernel,
        in_specs=[HB] * 4 + [SM] * 2 + [HB] * 9,
        out_specs=[HB, HB, VM, VM],
        out_shape=[sd((2, D, LEN), bf16), sd((2, F, LEN), bf16), sd((A_ROWS, 128), f32), sd((B_ROWS, 128), f32)],
        scratch_shapes=[
            V((2, F, LEN), bf16), V((2, D, LEN), bf16), V((2, LEN), f32), V((2, NLAG), jnp.int32), V((2, NDATE), jnp.int32),
            *[V((SPECS[n][1],), bf16) for n in NAMES], V((2, 9), bf16), V((8, LEN), f32), V((8, LEN), f32),
            V((2, D, LEN), bf16), V((2, F, LEN), bf16),
            V((A_ROWS, 128), f32), V((B_ROWS, 128), bf16),
            V((2, 16, 4, A_ROWS, 128), f32), V((2, 16, 4, B_ROWS, 128), bf16),
            V((128 * A_ROWS, 128), f32), V((128 * B_ROWS, 128), f32),
            V((16, 4, A_ROWS, 128), f32), V((16, 4, B_ROWS, 128), bf16),
            V((16, 4, A_ROWS, 128), f32), V((16, 4, B_ROWS, 128), bf16),
            V((4, A_ROWS, 128), f32), V((4, B_ROWS, 128), bf16),
            *[V(tiled(n), f32) for n in NAMES], *[V(s, bf16) for s in shapes], *[V(s[::-1], bf16) for s in shapes],
            V((D, 2), f32), V((2, D, 128), f32), V((128, 8), f32), V((1, 128), f32),
            V((2, F, LEN), bf16), V((2, D, LEN), f32), V((2, 1, LEN), f32), V((2, D, LEN), bf16),
            V((2, H, HD, LEN), bf16), V((2, H, HD, LEN), bf16), V((2, H, HD, LEN), bf16),
            *[V((2, H, (j + 1) * QT, QT), bf16) for j in range(4)],
            V((2, LEN, QT), f32), V((2, H, 1, LEN), f32), V((2, H, HD, LEN), f32), V((2, H, HD, LEN), bf16),
            V((D, LEN), bf16), V((FF, LEN), bf16), V((2 * FF, LEN), bf16),
            V((2, D, LEN), f32), V((D, LEN), bf16), V((2, H, HD, LEN), f32), V((2, 3, H, HD, LEN), bf16), V((D, LEN), bf16),
            V((2, LEN, QT), bf16), *[V((GROUP, HD, LEN), f32)] * 3,
            *[pltpu.SemaphoreType.DMA((2, 3))] * 4, pltpu.SemaphoreType.DMA((15,)),
        ],
        compiler_params=pltpu.CompilerParams(collective_id=0, has_side_effects=True, vmem_limit_bytes=63 * 2**20),
    )(feats_t, targets, lag_mask, date_mask, freq_ids, dataset_ids, *weights, gains, dout_t, jnp.asarray(cos), jnp.asarray(sin))


def finish_kernel(out_h, gfeats_h, tot_a_h, tot_b_h, running_h, out, gfeats, o_in, o_qkv, o_out, o_gu, o_down, o_gain, o_running,
                  out_v, gfeats_v, tot_a, tot_b, running, sems):
    pairs = ((tot_a_h, tot_a), (tot_b_h, tot_b), (running_h, running), (out_h, out_v), (gfeats_h, gfeats_v))
    copies = [pltpu.make_async_copy(src, dst, sems.at[i]) for i, (src, dst) in enumerate(pairs)]
    stores = [pltpu.make_async_copy(src, dst, sems.at[5 + i]) for i, (src, dst) in enumerate(((out_v, out), (gfeats_v, gfeats)))]
    for copy in copies:
        copy.start()
    for copy in copies:
        copy.wait()
    for store in stores:
        store.start()
    for name, ref in (("in", o_in), ("qkv", o_qkv), ("out", o_out), ("gu", o_gu), ("down", o_down)):
        _, chunk, _, _, which, base = SPECS[name]
        for t, at, width in lane_tiles(chunk):
            ref[pl.ds(at, width)] = (tot_a if which == "a" else tot_b)[base + t, :width]
    o_gain[0:1, :] = tot_a[0:1, 108:117]
    o_gain[1:2, :] = tot_a[0:1, 117:126]
    sums, counts = tot_a[5, :NSET], tot_a[5, NSET : 2 * NSET]
    old = running[...]
    o_running[...] = jnp.where(counts > 0.5, 0.75 * old + 0.25 * (sums / jnp.maximum(counts, 1.0)), old)
    for store in stores:
        store.wait()


def hand_out(out, gfeats, tot_a, tot_b, running):
    sd, V = jax.ShapeDtypeStruct, pltpu.VMEM
    return pl.pallas_call(
        finish_kernel,
        in_specs=[HB] * 5,
        out_specs=[HB, HB] + [VM] * 7,
        out_shape=[sd((2, D, LEN), bf16), sd((2, F, LEN), bf16)]
        + [sd((SPECS[n][1],), f32) for n in NAMES] + [sd((2, 9), f32), sd((NSET,), f32)],
        scratch_shapes=[V((2, D, LEN), bf16), V((2, F, LEN), bf16), V((A_ROWS, 128), f32), V((B_ROWS, 128), f32), V((NSET,), f32),
                        pltpu.SemaphoreType.DMA((7,))],
        compiler_params=pltpu.CompilerParams(vmem_limit_bytes=60 * 2**20),
    )(out, gfeats, tot_a, tot_b, running)


def body(feats, targets, lag_mask, date_mask, freq_ids, dataset_ids, w_in, w_qkv, w_out, w_gu, w_down, gains, running, d_out):
    done = run_layer(
        jnp.swapaxes(feats, 1, 2), targets, lag_mask, date_mask, freq_ids, dataset_ids,
        (w_in, w_qkv, w_out, w_gu, w_down), gains, jnp.swapaxes(d_out, 1, 2),
    )
    out, gfeats, *rest = hand_out(*done, running)
    return (jnp.swapaxes(out, 1, 2), jnp.swapaxes(gfeats, 1, 2), *rest)


def solution(mesh):
    flat, rows, cube = P(BOTH), P(BOTH, None), P(BOTH, None, None)
    return jax.shard_map(
        body,
        mesh=mesh,
        in_specs=(cube, rows, rows, rows, flat, flat, flat, flat, flat, flat, flat, P(None, "dp"), P(), cube),
        out_specs=(cube, cube, flat, flat, flat, flat, flat, P(None, "dp"), P()),
        check_vma=False,
    )
```

```python
import functools

import jax
import jax.numpy as jnp
import numpy as np
from jax import lax
from jax.experimental import pallas as pl
from jax.experimental.pallas import tpu as pltpu
from jax.sharding import PartitionSpec as P

D, H, HD, FF, NDATE, NLAG, F, NSET, LEN = 144, 9, 16, 512, 12, 84, 96, 8, 1024
EPS = 1e-05
TOK_IN = 1024
TOK_MLP = 1024
TOK_BACK = 1024
QT = 256
CH = 128
GROUP = 9
f32, bf16 = jnp.float32, jnp.bfloat16
MESH = pl.DeviceIdType.MESH
BOTH = ("dp", "fsdp")

A_ROWS, B_ROWS = 8, 16
SPECS = {
    "in": (D, 108, 4, 3, "a", 0),
    "qkv": (3 * D, 486, 8, 9, "a", 1),
    "gu": (2 * FF, 1152, 8, 9, "b", 0),
    "down": (D, 576, 2, 8, "b", 9),
    "out": (D, 162, 8, 9, "b", 14),
}
ROWS = {"in": F, "qkv": D, "gu": D, "down": FF, "out": D}


def dot(a, b, ca=1, cb=0, **kw):
    return lax.dot_general(a, b, (((ca,), (cb,)), ((), ())), preferred_element_type=f32, **kw)


def lane_tiles(width):
    return [(t // 128, t, min(128, width - t)) for t in range(0, width, 128)]


def pieces(piece, source, count):
    cuts = []
    for i in range(count):
        at, left, parts = i * piece, piece, []
        while left:
            c, o = divmod(at, source)
            n = min(left, source - o)
            parts.append((c, o, n))
            at, left = at + n, left - n
        cuts.append(parts)
    return cuts


def spot(c):
    return (c % 2) * 64 + c // 2


def join(parts):
    return parts[0] if len(parts) == 1 else jnp.concatenate(parts, axis=1)


def unpack(flat, rows, name, dst):
    cols, chunk, gc, gr, _, base = SPECS[name]
    groups, kept = 128 // gc, {}

    def owner(c):
        if c not in kept:
            kept[c] = join(
                [flat[pl.ds(spot(c) * rows + base + t, groups, stride=gc // 2 * rows), :] for t, _, _ in lane_tiles(chunk)]
            )
        return kept[c]

    for i, parts in enumerate(pieces(cols, chunk, gr)):
        row = join([owner(c)[:, o : o + n] for c, o, n in parts])
        for t, at, width in lane_tiles(cols):
            dst[t, pl.ds(i, groups, stride=gr), :width] = row[:, at : at + width]


def pack(src, name, flat, rows):
    cols, chunk, gc, gr, _, base = SPECS[name]
    groups, kept = 128 // gc, {}

    def line(i):
        if i not in kept:
            kept[i] = join([src[t, pl.ds(i, groups, stride=gr), :] for t, _, _ in lane_tiles(cols)])
        return kept[i]

    for c, parts in enumerate(pieces(chunk, cols, gc)):
        run = [line(i)[:, o : o + n] for i, o, n in parts]
        run = join(run + ([jnp.zeros((groups, -chunk % 128), f32)] if chunk % 128 else []))
        for t, at, _ in lane_tiles(chunk):
            flat[pl.ds(spot(c) * rows + base + t, groups, stride=gc // 2 * rows), :] = run[:, at : at + 128]


def place():
    fs = lax.axis_index("fsdp")
    return lax.axis_index("dp"), fs // 2, fs % 2


def partners():
    dp, y, core = place()
    across = lambda o: (lax.rem(dp + o, 16), 2 * y + core)
    along = lambda o: (dp, 2 * lax.rem(y + o, 4) + core)
    return across, along, (dp, 2 * y + 1 - core)


def chip(dz, dx, dy):
    dp, y, _ = place()
    z, x = dp // 4, lax.rem(dp, 4)
    return 4 * lax.rem(z + dz, 4) + lax.rem(x + dx, 4), lax.rem(y + dy, 4)


def device(dz, dx, dy):
    dp, y = chip(dz, dx, dy)
    return dp, 2 * y + place()[2]


STEPS = (1, 2, 3)
LINES = [(0, 0, o) for o in STEPS] + [(0, o, 0) for o in STEPS] + [(o, 0, 0) for o in STEPS]
X_PLANES = [(0, o, p) for o in STEPS for p in STEPS] + [(p, o, 0) for o in STEPS for p in STEPS]
REST = [(o, p, r) for o in STEPS for p in STEPS for r in STEPS] + [(o, 0, p) for o in STEPS for p in STEPS]


def signal(sem, to):
    pl.semaphore_signal(sem, inc=1, device_id=to, device_id_type=MESH)


def knock():
    barrier = pltpu.get_barrier_semaphore()
    for line in LINES:
        signal(barrier, device(*line))
    signal(barrier, partners()[2])


def enter(sem_x, sem_z, send_to, work):
    pl.semaphore_wait(pltpu.get_barrier_semaphore(), 10)
    for o in STEPS:
        signal(sem_x, device(0, o, 0))
    for line in LINES:
        send_to(*line)
    work[0]()
    pl.semaphore_wait(sem_x, 3)
    for o in STEPS:
        signal(sem_z, device(o, 0, 0))
    for line in X_PLANES:
        send_to(*line)
    work[1]()
    pl.semaphore_wait(sem_z, 3)
    for line in REST:
        send_to(*line)


def send(src, dst, sems, k, to):
    pltpu.make_async_remote_copy(
        src_ref=src, dst_ref=dst, send_sem=sems.at[0, k], recv_sem=sems.at[1, k], device_id=to, device_id_type=MESH
    ).start()


def wait(ref, sem):
    pltpu.make_async_copy(ref, ref, sem).wait()


class GatherDirect:
    def __init__(self, own, everyone, sems):
        self.own, self.all, self.sems = own, everyone, sems

    def to(self, *line):
        dp, y, core = place()
        send(self.own, self.all.at[core, 4 * dp + y], self.sems, 0, device(*line))

    def second(self):
        dp, y, core = place()
        self.all[core, 4 * dp + y] = self.own[...]
        wait(self.all.at[core, pl.ds(0, 63)], self.sems.at[1, 0])
        wait(self.all.at[core, pl.ds(0, 63)], self.sems.at[0, 0])
        send(self.all.at[core], self.all.at[core], self.sems, 1, partners()[2])

    def last(self):
        _, _, core = place()
        wait(self.all.at[core], self.sems.at[1, 1])
        wait(self.all.at[core], self.sems.at[0, 1])


class ReduceDirect:
    def __init__(self, parts, half, got, sems):
        self.parts, self.half, self.got, self.sems = parts, half, got, sems

    def first(self):
        _, _, core = place()
        send(self.parts.at[1 - core], self.half, self.sems, 0, partners()[2])

    def second(self):
        dp, y, core = place()
        wait(self.half, self.sems.at[1, 0])
        wait(self.half, self.sems.at[0, 0])
        self.half[...] += self.parts[core]
        for line in REST + X_PLANES + LINES:
            to_dp, to_y = chip(*line)
            send(self.half.at[4 * to_dp + to_y], self.got.at[4 * dp + y], self.sems, 1, device(*line))
        self.got[4 * dp + y] = self.half[4 * dp + y]

    def last(self):
        wait(self.got.at[pl.ds(0, 63)], self.sems.at[1, 1])
        wait(self.got.at[pl.ds(0, 63)], self.sems.at[0, 1])
        return jnp.sum(self.got[...], axis=0)


class Gather:
    def __init__(self, own, everyone, sems):
        self.own, self.all, self.sems = own, everyone, sems

    def first(self):
        dp, y, core = place()
        _, along, _ = partners()
        for o in (1, 2, 3):
            send(self.own, self.all.at[core, dp, y], self.sems, 0, along(o))
        self.all[core, dp, y] = self.own[...]

    def second(self):
        dp, y, core = place()
        across, _, _ = partners()
        wait(self.all.at[core, dp, pl.ds(0, 3)], self.sems.at[1, 0])
        wait(self.all.at[core, dp, pl.ds(0, 3)], self.sems.at[0, 0])
        line = self.all.at[core, dp]

        @pl.loop(1, 16)
        def _(o):
            send(line, line, self.sems, 1, across(o))

    def third(self):
        _, _, core = place()
        _, _, sibling = partners()
        wait(self.all.at[core, pl.ds(0, 15)], self.sems.at[1, 1])
        wait(self.all.at[core, pl.ds(0, 15)], self.sems.at[0, 1])
        send(self.all.at[core], self.all.at[core], self.sems, 2, sibling)

    def last(self):
        _, _, core = place()
        wait(self.all.at[core], self.sems.at[1, 2])
        wait(self.all.at[core], self.sems.at[0, 2])


class Reduce:
    def __init__(self, parts, half, row, line, sems):
        self.parts, self.half, self.row, self.line, self.sems = parts, half, row, line, sems

    def first(self):
        _, _, core = place()
        _, _, sibling = partners()
        send(self.parts.at[1 - core], self.half, self.sems, 0, sibling)

    def second(self):
        dp, y, core = place()
        across, _, _ = partners()
        wait(self.half, self.sems.at[1, 0])
        wait(self.half, self.sems.at[0, 0])
        self.half[...] = (self.half[...].astype(f32) + self.parts[core].astype(f32)).astype(self.half.dtype)

        @pl.loop(1, 16)
        def _(o):
            send(self.half.at[lax.rem(dp + o, 16)], self.row.at[dp], self.sems, 1, across(o))

        self.row[dp] = self.half[dp]

    def third(self):
        dp, y, core = place()
        _, along, _ = partners()
        wait(self.row.at[pl.ds(0, 15)], self.sems.at[1, 1])
        wait(self.row.at[pl.ds(0, 15)], self.sems.at[0, 1])
        mine = jnp.sum(self.row[...].astype(f32), axis=0).astype(self.row.dtype)
        self.half[0] = mine
        for o in (1, 2, 3):
            send(self.half.at[0, lax.rem(y + o, 4)], self.line.at[y], self.sems, 2, along(o))
        self.line[y] = self.half[0, y]

    def last(self):
        wait(self.line.at[pl.ds(0, 3)], self.sems.at[1, 2])
        wait(self.line.at[pl.ds(0, 3)], self.sems.at[0, 2])
        return jnp.sum(self.line[...].astype(f32), axis=0)


def rope_tables():
    freqs = np.float32(10000.0) ** (-np.arange(HD // 2, dtype=np.float32) * np.float32(2.0) / np.float32(HD))
    angle = np.arange(LEN, dtype=np.float32)[None, :] * freqs.astype(np.float32)[:, None]
    return np.cos(angle.astype(np.float64)).astype(np.float32), np.sin(angle.astype(np.float64)).astype(np.float32)


def own_tiles(w_in, w_qkv, w_out, w_gu, w_down, gains, tile_a, tile_b, wide):
    tile_a[...] = jnp.zeros_like(tile_a)
    wide[...] = jnp.zeros_like(wide)
    for name, ref in (("in", w_in), ("qkv", w_qkv), ("out", w_out), ("gu", w_gu), ("down", w_down)):
        _, chunk, _, _, which, base = SPECS[name]
        for t, at, width in lane_tiles(chunk):
            (tile_a if which == "a" else wide)[base + t, :width] = ref[pl.ds(at, width)].astype(f32)
    tile_a[0:1, 108:117] = gains[0:1, :].astype(f32)
    tile_a[0:1, 117:126] = gains[1:2, :].astype(f32)
    tile_b[...] = wide[...].astype(bf16)


def gain_columns(flat, out):
    rows = flat[pl.ds(0, 16, stride=4 * A_ROWS), :]
    r = lax.broadcasted_iota(jnp.int32, (D, 16), 0) // 9
    spread = dot((r == lax.broadcasted_iota(jnp.int32, (D, 16), 1)).astype(f32), rows)
    lane = lax.broadcasted_iota(jnp.int32, (D, 128), 1)
    e = lax.rem(lax.broadcasted_iota(jnp.int32, (D, 128), 0), 9)
    for i in (0, 1):
        out[:, i : i + 1] = jnp.sum(jnp.where(lane == e + 108 + 9 * i, spread, 0.0), axis=1, keepdims=True)


def gain_rows(partial, flat):
    pos = lax.broadcasted_iota(jnp.int32, (128, D), 0)
    r = lax.broadcasted_iota(jnp.int32, (128, D), 1) // 9
    pick = (lax.rem(pos, 64) // 4 == r).astype(f32)
    lane = lax.broadcasted_iota(jnp.int32, (D, 128), 1)
    e = lax.rem(lax.broadcasted_iota(jnp.int32, (D, 128), 0), 9)
    cols = jnp.zeros((D, 128), f32)
    for i in (0, 1):
        cols += jnp.where(lane == e + 108 + 9 * i, jnp.sum(partial[i], axis=1, keepdims=True), 0.0)
    spread = dot(pick, cols, precision=lax.Precision.HIGHEST)
    flat[pl.ds(0, 128, stride=A_ROWS), :] += spread


def series_scalars(targets, lag_mask, date_mask, freq, sets, factor, stats):
    scale = jnp.sum(jnp.abs(targets[...]), axis=1, keepdims=True) / LEN + 1e-5
    lag = lag_mask[...].astype(f32) / scale
    second = lax.broadcasted_iota(jnp.int32, (2, NDATE), 0) == 1
    start = jnp.where(second, freq[1], freq[0]) * (NDATE // 3)
    keep = jnp.where(lax.broadcasted_iota(jnp.int32, (2, NDATE), 1) >= start, date_mask[...], 0).astype(f32)
    both = jnp.concatenate([lag, keep], axis=1)
    both = jnp.concatenate([both, jnp.zeros((2, 32), f32)], axis=1)
    both = jnp.concatenate([both, jnp.zeros((6, 128), f32)], axis=0)
    factor[...] = both.T
    lane = lax.broadcasted_iota(jnp.int32, (1, 128), 1)
    row = jnp.zeros((1, 128), f32)
    for s in (0, 1):
        row += jnp.where(lane == sets[s], scale[s : s + 1], 0.0) + jnp.where(lane == sets[s] + NSET, 1.0, 0.0)
    stats[...] = row

def fold(op, a):
    return op(a.reshape(a.shape[0] // 8, 8, a.shape[1]), axis=0)


def weave(gens):
    gens = list(gens)
    while gens:
        for g in list(gens):
            try:
                next(g)
            except StopIteration:
                gens.remove(g)


VM = pl.BlockSpec(memory_space=pltpu.VMEM)
SM = pl.BlockSpec(memory_space=pltpu.SMEM)
HB = pl.BlockSpec(memory_space=pl.ANY)
NAMES = ("in", "qkv", "out", "gu", "down")


def tiled(name):
    return (-(-SPECS[name][0] // 128), ROWS[name], 128)


def attend(s, hh, q, k, v, prob, sbuf, rl, osum, mixed):
    diag = lambda c0: (lax.broadcasted_iota(jnp.int32, (CH, QT), 0) + c0) <= lax.broadcasted_iota(jnp.int32, (CH, QT), 1)
    heads = [hh * GROUP + u for u in range(GROUP)]
    kts = [k[s, h].astype(f32).T.astype(bf16) for h in heads]
    ones = (lax.broadcasted_iota(jnp.int32, (HD, LEN), 0) == 0).astype(f32).astype(bf16)
    vs = [jnp.concatenate([v[s, h], ones], axis=0) for h in heads]
    tasks = [(u, j) for j in range(LEN // QT - 1, -1, -1) for u in range(GROUP)]
    tops = {}

    def score(i):
        u, j = tasks[i]
        n, best = (j + 1) * QT, None
        for c in range(0, n, CH):
            x = dot(kts[u][c : c + CH], q[s, heads[u], :, j * QT : j * QT + QT])
            if c + CH > n - QT:
                x = jnp.where(diag(c - (n - QT)), x, -1e30)
            sbuf[i % 2, c : c + CH] = x
            top = fold(jnp.max, x)
            best = top if best is None else jnp.maximum(best, top)
            yield
        tops[i] = jnp.max(best, axis=0, keepdims=True)

    def exponent(i):
        u, j = tasks[i]
        for c in range(0, (j + 1) * QT, CH):
            prob[j][s, heads[u], c : c + CH] = jnp.exp(sbuf[i % 2, c : c + CH] - tops[i]).astype(bf16)
            yield

    def mix(i):
        u, j = tasks[i]
        h, n, cols = heads[u], (j + 1) * QT, pl.ds(j * QT, QT)
        o = dot(vs[u][:, :n], prob[j][s, h])
        inv = 1.0 / o[HD : HD + 1]
        o = o[:HD] * inv
        rl[s, h, :, cols] = inv
        osum[s, h, :, cols] = o
        mixed[s, h, :, cols] = o.astype(bf16)

    last = len(tasks)
    for i in range(last + 3):
        if 0 <= i - 3:
            mix(i - 3)
        weave(([score(i)] if i < last else []) + ([exponent(i - 1)] if 0 <= i - 1 < last else []))


def attend_back(s, hh, q, k, v, prob, rl, osum, gmixed, cosr, sinr, gjoint, dsb, dq, dk, dv):
    heads = [hh * GROUP + u for u in range(GROUP)]
    dos, deltas, vts = [], [], []
    for h in heads:
        do = (gmixed[s, h] * rl[s, h]).astype(bf16)
        dos.append(do)
        deltas.append(jnp.sum(do.astype(f32) * osum[s, h], axis=0, keepdims=True))
        vts.append(v[s, h].astype(f32).T.astype(bf16))
    dk[...] = jnp.zeros_like(dk)
    dv[...] = jnp.zeros_like(dv)
    tasks = [(u, j) for j in range(LEN // QT - 1, -1, -1) for u in range(GROUP)]

    def spread(i):
        u, j = tasks[i]
        n = (j + 1) * QT
        cols = slice(j * QT, n)
        for c in range(0, n, QT):
            dp = dot(vts[u][c : c + QT], dos[u][:, cols]) - deltas[u][:, cols]
            dsb[i % 2, c : c + QT] = (prob[j][s, heads[u], c : c + QT].astype(f32) * dp).astype(bf16)
            yield

    def to_query(i):
        u, j = tasks[i]
        n = (j + 1) * QT
        dq[u, :, j * QT : n] = dot(k[s, heads[u]][:, :n], dsb[i % 2, :n])
        yield

    def to_keys(i):
        u, j = tasks[i]
        for c in range(0, (j + 1) * QT, QT):
            dk[u, :, c : c + QT] += dot(q[s, heads[u], :, j * QT : j * QT + QT], dsb[i % 2, c : c + QT], 1, 1)
            yield

    def to_values(i):
        u, j = tasks[i]
        for c in range(0, (j + 1) * QT, QT):
            dv[u, :, c : c + QT] += dot(dos[u][:, j * QT : j * QT + QT], prob[j][s, heads[u], c : c + QT], 1, 1)
            yield

    last = len(tasks)
    for i in range(last + 1):
        weave(([spread(i)] if i < last else []) + ([to_query(i - 1), to_keys(i - 1), to_values(i - 1)] if i else []))
    c, sn = cosr[...], sinr[...]
    for u, h in enumerate(heads):
        for which, val in ((0, dq[u] * 0.25), (1, dk[u])):
            a, b = val[:8], val[8:]
            gjoint[s, which, h] = jnp.concatenate([a * c + b * sn, b * c - a * sn], axis=0).astype(bf16)
        gjoint[s, 2, h] = dv[u].astype(bf16)


def layer_kernel(
    feats_h, targets_h, lag_h, date_h, freq_h, sets_h, w_in_h, w_qkv_h, w_out_h, w_gu_h, w_down_h, gains_h, dout_h, cos_h, sin_h,
    out_h, gfeats_h, tot_a, tot_b,
    feats, dout, targets, lag_mask, date_mask, freq, sets, w_in, w_qkv, w_out, w_gu, w_down, gains_own, cosr, sinr, out, gfeats,
    tile_a, tile_b, all_a, all_b, flat_a, flat_b, half_a, half_b, row_a, row_b, line_b,
    m_in, m_qkv, m_out, m_gu, m_down, win, wqkv, wout, wgu, wdown, winT, wqkvT, woutT, wguT, wdownT,
    gains, g_gain, factor, stats, lifted, first, inv1, normed, q, k, v, p0, p1, p2, p3, sbuf, rl, osum, mixed, middle, second, hidden, both,
    gmid, gbranch, gmixed, gjoint, gfirst, dsb, dq, dk, dv, sem_a, sem_b, sem_c, sem_d, sem_l, sem_x, sem_z,
):
    knock()
    prob = (p0, p1, p2, p3)
    loads = [
        pltpu.make_async_copy(src, dst, sem_l.at[i])
        for i, (src, dst) in enumerate(
            (
                (w_in_h, w_in), (w_qkv_h, w_qkv), (w_out_h, w_out), (w_gu_h, w_gu), (w_down_h, w_down), (gains_h, gains_own),
                (feats_h, feats), (targets_h, targets), (lag_h, lag_mask), (date_h, date_mask), (freq_h, freq), (sets_h, sets),
                (cos_h, cosr), (sin_h, sinr), (dout_h, dout),
            )
        )
    ]
    for load in loads:
        load.start()
    for load in loads[:6]:
        load.wait()
    own_tiles(w_in, w_qkv, w_out, w_gu, w_down, gains_own, tile_a, tile_b, flat_b.at[pl.ds(0, B_ROWS)])
    a, b = GatherDirect(tile_a, all_a, sem_a), Gather(tile_b, all_b, sem_b)

    def scalars():
        for load in loads[7:12]:
            load.wait()
        series_scalars(targets, lag_mask, date_mask, freq, sets, factor, stats)
        g_gain[...] = jnp.zeros_like(g_gain)

    def lift():
        for load in loads[6:7] + loads[12:14]:
            load.wait()
        for s in (0, 1):
            lifted[s] = (feats[s].astype(f32) * factor[:F, s : s + 1]).astype(bf16)

    enter(sem_x, sem_z, a.to, (scalars, lift))
    a.second()
    b.first()
    a.last()
    flat_a[...] = all_a[...].reshape(128 * A_ROWS, 128)
    gain_columns(flat_a, gains)

    def emit(name, flat, rows, mat, out, outT):
        unpack(flat, rows, name, mat)
        for t, at, width in lane_tiles(SPECS[name][0]):
            val = mat[t][:, :width]
            out[:, at : at + width] = val.astype(bf16)
            outT[at : at + width, :] = val.T.astype(bf16)
        mat[...] = jnp.zeros_like(mat)

    emit("in", flat_a, A_ROWS, m_in, win, winT)
    emit("qkv", flat_a, A_ROWS, m_qkv, wqkv, wqkvT)

    def add_to(ref, val):
        for t, at, width in lane_tiles(val.shape[1]):
            ref[t, :, :width] += val[:, at : at + width]

    gain0 = gains[:, 0:1]
    gain1 = gains[:, 1:2]

    @pl.loop(0, 2)
    def _(s):
        @pl.loop(0, LEN // TOK_IN)
        def _(i):
            t = pl.ds(pl.multiple_of(i * TOK_IN, TOK_IN), TOK_IN)
            x = dot(winT[...], lifted[s, :, t])
            first[s, :, t] = x
            r = lax.rsqrt(jnp.mean(x * x, axis=0, keepdims=True) + EPS)
            inv1[s, :, t] = r
            n = (x * r * gain0).astype(bf16)
            normed[s, :, t] = n
            joint = dot(wqkvT[...], n).reshape(3, H, HD, TOK_IN)
            c, sn = cosr[:, t][None], sinr[:, t][None]
            for which, ref, scale in ((0, q, 0.25), (1, k, 1.0)):
                u, w = joint[which, :, :8], joint[which, :, 8:]
                ref[s, :, :, t] = (jnp.concatenate([u * c - w * sn, w * c + u * sn], axis=1) * scale).astype(bf16)
            v[s, :, :, t] = joint[2].astype(bf16)

    b.second()

    @pl.loop(0, H // GROUP)
    def _(hh):
        attend(0, hh, q, k, v, prob, sbuf, rl, osum, mixed)

    b.third()

    @pl.loop(0, H // GROUP)
    def _(hh):
        attend(1, hh, q, k, v, prob, sbuf, rl, osum, mixed)

    b.last()
    flat_b[...] = all_b[...].astype(f32).reshape(128 * B_ROWS, 128)
    emit("out", flat_b, B_ROWS, m_out, wout, woutT)
    emit("gu", flat_b, B_ROWS, m_gu, wgu, wguT)
    emit("down", flat_b, B_ROWS, m_down, wdown, wdownT)
    loads[14].wait()

    @pl.loop(0, 2)
    def _(s):
        @pl.loop(0, LEN // TOK_MLP)
        def _(i):
            t = pl.ds(pl.multiple_of(i * TOK_MLP, TOK_MLP), TOK_MLP)
            mid = first[s, :, t] + dot(woutT[...], mixed[s, :, :, t].reshape(D, TOK_MLP))
            r = lax.rsqrt(jnp.mean(mid * mid, axis=0, keepdims=True) + EPS)
            sec = (mid * r * gain1).astype(bf16)
            second[:, t] = sec
            g = dout[s, :, t]
            for f in range(0, FF, 128):
                gate = dot(wguT[f : f + 128], sec)
                up = dot(wguT[FF + f : FF + f + 128], sec)
                gh = dot(wdown[f : f + 128], g)
                sig = 1.0 / (1.0 + jnp.exp(-gate))
                silu = gate * sig
                hidden[s, f : f + 128, t] = (silu * up).astype(bf16)
                both[FF + f : FF + f + 128, t] = (gh * silu).astype(bf16)
                both[f : f + 128, t] = (gh * up * (sig + silu * (1.0 - sig))).astype(bf16)
            middle[s, :, t] = mid
            c = dot(wgu[...], both[:, t])
            cg = c * gain1
            inner = jnp.mean(cg * mid, axis=0, keepdims=True)
            gain_part = c * mid * r
            g_gain[1] += functools.reduce(jnp.add, [gain_part[:, x : x + 128] for x in range(0, TOK_MLP, 128)])
            gm = g.astype(f32) + r * cg - mid * (r * r * r * inner)
            gmid[s, :, t] = gm
            gb = gm.astype(bf16)
            gbranch[:, t] = gb
            gmixed[s, :, :, t] = dot(wout[...], gb).reshape(H, HD, TOK_MLP)

        add_to(m_down, dot(hidden[s], dout[s], 1, 1))
        add_to(m_gu, dot(second[...], both[...], 1, 1))
        add_to(m_out, dot(mixed[s].reshape(D, LEN), gbranch[...], 1, 1))

    flat_b[...] = jnp.zeros_like(flat_b)
    pack(m_out, "out", flat_b, B_ROWS)
    pack(m_gu, "gu", flat_b, B_ROWS)
    pack(m_down, "down", flat_b, B_ROWS)
    all_b[...] = flat_b[...].reshape(all_b.shape).astype(bf16)
    a, b = ReduceDirect(all_a, half_a, row_a, sem_c), Reduce(all_b, half_b, row_b, line_b, sem_d)
    b.first()

    @pl.loop(0, H // GROUP)
    def _(hh):
        attend_back(0, hh, q, k, v, prob, rl, osum, gmixed, cosr, sinr, gjoint, dsb, dq, dk, dv)

    b.second()

    @pl.loop(0, H // GROUP)
    def _(hh):
        attend_back(1, hh, q, k, v, prob, rl, osum, gmixed, cosr, sinr, gjoint, dsb, dq, dk, dv)

    b.third()

    @pl.loop(0, 2)
    def _(s):
        add_to(m_qkv, dot(normed[s], gjoint[s].reshape(3 * D, LEN), 1, 1))
        @pl.loop(0, LEN // TOK_BACK)
        def _(i):
            t = pl.ds(pl.multiple_of(i * TOK_BACK, TOK_BACK), TOK_BACK)
            c = dot(wqkv[...], gjoint[s, :, :, :, t].reshape(3 * D, TOK_BACK))
            x, r = first[s, :, t], inv1[s, :, t]
            cg = c * gain0
            inner = jnp.mean(cg * x, axis=0, keepdims=True)
            gain_part = c * x * r
            g_gain[0] += functools.reduce(jnp.add, [gain_part[:, x : x + 128] for x in range(0, TOK_BACK, 128)])
            gf = (gmid[s, :, t] + r * cg - x * (r * r * r * inner)).astype(bf16)
            gfirst[s, :, t] = gf

        add_to(m_in, dot(lifted[s], gfirst[s], 1, 1))

    flat_a[...] = jnp.zeros_like(flat_a)
    pack(m_in, "in", flat_a, A_ROWS)
    pack(m_qkv, "qkv", flat_a, A_ROWS)
    gain_rows(g_gain, flat_a)
    flat_a[pl.ds(5, 128, stride=A_ROWS), :] = jnp.broadcast_to(stats[...], (128, 128))
    all_a[...] = flat_a[...].reshape(all_a.shape)
    a.first()
    tot_b[...] = b.last()
    a.second()

    for s in (0, 1):
        out[s] = (middle[s] + dot(wdownT[...], hidden[s])).astype(bf16)
        gfeats[s] = (dot(win[...], gfirst[s]) * factor[:F, s : s + 1]).astype(bf16)
    store_out = pltpu.make_async_copy(out, out_h, sem_l.at[15])
    store_out.start()
    store_gfeats = pltpu.make_async_copy(gfeats, gfeats_h, sem_l.at[16])
    store_gfeats.start()
    tot_a[...] = a.last()
    store_out.wait()
    store_gfeats.wait()


def run_layer(feats_t, targets, lag_mask, date_mask, freq_ids, dataset_ids, weights, gains, dout_t):
    cos, sin = rope_tables()
    sd, V = jax.ShapeDtypeStruct, pltpu.VMEM
    shapes = [(ROWS[n], SPECS[n][0]) for n in NAMES]
    return pl.pallas_call(
        layer_kernel,
        in_specs=[HB] * 15,
        out_specs=[HB, HB, VM, VM],
        out_shape=[sd((2, D, LEN), bf16), sd((2, F, LEN), bf16), sd((A_ROWS, 128), f32), sd((B_ROWS, 128), f32)],
        scratch_shapes=[
            V((2, F, LEN), bf16), V((2, D, LEN), bf16), V((2, LEN), f32), V((2, NLAG), jnp.int32), V((2, NDATE), jnp.int32),
            *[pltpu.SMEM((2,), jnp.int32)] * 2,
            *[V((SPECS[n][1],), bf16) for n in NAMES], V((2, 9), bf16), V((8, LEN), f32), V((8, LEN), f32),
            V((2, D, LEN), bf16), V((2, F, LEN), bf16),
            V((A_ROWS, 128), f32), V((B_ROWS, 128), bf16),
            V((2, 64, A_ROWS, 128), f32), V((2, 16, 4, B_ROWS, 128), bf16),
            V((128 * A_ROWS, 128), f32), V((128 * B_ROWS, 128), f32),
            V((64, A_ROWS, 128), f32), V((16, 4, B_ROWS, 128), bf16),
            V((64, A_ROWS, 128), f32), V((16, 4, B_ROWS, 128), bf16),
            V((4, B_ROWS, 128), bf16),
            *[V(tiled(n), f32) for n in NAMES], *[V(s, bf16) for s in shapes], *[V(s[::-1], bf16) for s in shapes],
            V((D, 2), f32), V((2, D, 128), f32), V((128, 8), f32), V((1, 128), f32),
            V((2, F, LEN), bf16), V((2, D, LEN), f32), V((2, 1, LEN), f32), V((2, D, LEN), bf16),
            V((2, H, HD, LEN), bf16), V((2, H, HD, LEN), bf16), V((2, H, HD, LEN), bf16),
            *[V((2, H, (j + 1) * QT, QT), bf16) for j in range(4)],
            V((2, LEN, QT), f32), V((2, H, 1, LEN), f32), V((2, H, HD, LEN), f32), V((2, H, HD, LEN), bf16),
            V((2, D, LEN), f32), V((D, LEN), bf16), V((2, FF, LEN), bf16), V((2 * FF, LEN), bf16),
            V((2, D, LEN), f32), V((D, LEN), bf16), V((2, H, HD, LEN), f32), V((2, 3, H, HD, LEN), bf16), V((2, D, LEN), bf16),
            V((2, LEN, QT), bf16), *[V((GROUP, HD, LEN), f32)] * 3,
            *[pltpu.SemaphoreType.DMA((2, 3))] * 4, pltpu.SemaphoreType.DMA((17,)), *[pltpu.SemaphoreType.REGULAR] * 2,
        ],
        compiler_params=pltpu.CompilerParams(collective_id=0, has_side_effects=True, vmem_limit_bytes=63 * 2**20),
    )(feats_t, targets, lag_mask, date_mask, freq_ids, dataset_ids, *weights, gains, dout_t, jnp.asarray(cos), jnp.asarray(sin))


def finish_kernel(out_h, gfeats_h, tot_a_h, tot_b_h, running_h, out, gfeats, o_in, o_qkv, o_out, o_gu, o_down, o_gain, o_running,
                  out_v, gfeats_v, tot_a, tot_b, running, sems):
    pairs = ((tot_a_h, tot_a), (tot_b_h, tot_b), (running_h, running), (out_h, out_v), (gfeats_h, gfeats_v))
    copies = [pltpu.make_async_copy(src, dst, sems.at[i]) for i, (src, dst) in enumerate(pairs)]
    stores = [pltpu.make_async_copy(src, dst, sems.at[5 + i]) for i, (src, dst) in enumerate(((out_v, out), (gfeats_v, gfeats)))]
    for copy in copies:
        copy.start()
    for copy in copies:
        copy.wait()
    for store in stores:
        store.start()
    for name, ref in (("in", o_in), ("qkv", o_qkv), ("out", o_out), ("gu", o_gu), ("down", o_down)):
        _, chunk, _, _, which, base = SPECS[name]
        for t, at, width in lane_tiles(chunk):
            ref[pl.ds(at, width)] = (tot_a if which == "a" else tot_b)[base + t, :width]
    o_gain[0:1, :] = tot_a[0:1, 108:117]
    o_gain[1:2, :] = tot_a[0:1, 117:126]
    sums, counts = tot_a[5, :NSET], tot_a[5, NSET : 2 * NSET]
    old = running[...]
    o_running[...] = jnp.where(counts > 0.5, 0.75 * old + 0.25 * (sums / jnp.maximum(counts, 1.0)), old)
    for store in stores:
        store.wait()


def hand_out(out, gfeats, tot_a, tot_b, running):
    sd, V = jax.ShapeDtypeStruct, pltpu.VMEM
    return pl.pallas_call(
        finish_kernel,
        in_specs=[HB] * 5,
        out_specs=[HB, HB] + [VM] * 7,
        out_shape=[sd((2, D, LEN), bf16), sd((2, F, LEN), bf16)]
        + [sd((SPECS[n][1],), f32) for n in NAMES] + [sd((2, 9), f32), sd((NSET,), f32)],
        scratch_shapes=[V((2, D, LEN), bf16), V((2, F, LEN), bf16), V((A_ROWS, 128), f32), V((B_ROWS, 128), f32), V((NSET,), f32),
                        pltpu.SemaphoreType.DMA((7,))],
        compiler_params=pltpu.CompilerParams(vmem_limit_bytes=60 * 2**20),
    )(out, gfeats, tot_a, tot_b, running)


def body(feats, targets, lag_mask, date_mask, freq_ids, dataset_ids, w_in, w_qkv, w_out, w_gu, w_down, gains, running, d_out):
    done = run_layer(
        jnp.swapaxes(feats, 1, 2), targets, lag_mask, date_mask, freq_ids, dataset_ids,
        (w_in, w_qkv, w_out, w_gu, w_down), gains, jnp.swapaxes(d_out, 1, 2),
    )
    out, gfeats, *rest = hand_out(*done, running)
    return (jnp.swapaxes(out, 1, 2), jnp.swapaxes(gfeats, 1, 2), *rest)


def solution(mesh):
    flat, rows, cube = P(BOTH), P(BOTH, None), P(BOTH, None, None)
    return jax.shard_map(
        body,
        mesh=mesh,
        in_specs=(cube, rows, rows, rows, flat, flat, flat, flat, flat, flat, flat, P(None, "dp"), P(), cube),
        out_specs=(cube, cube, flat, flat, flat, flat, flat, P(None, "dp"), P()),
        check_vma=False,
    )
```

```python
import functools

import jax
import jax.numpy as jnp
import numpy as np
from jax import lax
from jax.experimental import pallas as pl
from jax.experimental.pallas import tpu as pltpu
from jax.sharding import PartitionSpec as P

D, H, HD, FF, NDATE, NLAG, F, NSET, LEN = 144, 9, 16, 512, 12, 84, 96, 8, 1024
EPS = 1e-05
TOK_IN = 1024
TOK_MLP = 1024
TOK_BACK = 1024
QT = 256
CH = 128
GROUP = 3
f32, bf16 = jnp.float32, jnp.bfloat16
MESH = pl.DeviceIdType.MESH
BOTH = ("dp", "fsdp")

A_ROWS, B_ROWS = 8, 16
SPECS = {
    "in": (D, 108, 4, 3, "a", 0),
    "qkv": (3 * D, 486, 8, 9, "a", 1),
    "gu": (2 * FF, 1152, 8, 9, "b", 0),
    "down": (D, 576, 2, 8, "b", 9),
    "out": (D, 162, 8, 9, "b", 14),
}
ROWS = {"in": F, "qkv": D, "gu": D, "down": FF, "out": D}


def dot(a, b, ca=1, cb=0, **kw):
    return lax.dot_general(a, b, (((ca,), (cb,)), ((), ())), preferred_element_type=f32, **kw)


def lane_tiles(width):
    return [(t // 128, t, min(128, width - t)) for t in range(0, width, 128)]


def pieces(piece, source, count):
    cuts = []
    for i in range(count):
        at, left, parts = i * piece, piece, []
        while left:
            c, o = divmod(at, source)
            n = min(left, source - o)
            parts.append((c, o, n))
            at, left = at + n, left - n
        cuts.append(parts)
    return cuts


def spot(c):
    return (c % 2) * 64 + c // 2


def join(parts):
    return parts[0] if len(parts) == 1 else jnp.concatenate(parts, axis=1)


def unpack(flat, rows, name, dst):
    cols, chunk, gc, gr, _, base = SPECS[name]
    groups, kept = 128 // gc, {}

    def owner(c):
        if c not in kept:
            kept[c] = join(
                [flat[pl.ds(spot(c) * rows + base + t, groups, stride=gc // 2 * rows), :] for t, _, _ in lane_tiles(chunk)]
            )
        return kept[c]

    for i, parts in enumerate(pieces(cols, chunk, gr)):
        row = join([owner(c)[:, o : o + n] for c, o, n in parts])
        for t, at, width in lane_tiles(cols):
            dst[t, pl.ds(i, groups, stride=gr), :width] = row[:, at : at + width]


def pack(src, name, flat, rows):
    cols, chunk, gc, gr, _, base = SPECS[name]
    groups, kept = 128 // gc, {}

    def line(i):
        if i not in kept:
            kept[i] = join([src[t, pl.ds(i, groups, stride=gr), :] for t, _, _ in lane_tiles(cols)])
        return kept[i]

    for c, parts in enumerate(pieces(chunk, cols, gc)):
        run = [line(i)[:, o : o + n] for i, o, n in parts]
        run = join(run + ([jnp.zeros((groups, -chunk % 128), f32)] if chunk % 128 else []))
        for t, at, _ in lane_tiles(chunk):
            flat[pl.ds(spot(c) * rows + base + t, groups, stride=gc // 2 * rows), :] = run[:, at : at + 128]


def place():
    fs = lax.axis_index("fsdp")
    return lax.axis_index("dp"), fs // 2, fs % 2


def partners():
    dp, y, core = place()
    across = lambda o: (lax.rem(dp + o, 16), 2 * y + core)
    along = lambda o: (dp, 2 * lax.rem(y + o, 4) + core)
    return across, along, (dp, 2 * y + 1 - core)


def chip(dz, dx, dy):
    dp, y, _ = place()
    z, x = dp // 4, lax.rem(dp, 4)
    return 4 * lax.rem(z + dz, 4) + lax.rem(x + dx, 4), lax.rem(y + dy, 4)


def device(dz, dx, dy):
    dp, y = chip(dz, dx, dy)
    return dp, 2 * y + place()[2]


STEPS = (1, 2, 3)
LINES = [(0, 0, o) for o in STEPS] + [(0, o, 0) for o in STEPS] + [(o, 0, 0) for o in STEPS]
X_PLANES = [(0, o, p) for o in STEPS for p in STEPS] + [(p, o, 0) for o in STEPS for p in STEPS]
REST = [(o, p, r) for o in STEPS for p in STEPS for r in STEPS] + [(o, 0, p) for o in STEPS for p in STEPS]


def signal(sem, to):
    pl.semaphore_signal(sem, inc=1, device_id=to, device_id_type=MESH)


def knock():
    barrier = pltpu.get_barrier_semaphore()
    for line in LINES:
        signal(barrier, device(*line))
    signal(barrier, partners()[2])


def enter(sem_x, sem_z, send_to, work):
    pl.semaphore_wait(pltpu.get_barrier_semaphore(), 10)
    for o in STEPS:
        signal(sem_x, device(0, o, 0))
    for line in LINES:
        send_to(*line)
    work[0]()
    pl.semaphore_wait(sem_x, 3)
    for o in STEPS:
        signal(sem_z, device(o, 0, 0))
    for line in X_PLANES:
        send_to(*line)
    work[1]()
    pl.semaphore_wait(sem_z, 3)
    for line in REST:
        send_to(*line)


def send(src, dst, sems, k, to):
    pltpu.make_async_remote_copy(
        src_ref=src, dst_ref=dst, send_sem=sems.at[0, k], recv_sem=sems.at[1, k], device_id=to, device_id_type=MESH
    ).start()


def wait(ref, sem):
    pltpu.make_async_copy(ref, ref, sem).wait()


class GatherDirect:
    def __init__(self, own, everyone, sems):
        self.own, self.all, self.sems = own, everyone, sems

    def to(self, *line):
        dp, y, core = place()
        send(self.own, self.all.at[core, 4 * dp + y], self.sems, 0, device(*line))

    def second(self):
        dp, y, core = place()
        self.all[core, 4 * dp + y] = self.own[...]
        wait(self.all.at[core, pl.ds(0, 63)], self.sems.at[1, 0])
        wait(self.all.at[core, pl.ds(0, 63)], self.sems.at[0, 0])
        send(self.all.at[core], self.all.at[core], self.sems, 1, partners()[2])

    def last(self):
        _, _, core = place()
        wait(self.all.at[core], self.sems.at[1, 1])
        wait(self.all.at[core], self.sems.at[0, 1])


class ReduceDirect:
    def __init__(self, parts, half, got, sems):
        self.parts, self.half, self.got, self.sems = parts, half, got, sems

    def first(self):
        _, _, core = place()
        send(self.parts.at[1 - core], self.half, self.sems, 0, partners()[2])

    def second(self):
        dp, y, core = place()
        wait(self.half, self.sems.at[1, 0])
        wait(self.half, self.sems.at[0, 0])
        self.half[...] += self.parts[core]
        for line in REST + X_PLANES + LINES:
            to_dp, to_y = chip(*line)
            send(self.half.at[4 * to_dp + to_y], self.got.at[4 * dp + y], self.sems, 1, device(*line))
        self.got[4 * dp + y] = self.half[4 * dp + y]

    def last(self):
        wait(self.got.at[pl.ds(0, 63)], self.sems.at[1, 1])
        wait(self.got.at[pl.ds(0, 63)], self.sems.at[0, 1])
        return jnp.sum(self.got[...], axis=0)


class Gather:
    def __init__(self, own, everyone, sems):
        self.own, self.all, self.sems = own, everyone, sems

    def first(self):
        dp, y, core = place()
        _, along, _ = partners()
        for o in (1, 2, 3):
            send(self.own, self.all.at[core, dp, y], self.sems, 0, along(o))
        self.all[core, dp, y] = self.own[...]

    def second(self):
        dp, y, core = place()
        across, _, _ = partners()
        wait(self.all.at[core, dp, pl.ds(0, 3)], self.sems.at[1, 0])
        wait(self.all.at[core, dp, pl.ds(0, 3)], self.sems.at[0, 0])
        line = self.all.at[core, dp]

        @pl.loop(1, 16)
        def _(o):
            send(line, line, self.sems, 1, across(o))

    def third(self):
        _, _, core = place()
        _, _, sibling = partners()
        wait(self.all.at[core, pl.ds(0, 15)], self.sems.at[1, 1])
        wait(self.all.at[core, pl.ds(0, 15)], self.sems.at[0, 1])
        send(self.all.at[core], self.all.at[core], self.sems, 2, sibling)

    def last(self):
        _, _, core = place()
        wait(self.all.at[core], self.sems.at[1, 2])
        wait(self.all.at[core], self.sems.at[0, 2])


class Reduce:
    def __init__(self, parts, half, row, line, sems):
        self.parts, self.half, self.row, self.line, self.sems = parts, half, row, line, sems

    def first(self):
        _, _, core = place()
        _, _, sibling = partners()
        send(self.parts.at[1 - core], self.half, self.sems, 0, sibling)

    def second(self):
        dp, y, core = place()
        across, _, _ = partners()
        wait(self.half, self.sems.at[1, 0])
        wait(self.half, self.sems.at[0, 0])
        self.half[...] = (self.half[...].astype(f32) + self.parts[core].astype(f32)).astype(self.half.dtype)

        @pl.loop(1, 16)
        def _(o):
            send(self.half.at[lax.rem(dp + o, 16)], self.row.at[dp], self.sems, 1, across(o))

        self.row[dp] = self.half[dp]

    def third(self):
        dp, y, core = place()
        _, along, _ = partners()
        wait(self.row.at[pl.ds(0, 15)], self.sems.at[1, 1])
        wait(self.row.at[pl.ds(0, 15)], self.sems.at[0, 1])
        mine = jnp.sum(self.row[...].astype(f32), axis=0).astype(self.row.dtype)
        self.half[0] = mine
        for o in (1, 2, 3):
            send(self.half.at[0, lax.rem(y + o, 4)], self.line.at[y], self.sems, 2, along(o))
        self.line[y] = self.half[0, y]

    def last(self):
        wait(self.line.at[pl.ds(0, 3)], self.sems.at[1, 2])
        wait(self.line.at[pl.ds(0, 3)], self.sems.at[0, 2])
        return jnp.sum(self.line[...].astype(f32), axis=0)


def rope_tables():
    freqs = np.float32(10000.0) ** (-np.arange(HD // 2, dtype=np.float32) * np.float32(2.0) / np.float32(HD))
    angle = np.arange(LEN, dtype=np.float32)[None, :] * freqs.astype(np.float32)[:, None]
    return np.cos(angle.astype(np.float64)).astype(np.float32), np.sin(angle.astype(np.float64)).astype(np.float32)


def own_tiles(w_in, w_qkv, w_out, w_gu, w_down, gains, tile_a, tile_b, wide):
    tile_a[...] = jnp.zeros_like(tile_a)
    wide[...] = jnp.zeros_like(wide)
    for name, ref in (("in", w_in), ("qkv", w_qkv), ("out", w_out), ("gu", w_gu), ("down", w_down)):
        _, chunk, _, _, which, base = SPECS[name]
        for t, at, width in lane_tiles(chunk):
            (tile_a if which == "a" else wide)[base + t, :width] = ref[pl.ds(at, width)].astype(f32)
    tile_a[0:1, 108:117] = gains[0:1, :].astype(f32)
    tile_a[0:1, 117:126] = gains[1:2, :].astype(f32)
    tile_b[...] = wide[...].astype(bf16)


def gain_columns(flat, out):
    rows = flat[pl.ds(0, 16, stride=4 * A_ROWS), :]
    r = lax.broadcasted_iota(jnp.int32, (D, 16), 0) // 9
    spread = dot((r == lax.broadcasted_iota(jnp.int32, (D, 16), 1)).astype(f32), rows)
    lane = lax.broadcasted_iota(jnp.int32, (D, 128), 1)
    e = lax.rem(lax.broadcasted_iota(jnp.int32, (D, 128), 0), 9)
    for i in (0, 1):
        out[:, i : i + 1] = jnp.sum(jnp.where(lane == e + 108 + 9 * i, spread, 0.0), axis=1, keepdims=True)


def gain_rows(partial, flat):
    pos = lax.broadcasted_iota(jnp.int32, (128, D), 0)
    r = lax.broadcasted_iota(jnp.int32, (128, D), 1) // 9
    pick = (lax.rem(pos, 64) // 4 == r).astype(f32)
    lane = lax.broadcasted_iota(jnp.int32, (D, 128), 1)
    e = lax.rem(lax.broadcasted_iota(jnp.int32, (D, 128), 0), 9)
    cols = jnp.zeros((D, 128), f32)
    for i in (0, 1):
        cols += jnp.where(lane == e + 108 + 9 * i, jnp.sum(partial[i], axis=1, keepdims=True), 0.0)
    spread = dot(pick, cols, precision=lax.Precision.HIGHEST)
    flat[pl.ds(0, 128, stride=A_ROWS), :] += spread


def series_scalars(targets, lag_mask, date_mask, freq, sets, factor, stats):
    scale = jnp.sum(jnp.abs(targets[...]), axis=1, keepdims=True) / LEN + 1e-5
    lag = lag_mask[...].astype(f32) / scale
    second = lax.broadcasted_iota(jnp.int32, (2, NDATE), 0) == 1
    start = jnp.where(second, freq[1], freq[0]) * (NDATE // 3)
    keep = jnp.where(lax.broadcasted_iota(jnp.int32, (2, NDATE), 1) >= start, date_mask[...], 0).astype(f32)
    both = jnp.concatenate([lag, keep], axis=1)
    both = jnp.concatenate([both, jnp.zeros((2, 32), f32)], axis=1)
    both = jnp.concatenate([both, jnp.zeros((6, 128), f32)], axis=0)
    factor[...] = both.T
    lane = lax.broadcasted_iota(jnp.int32, (1, 128), 1)
    row = jnp.zeros((1, 128), f32)
    for s in (0, 1):
        row += jnp.where(lane == sets[s], scale[s : s + 1], 0.0) + jnp.where(lane == sets[s] + NSET, 1.0, 0.0)
    stats[...] = row

def fold(op, a):
    return op(a.reshape(a.shape[0] // 8, 8, a.shape[1]), axis=0)


def weave(gens):
    gens = list(gens)
    while gens:
        for g in list(gens):
            try:
                next(g)
            except StopIteration:
                gens.remove(g)


VM = pl.BlockSpec(memory_space=pltpu.VMEM)
SM = pl.BlockSpec(memory_space=pltpu.SMEM)
HB = pl.BlockSpec(memory_space=pl.ANY)
NAMES = ("in", "qkv", "out", "gu", "down")


def tiled(name):
    return (-(-SPECS[name][0] // 128), ROWS[name], 128)


def attend(s, hh, q, k, v, prob, sbuf, rl, osum, mixed):
    diag = lambda c0: (lax.broadcasted_iota(jnp.int32, (CH, QT), 0) + c0) <= lax.broadcasted_iota(jnp.int32, (CH, QT), 1)
    heads = [hh * GROUP + u for u in range(GROUP)]
    kts = [k[s, h].astype(f32).T.astype(bf16) for h in heads]
    ones = (lax.broadcasted_iota(jnp.int32, (HD, LEN), 0) == 0).astype(f32).astype(bf16)
    vs = [jnp.concatenate([v[s, h], ones], axis=0) for h in heads]
    tasks = [(u, j) for j in range(LEN // QT - 1, -1, -1) for u in range(GROUP)]
    tops = {}

    def score(i):
        u, j = tasks[i]
        n, best = (j + 1) * QT, None
        for c in range(0, n, CH):
            x = dot(kts[u][c : c + CH], q[s, heads[u], :, j * QT : j * QT + QT])
            if c + CH > n - QT:
                x = jnp.where(diag(c - (n - QT)), x, -1e30)
            sbuf[i % 2, c : c + CH] = x
            top = fold(jnp.max, x)
            best = top if best is None else jnp.maximum(best, top)
            yield
        tops[i] = jnp.max(best, axis=0, keepdims=True)

    def exponent(i):
        u, j = tasks[i]
        for c in range(0, (j + 1) * QT, CH):
            prob[j][s, heads[u], c : c + CH] = jnp.exp(sbuf[i % 2, c : c + CH] - tops[i]).astype(bf16)
            yield

    def mix(i):
        u, j = tasks[i]
        h, n, cols = heads[u], (j + 1) * QT, pl.ds(j * QT, QT)
        o = dot(vs[u][:, :n], prob[j][s, h])
        inv = 1.0 / o[HD : HD + 1]
        o = o[:HD] * inv
        rl[s, h, :, cols] = inv
        osum[s, h, :, cols] = o
        mixed[s, h, :, cols] = o.astype(bf16)

    last = len(tasks)
    for i in range(last + 3):
        if 0 <= i - 3:
            mix(i - 3)
        weave(([score(i)] if i < last else []) + ([exponent(i - 1)] if 0 <= i - 1 < last else []))


def attend_back(s, hh, q, k, v, prob, rl, osum, gmixed, cosr, sinr, gjoint, dsb, dq, dk, dv):
    heads = [hh * GROUP + u for u in range(GROUP)]
    dos, deltas, vts = [], [], []
    for h in heads:
        do = (gmixed[s, h] * rl[s, h]).astype(bf16)
        dos.append(do)
        deltas.append(jnp.sum(do.astype(f32) * osum[s, h], axis=0, keepdims=True))
        vts.append(v[s, h].astype(f32).T.astype(bf16))
    dk[...] = jnp.zeros_like(dk)
    dv[...] = jnp.zeros_like(dv)
    tasks = [(u, j) for j in range(LEN // QT - 1, -1, -1) for u in range(GROUP)]

    def spread(i):
        u, j = tasks[i]
        n = (j + 1) * QT
        cols = slice(j * QT, n)
        for c in range(0, n, QT):
            dp = dot(vts[u][c : c + QT], dos[u][:, cols]) - deltas[u][:, cols]
            dsb[i % 2, c : c + QT] = (prob[j][s, heads[u], c : c + QT].astype(f32) * dp).astype(bf16)
            yield

    def to_query(i):
        u, j = tasks[i]
        n = (j + 1) * QT
        dq[u, :, j * QT : n] = dot(k[s, heads[u]][:, :n], dsb[i % 2, :n])
        yield

    def to_keys(i):
        u, j = tasks[i]
        for c in range(0, (j + 1) * QT, QT):
            dk[u, :, c : c + QT] += dot(q[s, heads[u], :, j * QT : j * QT + QT], dsb[i % 2, c : c + QT], 1, 1)
            yield

    def to_values(i):
        u, j = tasks[i]
        for c in range(0, (j + 1) * QT, QT):
            dv[u, :, c : c + QT] += dot(dos[u][:, j * QT : j * QT + QT], prob[j][s, heads[u], c : c + QT], 1, 1)
            yield

    last = len(tasks)
    for i in range(last + 1):
        weave(([spread(i)] if i < last else []) + ([to_query(i - 1), to_keys(i - 1), to_values(i - 1)] if i else []))
    c, sn = cosr[...], sinr[...]
    for u, h in enumerate(heads):
        for which, val in ((0, dq[u] * 0.25), (1, dk[u])):
            a, b = val[:8], val[8:]
            gjoint[s, which, h] = jnp.concatenate([a * c + b * sn, b * c - a * sn], axis=0).astype(bf16)
        gjoint[s, 2, h] = dv[u].astype(bf16)


def layer_kernel(
    feats_h, targets_h, lag_h, date_h, freq_h, sets_h, w_in_h, w_qkv_h, w_out_h, w_gu_h, w_down_h, gains_h, dout_h, cos_h, sin_h,
    out_h, gfeats_h, tot_a, tot_b,
    feats, dout, targets, lag_mask, date_mask, freq, sets, w_in, w_qkv, w_out, w_gu, w_down, gains_own, cosr, sinr, out, gfeats,
    tile_a, tile_b, all_a, all_b, flat_a, flat_b, half_a, half_b, row_a, row_b, line_b,
    m_in, m_qkv, m_out, m_gu, m_down, win, wqkv, wout, wgu, wdown, winT, wqkvT, woutT, wguT, wdownT,
    gains, g_gain, factor, stats, lifted, first, inv1, normed, q, k, v, p0, p1, p2, p3, sbuf, rl, osum, mixed, middle, second, hidden, both,
    gmid, gbranch, gmixed, gjoint, gfirst, dsb, dq, dk, dv, sem_a, sem_b, sem_c, sem_d, sem_l, sem_x, sem_z,
):
    knock()
    prob = (p0, p1, p2, p3)
    loads = [
        pltpu.make_async_copy(src, dst, sem_l.at[i])
        for i, (src, dst) in enumerate(
            (
                (w_in_h, w_in), (w_qkv_h, w_qkv), (w_out_h, w_out), (w_gu_h, w_gu), (w_down_h, w_down), (gains_h, gains_own),
                (feats_h, feats), (targets_h, targets), (lag_h, lag_mask), (date_h, date_mask), (freq_h, freq), (sets_h, sets),
                (cos_h, cosr), (sin_h, sinr), (dout_h, dout),
            )
        )
    ]
    for load in loads:
        load.start()
    for load in loads[:6]:
        load.wait()
    own_tiles(w_in, w_qkv, w_out, w_gu, w_down, gains_own, tile_a, tile_b, flat_b.at[pl.ds(0, B_ROWS)])
    a, b = GatherDirect(tile_a, all_a, sem_a), Gather(tile_b, all_b, sem_b)

    def scalars():
        for load in loads[7:12]:
            load.wait()
        series_scalars(targets, lag_mask, date_mask, freq, sets, factor, stats)
        g_gain[...] = jnp.zeros_like(g_gain)

    def lift():
        for load in loads[6:7] + loads[12:14]:
            load.wait()
        for s in (0, 1):
            lifted[s] = (feats[s].astype(f32) * factor[:F, s : s + 1]).astype(bf16)

    enter(sem_x, sem_z, a.to, (scalars, lift))
    a.second()
    b.first()
    a.last()
    flat_a[...] = all_a[...].reshape(128 * A_ROWS, 128)
    gain_columns(flat_a, gains)

    def emit(name, flat, rows, mat, out, outT):
        unpack(flat, rows, name, mat)
        for t, at, width in lane_tiles(SPECS[name][0]):
            val = mat[t][:, :width]
            out[:, at : at + width] = val.astype(bf16)
            outT[at : at + width, :] = val.T.astype(bf16)
        mat[...] = jnp.zeros_like(mat)

    emit("in", flat_a, A_ROWS, m_in, win, winT)
    emit("qkv", flat_a, A_ROWS, m_qkv, wqkv, wqkvT)

    def add_to(ref, val):
        for t, at, width in lane_tiles(val.shape[1]):
            ref[t, :, :width] += val[:, at : at + width]

    gain0 = gains[:, 0:1]
    gain1 = gains[:, 1:2]

    @pl.loop(0, 2)
    def _(s):
        @pl.loop(0, LEN // TOK_IN)
        def _(i):
            t = pl.ds(pl.multiple_of(i * TOK_IN, TOK_IN), TOK_IN)
            x = dot(winT[...], lifted[s, :, t])
            first[s, :, t] = x
            r = lax.rsqrt(jnp.mean(x * x, axis=0, keepdims=True) + EPS)
            inv1[s, :, t] = r
            n = (x * r * gain0).astype(bf16)
            normed[s, :, t] = n
            joint = dot(wqkvT[...], n).reshape(3, H, HD, TOK_IN)
            c, sn = cosr[:, t][None], sinr[:, t][None]
            for which, ref, scale in ((0, q, 0.25), (1, k, 1.0)):
                u, w = joint[which, :, :8], joint[which, :, 8:]
                ref[s, :, :, t] = (jnp.concatenate([u * c - w * sn, w * c + u * sn], axis=1) * scale).astype(bf16)
            v[s, :, :, t] = joint[2].astype(bf16)

    b.second()

    @pl.loop(0, 2)
    def _(s):
        @pl.loop(0, H // GROUP)
        def _(hh):
            attend(s, hh, q, k, v, prob, sbuf, rl, osum, mixed)

        @pl.when(s == 0)
        def _():
            b.third()

    b.last()
    flat_b[...] = all_b[...].astype(f32).reshape(128 * B_ROWS, 128)
    emit("out", flat_b, B_ROWS, m_out, wout, woutT)
    emit("gu", flat_b, B_ROWS, m_gu, wgu, wguT)
    emit("down", flat_b, B_ROWS, m_down, wdown, wdownT)
    loads[14].wait()

    @pl.loop(0, 2)
    def _(s):
        @pl.loop(0, LEN // TOK_MLP)
        def _(i):
            t = pl.ds(pl.multiple_of(i * TOK_MLP, TOK_MLP), TOK_MLP)
            mid = first[s, :, t] + dot(woutT[...], mixed[s, :, :, t].reshape(D, TOK_MLP))
            r = lax.rsqrt(jnp.mean(mid * mid, axis=0, keepdims=True) + EPS)
            sec = (mid * r * gain1).astype(bf16)
            second[:, t] = sec
            g = dout[s, :, t]
            for f in range(0, FF, 128):
                gate = dot(wguT[f : f + 128], sec)
                up = dot(wguT[FF + f : FF + f + 128], sec)
                gh = dot(wdown[f : f + 128], g)
                sig = 1.0 / (1.0 + jnp.exp(-gate))
                silu = gate * sig
                hidden[s, f : f + 128, t] = (silu * up).astype(bf16)
                both[FF + f : FF + f + 128, t] = (gh * silu).astype(bf16)
                both[f : f + 128, t] = (gh * up * (sig + silu * (1.0 - sig))).astype(bf16)
            middle[s, :, t] = mid
            c = dot(wgu[...], both[:, t])
            cg = c * gain1
            inner = jnp.mean(cg * mid, axis=0, keepdims=True)
            gain_part = c * mid * r
            g_gain[1] += functools.reduce(jnp.add, [gain_part[:, x : x + 128] for x in range(0, TOK_MLP, 128)])
            gm = g.astype(f32) + r * cg - mid * (r * r * r * inner)
            gmid[s, :, t] = gm
            gb = gm.astype(bf16)
            gbranch[:, t] = gb
            gmixed[s, :, :, t] = dot(wout[...], gb).reshape(H, HD, TOK_MLP)

        add_to(m_down, dot(hidden[s], dout[s], 1, 1))
        add_to(m_gu, dot(second[...], both[...], 1, 1))
        add_to(m_out, dot(mixed[s].reshape(D, LEN), gbranch[...], 1, 1))

    flat_b[...] = jnp.zeros_like(flat_b)
    pack(m_out, "out", flat_b, B_ROWS)
    pack(m_gu, "gu", flat_b, B_ROWS)
    pack(m_down, "down", flat_b, B_ROWS)
    all_b[...] = flat_b[...].reshape(all_b.shape).astype(bf16)
    a, b = ReduceDirect(all_a, half_a, row_a, sem_c), Reduce(all_b, half_b, row_b, line_b, sem_d)
    b.first()

    @pl.loop(0, 2)
    def _(s):
        @pl.loop(0, H // GROUP)
        def _(hh):
            attend_back(s, hh, q, k, v, prob, rl, osum, gmixed, cosr, sinr, gjoint, dsb, dq, dk, dv)

        @pl.when(s == 0)
        def _():
            b.second()

    b.third()

    @pl.loop(0, 2)
    def _(s):
        add_to(m_qkv, dot(normed[s], gjoint[s].reshape(3 * D, LEN), 1, 1))
        @pl.loop(0, LEN // TOK_BACK)
        def _(i):
            t = pl.ds(pl.multiple_of(i * TOK_BACK, TOK_BACK), TOK_BACK)
            c = dot(wqkv[...], gjoint[s, :, :, :, t].reshape(3 * D, TOK_BACK))
            x, r = first[s, :, t], inv1[s, :, t]
            cg = c * gain0
            inner = jnp.mean(cg * x, axis=0, keepdims=True)
            gain_part = c * x * r
            g_gain[0] += functools.reduce(jnp.add, [gain_part[:, x : x + 128] for x in range(0, TOK_BACK, 128)])
            gf = (gmid[s, :, t] + r * cg - x * (r * r * r * inner)).astype(bf16)
            gfirst[s, :, t] = gf

        add_to(m_in, dot(lifted[s], gfirst[s], 1, 1))

    flat_a[...] = jnp.zeros_like(flat_a)
    pack(m_in, "in", flat_a, A_ROWS)
    pack(m_qkv, "qkv", flat_a, A_ROWS)
    gain_rows(g_gain, flat_a)
    flat_a[pl.ds(5, 128, stride=A_ROWS), :] = jnp.broadcast_to(stats[...], (128, 128))
    all_a[...] = flat_a[...].reshape(all_a.shape)
    a.first()
    tot_b[...] = b.last()
    a.second()

    for s in (0, 1):
        out[s] = (middle[s] + dot(wdownT[...], hidden[s])).astype(bf16)
        gfeats[s] = (dot(win[...], gfirst[s]) * factor[:F, s : s + 1]).astype(bf16)
    store_out = pltpu.make_async_copy(out, out_h, sem_l.at[15])
    store_out.start()
    store_gfeats = pltpu.make_async_copy(gfeats, gfeats_h, sem_l.at[16])
    store_gfeats.start()
    tot_a[...] = a.last()
    store_out.wait()
    store_gfeats.wait()


def run_layer(feats_t, targets, lag_mask, date_mask, freq_ids, dataset_ids, weights, gains, dout_t):
    cos, sin = rope_tables()
    sd, V = jax.ShapeDtypeStruct, pltpu.VMEM
    shapes = [(ROWS[n], SPECS[n][0]) for n in NAMES]
    return pl.pallas_call(
        layer_kernel,
        in_specs=[HB] * 15,
        out_specs=[HB, HB, VM, VM],
        out_shape=[sd((2, D, LEN), bf16), sd((2, F, LEN), bf16), sd((A_ROWS, 128), f32), sd((B_ROWS, 128), f32)],
        scratch_shapes=[
            V((2, F, LEN), bf16), V((2, D, LEN), bf16), V((2, LEN), f32), V((2, NLAG), jnp.int32), V((2, NDATE), jnp.int32),
            *[pltpu.SMEM((2,), jnp.int32)] * 2,
            *[V((SPECS[n][1],), bf16) for n in NAMES], V((2, 9), bf16), V((8, LEN), f32), V((8, LEN), f32),
            V((2, D, LEN), bf16), V((2, F, LEN), bf16),
            V((A_ROWS, 128), f32), V((B_ROWS, 128), bf16),
            V((2, 64, A_ROWS, 128), f32), V((2, 16, 4, B_ROWS, 128), bf16),
            V((128 * A_ROWS, 128), f32), V((128 * B_ROWS, 128), f32),
            V((64, A_ROWS, 128), f32), V((16, 4, B_ROWS, 128), bf16),
            V((64, A_ROWS, 128), f32), V((16, 4, B_ROWS, 128), bf16),
            V((4, B_ROWS, 128), bf16),
            *[V(tiled(n), f32) for n in NAMES], *[V(s, bf16) for s in shapes], *[V(s[::-1], bf16) for s in shapes],
            V((D, 2), f32), V((2, D, 128), f32), V((128, 8), f32), V((1, 128), f32),
            V((2, F, LEN), bf16), V((2, D, LEN), f32), V((2, 1, LEN), f32), V((2, D, LEN), bf16),
            V((2, H, HD, LEN), bf16), V((2, H, HD, LEN), bf16), V((2, H, HD, LEN), bf16),
            *[V((2, H, (j + 1) * QT, QT), bf16) for j in range(4)],
            V((2, LEN, QT), f32), V((2, H, 1, LEN), f32), V((2, H, HD, LEN), f32), V((2, H, HD, LEN), bf16),
            V((2, D, LEN), f32), V((D, LEN), bf16), V((2, FF, LEN), bf16), V((2 * FF, LEN), bf16),
            V((2, D, LEN), f32), V((D, LEN), bf16), V((2, H, HD, LEN), f32), V((2, 3, H, HD, LEN), bf16), V((2, D, LEN), bf16),
            V((2, LEN, QT), bf16), *[V((GROUP, HD, LEN), f32)] * 3,
            *[pltpu.SemaphoreType.DMA((2, 3))] * 4, pltpu.SemaphoreType.DMA((17,)), *[pltpu.SemaphoreType.REGULAR] * 2,
        ],
        compiler_params=pltpu.CompilerParams(collective_id=0, has_side_effects=True, vmem_limit_bytes=63 * 2**20),
    )(feats_t, targets, lag_mask, date_mask, freq_ids, dataset_ids, *weights, gains, dout_t, jnp.asarray(cos), jnp.asarray(sin))


def finish_kernel(out_h, gfeats_h, tot_a_h, tot_b_h, running_h, out, gfeats, o_in, o_qkv, o_out, o_gu, o_down, o_gain, o_running,
                  out_v, gfeats_v, tot_a, tot_b, running, sems):
    pairs = ((tot_a_h, tot_a), (tot_b_h, tot_b), (running_h, running), (out_h, out_v), (gfeats_h, gfeats_v))
    copies = [pltpu.make_async_copy(src, dst, sems.at[i]) for i, (src, dst) in enumerate(pairs)]
    stores = [pltpu.make_async_copy(src, dst, sems.at[5 + i]) for i, (src, dst) in enumerate(((out_v, out), (gfeats_v, gfeats)))]
    for copy in copies:
        copy.start()
    for copy in copies:
        copy.wait()
    for store in stores:
        store.start()
    for name, ref in (("in", o_in), ("qkv", o_qkv), ("out", o_out), ("gu", o_gu), ("down", o_down)):
        _, chunk, _, _, which, base = SPECS[name]
        for t, at, width in lane_tiles(chunk):
            ref[pl.ds(at, width)] = (tot_a if which == "a" else tot_b)[base + t, :width]
    o_gain[0:1, :] = tot_a[0:1, 108:117]
    o_gain[1:2, :] = tot_a[0:1, 117:126]
    sums, counts = tot_a[5, :NSET], tot_a[5, NSET : 2 * NSET]
    old = running[...]
    o_running[...] = jnp.where(counts > 0.5, 0.75 * old + 0.25 * (sums / jnp.maximum(counts, 1.0)), old)
    for store in stores:
        store.wait()


def hand_out(out, gfeats, tot_a, tot_b, running):
    sd, V = jax.ShapeDtypeStruct, pltpu.VMEM
    return pl.pallas_call(
        finish_kernel,
        in_specs=[HB] * 5,
        out_specs=[HB, HB] + [VM] * 7,
        out_shape=[sd((2, D, LEN), bf16), sd((2, F, LEN), bf16)]
        + [sd((SPECS[n][1],), f32) for n in NAMES] + [sd((2, 9), f32), sd((NSET,), f32)],
        scratch_shapes=[V((2, D, LEN), bf16), V((2, F, LEN), bf16), V((A_ROWS, 128), f32), V((B_ROWS, 128), f32), V((NSET,), f32),
                        pltpu.SemaphoreType.DMA((7,))],
        compiler_params=pltpu.CompilerParams(vmem_limit_bytes=60 * 2**20),
    )(out, gfeats, tot_a, tot_b, running)


def body(feats, targets, lag_mask, date_mask, freq_ids, dataset_ids, w_in, w_qkv, w_out, w_gu, w_down, gains, running, d_out):
    done = run_layer(
        jnp.swapaxes(feats, 1, 2), targets, lag_mask, date_mask, freq_ids, dataset_ids,
        (w_in, w_qkv, w_out, w_gu, w_down), gains, jnp.swapaxes(d_out, 1, 2),
    )
    out, gfeats, *rest = hand_out(*done, running)
    return (jnp.swapaxes(out, 1, 2), jnp.swapaxes(gfeats, 1, 2), *rest)


def solution(mesh):
    flat, rows, cube = P(BOTH), P(BOTH, None), P(BOTH, None, None)
    return jax.shard_map(
        body,
        mesh=mesh,
        in_specs=(cube, rows, rows, rows, flat, flat, flat, flat, flat, flat, flat, P(None, "dp"), P(), cube),
        out_specs=(cube, cube, flat, flat, flat, flat, flat, P(None, "dp"), P()),
        check_vma=False,
    )
```

```python
import functools

import jax
import jax.numpy as jnp
import numpy as np
from jax import lax
from jax.experimental import pallas as pl
from jax.experimental.pallas import tpu as pltpu
from jax.sharding import PartitionSpec as P

D, H, HD, FF, NDATE, NLAG, F, NSET, LEN = 144, 9, 16, 512, 12, 84, 96, 8, 1024
EPS = 1e-05
TOK_IN = 1024
TOK_MLP = 1024
TOK_BACK = 1024
BLOCK = 128
CH = 128
GROUP = 3
f32, bf16 = jnp.float32, jnp.bfloat16
MESH = pl.DeviceIdType.MESH
BOTH = ("dp", "fsdp")

A_ROWS, B_ROWS = 8, 16
SPECS = {
    "in": (D, 108, 4, 3, "a", 0),
    "qkv": (3 * D, 486, 8, 9, "a", 1),
    "gu": (2 * FF, 1152, 8, 9, "b", 0),
    "down": (D, 576, 2, 8, "b", 9),
    "out": (D, 162, 8, 9, "b", 14),
}
ROWS = {"in": F, "qkv": D, "gu": D, "down": FF, "out": D}


def dot(a, b, ca=1, cb=0, **kw):
    return lax.dot_general(a, b, (((ca,), (cb,)), ((), ())), preferred_element_type=f32, **kw)


def lane_tiles(width):
    return [(t // 128, t, min(128, width - t)) for t in range(0, width, 128)]


def pieces(piece, source, count):
    cuts = []
    for i in range(count):
        at, left, parts = i * piece, piece, []
        while left:
            c, o = divmod(at, source)
            n = min(left, source - o)
            parts.append((c, o, n))
            at, left = at + n, left - n
        cuts.append(parts)
    return cuts


def spot(c):
    return (c % 2) * 64 + c // 2


def join(parts):
    return parts[0] if len(parts) == 1 else jnp.concatenate(parts, axis=1)


def unpack(flat, rows, name, dst):
    cols, chunk, gc, gr, _, base = SPECS[name]
    groups, kept = 128 // gc, {}

    def owner(c):
        if c not in kept:
            kept[c] = join(
                [flat[pl.ds(spot(c) * rows + base + t, groups, stride=gc // 2 * rows), :] for t, _, _ in lane_tiles(chunk)]
            )
        return kept[c]

    for i, parts in enumerate(pieces(cols, chunk, gr)):
        row = join([owner(c)[:, o : o + n] for c, o, n in parts])
        for t, at, width in lane_tiles(cols):
            dst[t, pl.ds(i, groups, stride=gr), :width] = row[:, at : at + width]


def pack(src, name, flat, rows):
    cols, chunk, gc, gr, _, base = SPECS[name]
    groups, kept = 128 // gc, {}

    def line(i):
        if i not in kept:
            kept[i] = join([src[t, pl.ds(i, groups, stride=gr), :] for t, _, _ in lane_tiles(cols)])
        return kept[i]

    for c, parts in enumerate(pieces(chunk, cols, gc)):
        run = [line(i)[:, o : o + n] for i, o, n in parts]
        run = join(run + ([jnp.zeros((groups, -chunk % 128), f32)] if chunk % 128 else []))
        for t, at, _ in lane_tiles(chunk):
            flat[pl.ds(spot(c) * rows + base + t, groups, stride=gc // 2 * rows), :] = run[:, at : at + 128]


def place():
    fs = lax.axis_index("fsdp")
    return lax.axis_index("dp"), fs // 2, fs % 2


def partners():
    dp, y, core = place()
    across = lambda o: (lax.rem(dp + o, 16), 2 * y + core)
    along = lambda o: (dp, 2 * lax.rem(y + o, 4) + core)
    return across, along, (dp, 2 * y + 1 - core)


def chip(dz, dx, dy):
    dp, y, _ = place()
    z, x = dp // 4, lax.rem(dp, 4)
    return 4 * lax.rem(z + dz, 4) + lax.rem(x + dx, 4), lax.rem(y + dy, 4)


def device(dz, dx, dy):
    dp, y = chip(dz, dx, dy)
    return dp, 2 * y + place()[2]


STEPS = (1, 2, 3)
LINES = [(0, 0, o) for o in STEPS] + [(0, o, 0) for o in STEPS] + [(o, 0, 0) for o in STEPS]
X_PLANES = [(0, o, p) for o in STEPS for p in STEPS] + [(p, o, 0) for o in STEPS for p in STEPS]
REST = [(o, p, r) for o in STEPS for p in STEPS for r in STEPS] + [(o, 0, p) for o in STEPS for p in STEPS]


def signal(sem, to):
    pl.semaphore_signal(sem, inc=1, device_id=to, device_id_type=MESH)


def knock():
    barrier = pltpu.get_barrier_semaphore()
    for line in LINES:
        signal(barrier, device(*line))
    signal(barrier, partners()[2])


def enter(sem_x, sem_z, send_to, work):
    pl.semaphore_wait(pltpu.get_barrier_semaphore(), 10)
    for o in STEPS:
        signal(sem_x, device(0, o, 0))
    work[0]()
    for line in LINES:
        send_to(*line)
    work[1]()
    pl.semaphore_wait(sem_x, 3)
    for o in STEPS:
        signal(sem_z, device(o, 0, 0))
    for line in X_PLANES:
        send_to(*line)
    work[2]()
    pl.semaphore_wait(sem_z, 3)
    for line in REST:
        send_to(*line)


def send(src, dst, sems, k, to):
    pltpu.make_async_remote_copy(
        src_ref=src, dst_ref=dst, send_sem=sems.at[0, k], recv_sem=sems.at[1, k], device_id=to, device_id_type=MESH
    ).start()


def wait(ref, sem):
    pltpu.make_async_copy(ref, ref, sem).wait()


class GatherDirect:
    def __init__(self, own, everyone, sems):
        self.own, self.all, self.sems = own, everyone, sems

    def to(self, *line):
        dp, y, core = place()
        send(self.own, self.all.at[core, 4 * dp + y], self.sems, 0, device(*line))

    def second(self):
        dp, y, core = place()
        self.all[core, 4 * dp + y] = self.own[...]
        wait(self.all.at[core, pl.ds(0, 63)], self.sems.at[1, 0])
        send(self.all.at[core], self.all.at[core], self.sems, 1, partners()[2])

    def last(self):
        _, _, core = place()
        wait(self.all.at[core], self.sems.at[1, 1])
        wait(self.all.at[core, pl.ds(0, 63)], self.sems.at[0, 0])
        wait(self.all.at[core], self.sems.at[0, 1])


class ReduceDirect:
    def __init__(self, parts, half, got, sems):
        self.parts, self.half, self.got, self.sems = parts, half, got, sems

    def first(self):
        _, _, core = place()
        send(self.parts.at[1 - core], self.half, self.sems, 0, partners()[2])

    def second(self):
        dp, y, core = place()
        wait(self.half, self.sems.at[1, 0])
        wait(self.half, self.sems.at[0, 0])
        self.half[...] += self.parts[core]
        for line in REST + X_PLANES + LINES:
            to_dp, to_y = chip(*line)
            send(self.half.at[4 * to_dp + to_y], self.got.at[4 * dp + y], self.sems, 1, device(*line))
        self.got[4 * dp + y] = self.half[4 * dp + y]

    def last(self):
        wait(self.got.at[pl.ds(0, 63)], self.sems.at[1, 1])
        wait(self.got.at[pl.ds(0, 63)], self.sems.at[0, 1])
        return jnp.sum(self.got[...], axis=0)


class Gather:
    def __init__(self, own, everyone, sems):
        self.own, self.all, self.sems = own, everyone, sems

    def first(self):
        dp, y, core = place()
        _, along, _ = partners()
        for o in (1, 2, 3):
            send(self.own, self.all.at[core, dp, y], self.sems, 0, along(o))
        self.all[core, dp, y] = self.own[...]

    def second(self):
        dp, y, core = place()
        across, _, _ = partners()
        wait(self.all.at[core, dp, pl.ds(0, 3)], self.sems.at[1, 0])
        wait(self.all.at[core, dp, pl.ds(0, 3)], self.sems.at[0, 0])
        line = self.all.at[core, dp]

        @pl.loop(1, 16)
        def _(o):
            send(line, line, self.sems, 1, across(o))

    def third(self):
        _, _, core = place()
        _, _, sibling = partners()
        wait(self.all.at[core, pl.ds(0, 15)], self.sems.at[1, 1])
        wait(self.all.at[core, pl.ds(0, 15)], self.sems.at[0, 1])
        send(self.all.at[core], self.all.at[core], self.sems, 2, sibling)

    def last(self):
        _, _, core = place()
        wait(self.all.at[core], self.sems.at[1, 2])
        wait(self.all.at[core], self.sems.at[0, 2])


class Reduce:
    def __init__(self, parts, half, row, line, sems):
        self.parts, self.half, self.row, self.line, self.sems = parts, half, row, line, sems

    def first(self):
        _, _, core = place()
        _, _, sibling = partners()
        send(self.parts.at[1 - core], self.half, self.sems, 0, sibling)

    def second(self):
        dp, y, core = place()
        across, _, _ = partners()
        wait(self.half, self.sems.at[1, 0])
        wait(self.half, self.sems.at[0, 0])
        self.half[...] = (self.half[...].astype(f32) + self.parts[core].astype(f32)).astype(self.half.dtype)

        @pl.loop(1, 16)
        def _(o):
            send(self.half.at[lax.rem(dp + o, 16)], self.row.at[dp], self.sems, 1, across(o))

        self.row[dp] = self.half[dp]

    def third(self):
        dp, y, core = place()
        _, along, _ = partners()
        wait(self.row.at[pl.ds(0, 15)], self.sems.at[1, 1])
        wait(self.row.at[pl.ds(0, 15)], self.sems.at[0, 1])
        mine = jnp.sum(self.row[...].astype(f32), axis=0).astype(self.row.dtype)
        self.half[0] = mine
        for o in (1, 2, 3):
            send(self.half.at[0, lax.rem(y + o, 4)], self.line.at[y], self.sems, 2, along(o))
        self.line[y] = self.half[0, y]

    def last(self):
        wait(self.line.at[pl.ds(0, 3)], self.sems.at[1, 2])
        wait(self.line.at[pl.ds(0, 3)], self.sems.at[0, 2])
        return jnp.sum(self.line[...].astype(f32), axis=0)


def rope_tables():
    freqs = np.float32(10000.0) ** (-np.arange(HD // 2, dtype=np.float32) * np.float32(2.0) / np.float32(HD))
    angle = np.arange(LEN, dtype=np.float32)[None, :] * freqs.astype(np.float32)[:, None]
    return np.cos(angle.astype(np.float64)).astype(np.float32), np.sin(angle.astype(np.float64)).astype(np.float32)


def own_tiles(w_in, w_qkv, w_out, w_gu, w_down, gains, tile_a, tile_b, wide):
    tile_a[...] = jnp.zeros_like(tile_a)
    wide[...] = jnp.zeros_like(wide)
    for name, ref in (("in", w_in), ("qkv", w_qkv), ("out", w_out), ("gu", w_gu), ("down", w_down)):
        _, chunk, _, _, which, base = SPECS[name]
        for t, at, width in lane_tiles(chunk):
            (tile_a if which == "a" else wide)[base + t, :width] = ref[pl.ds(at, width)].astype(f32)
    tile_a[0:1, 108:117] = gains[0:1, :].astype(f32)
    tile_a[0:1, 117:126] = gains[1:2, :].astype(f32)
    tile_b[...] = wide[...].astype(bf16)


def gain_columns(flat, out):
    rows = flat[pl.ds(0, 16, stride=4 * A_ROWS), :]
    r = lax.broadcasted_iota(jnp.int32, (D, 16), 0) // 9
    spread = dot((r == lax.broadcasted_iota(jnp.int32, (D, 16), 1)).astype(f32), rows)
    lane = lax.broadcasted_iota(jnp.int32, (D, 128), 1)
    e = lax.rem(lax.broadcasted_iota(jnp.int32, (D, 128), 0), 9)
    for i in (0, 1):
        out[:, i : i + 1] = jnp.sum(jnp.where(lane == e + 108 + 9 * i, spread, 0.0), axis=1, keepdims=True)


def gain_rows(partial, flat):
    pos = lax.broadcasted_iota(jnp.int32, (128, D), 0)
    r = lax.broadcasted_iota(jnp.int32, (128, D), 1) // 9
    pick = (lax.rem(pos, 64) // 4 == r).astype(f32)
    lane = lax.broadcasted_iota(jnp.int32, (D, 128), 1)
    e = lax.rem(lax.broadcasted_iota(jnp.int32, (D, 128), 0), 9)
    cols = jnp.zeros((D, 128), f32)
    for i in (0, 1):
        cols += jnp.where(lane == e + 108 + 9 * i, jnp.sum(partial[i], axis=1, keepdims=True), 0.0)
    spread = dot(pick, cols, precision=lax.Precision.HIGHEST)
    flat[pl.ds(0, 128, stride=A_ROWS), :] += spread


def series_scalars(targets, lag_mask, date_mask, freq, sets, factor, stats):
    scale = jnp.sum(jnp.abs(targets[...]), axis=1, keepdims=True) / LEN + 1e-5
    lag = lag_mask[...].astype(f32) / scale
    second = lax.broadcasted_iota(jnp.int32, (2, NDATE), 0) == 1
    start = jnp.where(second, freq[1], freq[0]) * (NDATE // 3)
    keep = jnp.where(lax.broadcasted_iota(jnp.int32, (2, NDATE), 1) >= start, date_mask[...], 0).astype(f32)
    both = jnp.concatenate([lag, keep], axis=1)
    both = jnp.concatenate([both, jnp.zeros((2, 32), f32)], axis=1)
    both = jnp.concatenate([both, jnp.zeros((6, 128), f32)], axis=0)
    factor[...] = both.T
    lane = lax.broadcasted_iota(jnp.int32, (1, 128), 1)
    row = jnp.zeros((1, 128), f32)
    for s in (0, 1):
        row += jnp.where(lane == sets[s], scale[s : s + 1], 0.0) + jnp.where(lane == sets[s] + NSET, 1.0, 0.0)
    stats[...] = row

def fold(op, a):
    return op(a.reshape(a.shape[0] // 8, 8, a.shape[1]), axis=0)


def weave(gens):
    gens = list(gens)
    while gens:
        for g in list(gens):
            try:
                next(g)
            except StopIteration:
                gens.remove(g)


VM = pl.BlockSpec(memory_space=pltpu.VMEM)
SM = pl.BlockSpec(memory_space=pltpu.SMEM)
HB = pl.BlockSpec(memory_space=pl.ANY)
NAMES = ("in", "qkv", "out", "gu", "down")


def tiled(name):
    return (-(-SPECS[name][0] // 128), ROWS[name], 128)


def heads_of(hh):
    return [hh * GROUP + u for u in range(GROUP)]


TASKS = [(u, j) for j in range(LEN // BLOCK - 1, -1, -1) for u in range(GROUP)]


def chunks(n, size):
    return [(c, min(size, n - c)) for c in range(0, n, size)]


def corners(pair, cols):
    empty = jnp.zeros((HD, BLOCK), bf16)
    return jnp.concatenate(
        [jnp.concatenate([pair[0][:, cols], empty], axis=1), jnp.concatenate([empty, pair[1][:, cols]], axis=1)], axis=0
    )


def attend(hh, q, k, v, prob, sbuf, rl, osum, mixed):
    heads = heads_of(hh)
    kts = [jnp.concatenate([k[0, h], k[1, h]], axis=0).astype(f32).T.astype(bf16) for h in heads]
    ones = (lax.broadcasted_iota(jnp.int32, (HD, LEN), 0) == 0).astype(f32).astype(bf16)
    vs = [jnp.concatenate([v[0, h], v[1, h], ones], axis=0) for h in heads]
    row = lax.broadcasted_iota(jnp.int32, (BLOCK, 2 * BLOCK), 0)
    diagonal = row <= lax.rem(lax.broadcasted_iota(jnp.int32, (BLOCK, 2 * BLOCK), 1), BLOCK)
    tops = {}

    def score(i):
        u, j = TASKS[i]
        n, best = (j + 1) * BLOCK, None
        both = corners((q[0, heads[u]], q[1, heads[u]]), slice(j * BLOCK, n))
        for c in range(0, n, CH):
            x = dot(kts[u][c : c + CH], both)
            if c + CH == n:
                x = jnp.where(diagonal, x, -1e30)
            sbuf[i % 2, c : c + CH] = x
            top = fold(jnp.max, x)
            best = top if best is None else jnp.maximum(best, top)
            yield
        tops[i] = jnp.max(best, axis=0, keepdims=True)

    def exponent(i):
        u, j = TASKS[i]
        for c in range(0, (j + 1) * BLOCK, CH):
            prob[j][heads[u], c : c + CH] = jnp.exp(sbuf[i % 2, c : c + CH] - tops[i]).astype(bf16)
            yield

    def mix(i):
        u, j = TASKS[i]
        h, n, cols = heads[u], (j + 1) * BLOCK, pl.ds(j * BLOCK, BLOCK)
        o = None
        for c, w in chunks(n, 2 * BLOCK):
            x = dot(vs[u][:, c : c + w], prob[j][h, c : c + w])
            o = x if o is None else o + x
            yield
        inv = 1.0 / o[2 * HD : 2 * HD + 1]
        for s in (0, 1):
            part = slice(s * BLOCK, s * BLOCK + BLOCK)
            own = o[s * HD : s * HD + HD, part] * inv[:, part]
            rl[s, h, :, cols] = inv[:, part]
            osum[s, h, :, cols] = own
            mixed[s, h, :, cols] = own.astype(bf16)

    last = len(TASKS)
    for i in range(last + 3):
        weave(
            ([mix(i - 3)] if 0 <= i - 3 else [])
            + ([score(i)] if i < last else [])
            + ([exponent(i - 1)] if 0 <= i - 1 < last else [])
        )


def attend_back(hh, q, k, v, prob, rl, osum, gmixed, cosr, sinr, gjoint, dsb, dq, dk, dv):
    heads = heads_of(hh)
    dos, deltas, vts, ks = [], [], [], []
    for h in heads:
        pair = [(gmixed[s, h] * rl[s, h]).astype(bf16) for s in (0, 1)]
        dos.append(pair)
        deltas.append([jnp.sum(pair[s].astype(f32) * osum[s, h], axis=0, keepdims=True) for s in (0, 1)])
        vts.append(jnp.concatenate([v[0, h], v[1, h]], axis=0).astype(f32).T.astype(bf16))
        ks.append(jnp.concatenate([k[0, h], k[1, h]], axis=0))
    dk[...] = jnp.zeros_like(dk)
    dv[...] = jnp.zeros_like(dv)

    def spread(i):
        u, j = TASKS[i]
        n = (j + 1) * BLOCK
        cols = slice(j * BLOCK, n)
        both = corners(dos[u], cols)
        delta = jnp.concatenate([deltas[u][0][:, cols], deltas[u][1][:, cols]], axis=1)
        for c, w in chunks(n, 2 * BLOCK):
            dp = dot(vts[u][c : c + w], both) - delta
            dsb[i % 2, c : c + w] = (prob[j][heads[u], c : c + w].astype(f32) * dp).astype(bf16)
            yield

    def to_query(i):
        u, j = TASKS[i]
        n = (j + 1) * BLOCK
        x = dot(ks[u][:, :n], dsb[i % 2, :n])
        for s in (0, 1):
            dq[u, s, :, j * BLOCK : n] = x[s * HD : s * HD + HD, s * BLOCK : s * BLOCK + BLOCK]
        yield

    def to_keys(i):
        u, j = TASKS[i]
        both = corners((q[0, heads[u]], q[1, heads[u]]), slice(j * BLOCK, (j + 1) * BLOCK))
        for c, w in chunks((j + 1) * BLOCK, 2 * BLOCK):
            dk[u, :, c : c + w] += dot(both, dsb[i % 2, c : c + w], 1, 1)
            yield

    def to_values(i):
        u, j = TASKS[i]
        both = corners(dos[u], slice(j * BLOCK, (j + 1) * BLOCK))
        for c, w in chunks((j + 1) * BLOCK, 2 * BLOCK):
            dv[u, :, c : c + w] += dot(both, prob[j][heads[u], c : c + w], 1, 1)
            yield

    last = len(TASKS)
    for i in range(last + 1):
        weave(([spread(i), to_values(i)] if i < last else []) + ([to_keys(i - 1), to_query(i - 1)] if i else []))
    c, sn = cosr[...], sinr[...]
    for u, h in enumerate(heads):
        for s in (0, 1):
            for which, val in ((0, dq[u, s] * 0.25), (1, dk[u, s * HD : s * HD + HD])):
                a, b = val[:8], val[8:]
                gjoint[s, which, h] = jnp.concatenate([a * c + b * sn, b * c - a * sn], axis=0).astype(bf16)
            gjoint[s, 2, h] = dv[u, s * HD : s * HD + HD].astype(bf16)


def layer_kernel(
    feats_h, targets_h, lag_h, date_h, freq_h, sets_h, w_in_h, w_qkv_h, w_out_h, w_gu_h, w_down_h, gains_h, dout_h, cos_h, sin_h,
    out_h, gfeats_h, tot_a, tot_b,
    feats, dout, targets, lag_mask, date_mask, freq, sets, w_in, w_qkv, w_out, w_gu, w_down, gains_own, cosr, sinr, out, gfeats,
    tile_a, tile_b, all_a, all_b, flat_a, flat_b, half_a, half_b, row_a, row_b, line_b,
    m_in, m_qkv, m_out, m_gu, m_down, win, wqkv, wout, wgu, wdown, winT, wqkvT, woutT, wguT, wdownT,
    gains, g_gain, factor, stats, lifted, first, inv1, normed, q, k, v, *rest,
):
    knock()
    prob = rest[: LEN // BLOCK]
    (
        sbuf, rl, osum, mixed, middle, second, hidden, both, gmid, gbranch, gmixed, gjoint, gfirst, dsb, dq, dk, dv, sem_a, sem_b, sem_c, sem_d, sem_l, sem_x, sem_z,
    ) = rest[LEN // BLOCK :]
    loads = [
        pltpu.make_async_copy(src, dst, sem_l.at[i])
        for i, (src, dst) in enumerate(
            (
                (w_in_h, w_in), (w_qkv_h, w_qkv), (w_out_h, w_out), (w_gu_h, w_gu), (w_down_h, w_down), (gains_h, gains_own),
                (feats_h, feats), (targets_h, targets), (lag_h, lag_mask), (date_h, date_mask), (freq_h, freq), (sets_h, sets),
                (cos_h, cosr), (sin_h, sinr), (dout_h, dout),
            )
        )
    ]
    for load in loads:
        load.start()

    def tiles():
        for load in loads[:6]:
            load.wait()
        own_tiles(w_in, w_qkv, w_out, w_gu, w_down, gains_own, tile_a, tile_b, flat_b.at[pl.ds(0, B_ROWS)])

    a, b = GatherDirect(tile_a, all_a, sem_a), Gather(tile_b, all_b, sem_b)

    def scalars():
        for load in loads[7:12]:
            load.wait()
        series_scalars(targets, lag_mask, date_mask, freq, sets, factor, stats)
        g_gain[...] = jnp.zeros_like(g_gain)

    def lift():
        for load in loads[6:7] + loads[12:14]:
            load.wait()
        for s in (0, 1):
            lifted[s] = (feats[s].astype(f32) * factor[:F, s : s + 1]).astype(bf16)

    enter(sem_x, sem_z, a.to, (tiles, scalars, lift))
    b.first()
    a.second()
    a.last()
    b.second()
    flat_a[...] = all_a[...].reshape(128 * A_ROWS, 128)
    gain_columns(flat_a, gains)

    def emit(name, flat, rows, mat, out, outT):
        unpack(flat, rows, name, mat)
        for t, at, width in lane_tiles(SPECS[name][0]):
            val = mat[t][:, :width]
            out[:, at : at + width] = val.astype(bf16)
            outT[at : at + width, :] = val.T.astype(bf16)
        mat[...] = jnp.zeros_like(mat)

    emit("in", flat_a, A_ROWS, m_in, win, winT)
    emit("qkv", flat_a, A_ROWS, m_qkv, wqkv, wqkvT)

    def add_to(ref, val):
        for t, at, width in lane_tiles(val.shape[1]):
            ref[t, :, :width] += val[:, at : at + width]

    gain0 = gains[:, 0:1]
    gain1 = gains[:, 1:2]

    @pl.loop(0, 2)
    def _(s):
        @pl.loop(0, LEN // TOK_IN)
        def _(i):
            t = pl.ds(pl.multiple_of(i * TOK_IN, TOK_IN), TOK_IN)
            x = dot(winT[...], lifted[s, :, t])
            first[s, :, t] = x
            r = lax.rsqrt(jnp.mean(x * x, axis=0, keepdims=True) + EPS)
            inv1[s, :, t] = r
            n = (x * r * gain0).astype(bf16)
            normed[s, :, t] = n
            joint = dot(wqkvT[...], n).reshape(3, H, HD, TOK_IN)
            c, sn = cosr[:, t][None], sinr[:, t][None]
            for which, ref, scale in ((0, q, 0.25), (1, k, 1.0)):
                u, w = joint[which, :, :8], joint[which, :, 8:]
                ref[s, :, :, t] = (jnp.concatenate([u * c - w * sn, w * c + u * sn], axis=1) * scale).astype(bf16)
            v[s, :, :, t] = joint[2].astype(bf16)

    @pl.loop(0, H // GROUP)
    def _(hh):
        attend(hh, q, k, v, prob, sbuf, rl, osum, mixed)

        @pl.when(hh == 0)
        def _():
            b.third()

    b.last()
    flat_b[...] = all_b[...].astype(f32).reshape(128 * B_ROWS, 128)
    emit("out", flat_b, B_ROWS, m_out, wout, woutT)
    emit("gu", flat_b, B_ROWS, m_gu, wgu, wguT)
    emit("down", flat_b, B_ROWS, m_down, wdown, wdownT)
    loads[14].wait()

    @pl.loop(0, 2)
    def _(s):
        @pl.loop(0, LEN // TOK_MLP)
        def _(i):
            t = pl.ds(pl.multiple_of(i * TOK_MLP, TOK_MLP), TOK_MLP)
            mid = first[s, :, t] + dot(woutT[...], mixed[s, :, :, t].reshape(D, TOK_MLP))
            r = lax.rsqrt(jnp.mean(mid * mid, axis=0, keepdims=True) + EPS)
            sec = (mid * r * gain1).astype(bf16)
            second[:, t] = sec
            g = dout[s, :, t]
            for f in range(0, FF, 128):
                gate = dot(wguT[f : f + 128], sec)
                up = dot(wguT[FF + f : FF + f + 128], sec)
                gh = dot(wdown[f : f + 128], g)
                sig = 1.0 / (1.0 + jnp.exp(-gate))
                silu = gate * sig
                hidden[s, f : f + 128, t] = (silu * up).astype(bf16)
                both[FF + f : FF + f + 128, t] = (gh * silu).astype(bf16)
                both[f : f + 128, t] = (gh * up * (sig + silu * (1.0 - sig))).astype(bf16)
            middle[s, :, t] = mid
            c = dot(wgu[...], both[:, t])
            cg = c * gain1
            inner = jnp.mean(cg * mid, axis=0, keepdims=True)
            gain_part = c * mid * r
            g_gain[1] += functools.reduce(jnp.add, [gain_part[:, x : x + 128] for x in range(0, TOK_MLP, 128)])
            gm = g.astype(f32) + r * cg - mid * (r * r * r * inner)
            gmid[s, :, t] = gm
            gb = gm.astype(bf16)
            gbranch[:, t] = gb
            gmixed[s, :, :, t] = dot(wout[...], gb).reshape(H, HD, TOK_MLP)

        add_to(m_down, dot(hidden[s], dout[s], 1, 1))
        add_to(m_gu, dot(second[...], both[...], 1, 1))
        add_to(m_out, dot(mixed[s].reshape(D, LEN), gbranch[...], 1, 1))

    flat_b[...] = jnp.zeros_like(flat_b)
    pack(m_out, "out", flat_b, B_ROWS)
    pack(m_gu, "gu", flat_b, B_ROWS)
    pack(m_down, "down", flat_b, B_ROWS)
    all_b[...] = flat_b[...].reshape(all_b.shape).astype(bf16)
    a, b = ReduceDirect(all_a, half_a, row_a, sem_c), Reduce(all_b, half_b, row_b, line_b, sem_d)
    b.first()

    @pl.loop(0, H // GROUP)
    def _(hh):
        attend_back(hh, q, k, v, prob, rl, osum, gmixed, cosr, sinr, gjoint, dsb, dq, dk, dv)

        @pl.when(hh == 0)
        def _():
            b.second()

    b.third()

    @pl.loop(0, 2)
    def _(s):
        add_to(m_qkv, dot(normed[s], gjoint[s].reshape(3 * D, LEN), 1, 1))
        @pl.loop(0, LEN // TOK_BACK)
        def _(i):
            t = pl.ds(pl.multiple_of(i * TOK_BACK, TOK_BACK), TOK_BACK)
            c = dot(wqkv[...], gjoint[s, :, :, :, t].reshape(3 * D, TOK_BACK))
            x, r = first[s, :, t], inv1[s, :, t]
            cg = c * gain0
            inner = jnp.mean(cg * x, axis=0, keepdims=True)
            gain_part = c * x * r
            g_gain[0] += functools.reduce(jnp.add, [gain_part[:, x : x + 128] for x in range(0, TOK_BACK, 128)])
            gf = (gmid[s, :, t] + r * cg - x * (r * r * r * inner)).astype(bf16)
            gfirst[s, :, t] = gf

        add_to(m_in, dot(lifted[s], gfirst[s], 1, 1))

    flat_a[...] = jnp.zeros_like(flat_a)
    pack(m_in, "in", flat_a, A_ROWS)
    pack(m_qkv, "qkv", flat_a, A_ROWS)
    gain_rows(g_gain, flat_a)
    flat_a[pl.ds(5, 128, stride=A_ROWS), :] = jnp.broadcast_to(stats[...], (128, 128))
    all_a[...] = flat_a[...].reshape(all_a.shape)
    a.first()
    tot_b[...] = b.last()
    a.second()

    for s in (0, 1):
        out[s] = (middle[s] + dot(wdownT[...], hidden[s])).astype(bf16)
        gfeats[s] = (dot(win[...], gfirst[s]) * factor[:F, s : s + 1]).astype(bf16)
    store_out = pltpu.make_async_copy(out, out_h, sem_l.at[15])
    store_out.start()
    store_gfeats = pltpu.make_async_copy(gfeats, gfeats_h, sem_l.at[16])
    store_gfeats.start()
    tot_a[...] = a.last()
    store_out.wait()
    store_gfeats.wait()


def run_layer(feats_t, targets, lag_mask, date_mask, freq_ids, dataset_ids, weights, gains, dout_t):
    cos, sin = rope_tables()
    sd, V = jax.ShapeDtypeStruct, pltpu.VMEM
    shapes = [(ROWS[n], SPECS[n][0]) for n in NAMES]
    return pl.pallas_call(
        layer_kernel,
        in_specs=[HB] * 15,
        out_specs=[HB, HB, VM, VM],
        out_shape=[sd((2, D, LEN), bf16), sd((2, F, LEN), bf16), sd((A_ROWS, 128), f32), sd((B_ROWS, 128), f32)],
        scratch_shapes=[
            V((2, F, LEN), bf16), V((2, D, LEN), bf16), V((2, LEN), f32), V((2, NLAG), jnp.int32), V((2, NDATE), jnp.int32),
            *[pltpu.SMEM((2,), jnp.int32)] * 2,
            *[V((SPECS[n][1],), bf16) for n in NAMES], V((2, 9), bf16), V((8, LEN), f32), V((8, LEN), f32),
            V((2, D, LEN), bf16), V((2, F, LEN), bf16),
            V((A_ROWS, 128), f32), V((B_ROWS, 128), bf16),
            V((2, 64, A_ROWS, 128), f32), V((2, 16, 4, B_ROWS, 128), bf16),
            V((128 * A_ROWS, 128), f32), V((128 * B_ROWS, 128), f32),
            V((64, A_ROWS, 128), f32), V((16, 4, B_ROWS, 128), bf16),
            V((64, A_ROWS, 128), f32), V((16, 4, B_ROWS, 128), bf16),
            V((4, B_ROWS, 128), bf16),
            *[V(tiled(n), f32) for n in NAMES], *[V(s, bf16) for s in shapes], *[V(s[::-1], bf16) for s in shapes],
            V((D, 2), f32), V((2, D, 128), f32), V((128, 8), f32), V((1, 128), f32),
            V((2, F, LEN), bf16), V((2, D, LEN), f32), V((2, 1, LEN), f32), V((2, D, LEN), bf16),
            V((2, H, HD, LEN), bf16), V((2, H, HD, LEN), bf16), V((2, H, HD, LEN), bf16),
            *[V((H, (j + 1) * BLOCK, 2 * BLOCK), bf16) for j in range(LEN // BLOCK)],
            V((2, LEN, 2 * BLOCK), f32), V((2, H, 1, LEN), f32), V((2, H, HD, LEN), f32), V((2, H, HD, LEN), bf16),
            V((2, D, LEN), f32), V((D, LEN), bf16), V((2, FF, LEN), bf16), V((2 * FF, LEN), bf16),
            V((2, D, LEN), f32), V((D, LEN), bf16), V((2, H, HD, LEN), f32), V((2, 3, H, HD, LEN), bf16), V((2, D, LEN), bf16),
            V((2, LEN, 2 * BLOCK), bf16), V((GROUP, 2, HD, LEN), f32), *[V((GROUP, 2 * HD, LEN), f32)] * 2,
            *[pltpu.SemaphoreType.DMA((2, 3))] * 4, pltpu.SemaphoreType.DMA((17,)), *[pltpu.SemaphoreType.REGULAR] * 2,
        ],
        compiler_params=pltpu.CompilerParams(collective_id=0, has_side_effects=True, vmem_limit_bytes=63 * 2**20),
    )(feats_t, targets, lag_mask, date_mask, freq_ids, dataset_ids, *weights, gains, dout_t, jnp.asarray(cos), jnp.asarray(sin))


def finish_kernel(out_h, gfeats_h, tot_a_h, tot_b_h, running_h, out, gfeats, o_in, o_qkv, o_out, o_gu, o_down, o_gain, o_running,
                  out_v, gfeats_v, tot_a, tot_b, running, sems):
    pairs = ((tot_a_h, tot_a), (tot_b_h, tot_b), (running_h, running), (out_h, out_v), (gfeats_h, gfeats_v))
    copies = [pltpu.make_async_copy(src, dst, sems.at[i]) for i, (src, dst) in enumerate(pairs)]
    stores = [pltpu.make_async_copy(src, dst, sems.at[5 + i]) for i, (src, dst) in enumerate(((out_v, out), (gfeats_v, gfeats)))]
    for copy in copies:
        copy.start()
    for copy in copies:
        copy.wait()
    for store in stores:
        store.start()
    for name, ref in (("in", o_in), ("qkv", o_qkv), ("out", o_out), ("gu", o_gu), ("down", o_down)):
        _, chunk, _, _, which, base = SPECS[name]
        for t, at, width in lane_tiles(chunk):
            ref[pl.ds(at, width)] = (tot_a if which == "a" else tot_b)[base + t, :width]
    o_gain[0:1, :] = tot_a[0:1, 108:117]
    o_gain[1:2, :] = tot_a[0:1, 117:126]
    sums, counts = tot_a[5, :NSET], tot_a[5, NSET : 2 * NSET]
    old = running[...]
    o_running[...] = jnp.where(counts > 0.5, 0.75 * old + 0.25 * (sums / jnp.maximum(counts, 1.0)), old)
    for store in stores:
        store.wait()


def hand_out(out, gfeats, tot_a, tot_b, running):
    sd, V = jax.ShapeDtypeStruct, pltpu.VMEM
    return pl.pallas_call(
        finish_kernel,
        in_specs=[HB] * 5,
        out_specs=[HB, HB] + [VM] * 7,
        out_shape=[sd((2, D, LEN), bf16), sd((2, F, LEN), bf16)]
        + [sd((SPECS[n][1],), f32) for n in NAMES] + [sd((2, 9), f32), sd((NSET,), f32)],
        scratch_shapes=[V((2, D, LEN), bf16), V((2, F, LEN), bf16), V((A_ROWS, 128), f32), V((B_ROWS, 128), f32), V((NSET,), f32),
                        pltpu.SemaphoreType.DMA((7,))],
        compiler_params=pltpu.CompilerParams(vmem_limit_bytes=60 * 2**20),
    )(out, gfeats, tot_a, tot_b, running)


def body(feats, targets, lag_mask, date_mask, freq_ids, dataset_ids, w_in, w_qkv, w_out, w_gu, w_down, gains, running, d_out):
    done = run_layer(
        jnp.swapaxes(feats, 1, 2), targets, lag_mask, date_mask, freq_ids, dataset_ids,
        (w_in, w_qkv, w_out, w_gu, w_down), gains, jnp.swapaxes(d_out, 1, 2),
    )
    out, gfeats, *rest = hand_out(*done, running)
    return (jnp.swapaxes(out, 1, 2), jnp.swapaxes(gfeats, 1, 2), *rest)


def solution(mesh):
    flat, rows, cube = P(BOTH), P(BOTH, None), P(BOTH, None, None)
    return jax.shard_map(
        body,
        mesh=mesh,
        in_specs=(cube, rows, rows, rows, flat, flat, flat, flat, flat, flat, flat, P(None, "dp"), P(), cube),
        out_specs=(cube, cube, flat, flat, flat, flat, flat, P(None, "dp"), P()),
        check_vma=False,
    )
```

```python
import functools

import jax
import jax.numpy as jnp
import numpy as np
from jax import lax
from jax.experimental import pallas as pl
from jax.experimental.pallas import tpu as pltpu
from jax.sharding import PartitionSpec as P

D, H, HD, FF, NDATE, NLAG, F, NSET, LEN = 144, 9, 16, 512, 12, 84, 96, 8, 1024
EPS = 1e-05
TOK_IN = 1024
TOK_MLP = 1024
TOK_BACK = 1024
BLOCK = 128
CH = 128
GROUP = 3
f32, bf16 = jnp.float32, jnp.bfloat16
MESH = pl.DeviceIdType.MESH
BOTH = ("dp", "fsdp")

A_ROWS, B_ROWS = 8, 16
SPECS = {
    "in": (D, 108, 4, 3, "a", 0),
    "qkv": (3 * D, 486, 8, 9, "a", 1),
    "gu": (2 * FF, 1152, 8, 9, "b", 0),
    "down": (D, 576, 2, 8, "b", 9),
    "out": (D, 162, 8, 9, "b", 14),
}
ROWS = {"in": F, "qkv": D, "gu": D, "down": FF, "out": D}


def dot(a, b, ca=1, cb=0, **kw):
    return lax.dot_general(a, b, (((ca,), (cb,)), ((), ())), preferred_element_type=f32, **kw)


def lane_tiles(width):
    return [(t // 128, t, min(128, width - t)) for t in range(0, width, 128)]


def pieces(piece, source, count):
    cuts = []
    for i in range(count):
        at, left, parts = i * piece, piece, []
        while left:
            c, o = divmod(at, source)
            n = min(left, source - o)
            parts.append((c, o, n))
            at, left = at + n, left - n
        cuts.append(parts)
    return cuts


def spot(c):
    return (c % 2) * 64 + c // 2


def join(parts):
    return parts[0] if len(parts) == 1 else jnp.concatenate(parts, axis=1)


def unpack(flat, rows, name, dst):
    cols, chunk, gc, gr, _, base = SPECS[name]
    groups, kept = 128 // gc, {}

    def owner(c):
        if c not in kept:
            kept[c] = join(
                [flat[pl.ds(spot(c) * rows + base + t, groups, stride=gc // 2 * rows), :] for t, _, _ in lane_tiles(chunk)]
            )
        return kept[c]

    for i, parts in enumerate(pieces(cols, chunk, gr)):
        row = join([owner(c)[:, o : o + n] for c, o, n in parts])
        for t, at, width in lane_tiles(cols):
            dst[t, pl.ds(i, groups, stride=gr), :width] = row[:, at : at + width]


def pack(src, name, flat, rows):
    cols, chunk, gc, gr, _, base = SPECS[name]
    groups, kept = 128 // gc, {}

    def line(i):
        if i not in kept:
            kept[i] = join([src[t, pl.ds(i, groups, stride=gr), :] for t, _, _ in lane_tiles(cols)])
        return kept[i]

    for c, parts in enumerate(pieces(chunk, cols, gc)):
        run = [line(i)[:, o : o + n] for i, o, n in parts]
        run = join(run + ([jnp.zeros((groups, -chunk % 128), f32)] if chunk % 128 else []))
        for t, at, _ in lane_tiles(chunk):
            flat[pl.ds(spot(c) * rows + base + t, groups, stride=gc // 2 * rows), :] = run[:, at : at + 128]


def place():
    fs = lax.axis_index("fsdp")
    return lax.axis_index("dp"), fs // 2, fs % 2


def partners():
    dp, y, core = place()
    across = lambda o: (lax.rem(dp + o, 16), 2 * y + core)
    along = lambda o: (dp, 2 * lax.rem(y + o, 4) + core)
    return across, along, (dp, 2 * y + 1 - core)


def chip(dz, dx, dy):
    dp, y, _ = place()
    z, x = dp // 4, lax.rem(dp, 4)
    return 4 * lax.rem(z + dz, 4) + lax.rem(x + dx, 4), lax.rem(y + dy, 4)


def device(dz, dx, dy):
    dp, y = chip(dz, dx, dy)
    return dp, 2 * y + place()[2]


STEPS = (1, 2, 3)
LINES = [(0, 0, o) for o in STEPS] + [(0, o, 0) for o in STEPS] + [(o, 0, 0) for o in STEPS]
X_PLANES = [(0, o, p) for o in STEPS for p in STEPS] + [(p, o, 0) for o in STEPS for p in STEPS]
REST = [(o, p, r) for o in STEPS for p in STEPS for r in STEPS] + [(o, 0, p) for o in STEPS for p in STEPS]


def signal(sem, to):
    pl.semaphore_signal(sem, inc=1, device_id=to, device_id_type=MESH)


def knock():
    barrier = pltpu.get_barrier_semaphore()
    for line in LINES:
        signal(barrier, device(*line))
    signal(barrier, partners()[2])


def enter(sem_x, sem_z, send_to, work):
    pl.semaphore_wait(pltpu.get_barrier_semaphore(), 10)
    for o in STEPS:
        signal(sem_x, device(0, o, 0))
    work[0]()
    for line in LINES:
        send_to(*line)
    work[1]()
    pl.semaphore_wait(sem_x, 3)
    for o in STEPS:
        signal(sem_z, device(o, 0, 0))
    for line in X_PLANES:
        send_to(*line)
    work[2]()
    pl.semaphore_wait(sem_z, 3)
    for line in REST:
        send_to(*line)


def send(src, dst, sems, k, to):
    pltpu.make_async_remote_copy(
        src_ref=src, dst_ref=dst, send_sem=sems.at[0, k], recv_sem=sems.at[1, k], device_id=to, device_id_type=MESH
    ).start()


def wait(ref, sem):
    pltpu.make_async_copy(ref, ref, sem).wait()


class GatherDirect:
    def __init__(self, own, everyone, sems):
        self.own, self.all, self.sems = own, everyone, sems

    def to(self, *line):
        dp, y, core = place()
        send(self.own, self.all.at[core, 4 * dp + y], self.sems, 0, device(*line))

    def second(self):
        dp, y, core = place()
        self.all[core, 4 * dp + y] = self.own[...]
        wait(self.all.at[core, pl.ds(0, 63)], self.sems.at[1, 0])
        send(self.all.at[core], self.all.at[core], self.sems, 1, partners()[2])

    def last(self):
        _, _, core = place()
        wait(self.all.at[core], self.sems.at[1, 1])
        wait(self.all.at[core, pl.ds(0, 63)], self.sems.at[0, 0])
        wait(self.all.at[core], self.sems.at[0, 1])


class ReduceDirect:
    def __init__(self, parts, half, got, sems):
        self.parts, self.half, self.got, self.sems = parts, half, got, sems

    def first(self):
        _, _, core = place()
        send(self.parts.at[1 - core], self.half, self.sems, 0, partners()[2])

    def second(self):
        dp, y, core = place()
        wait(self.half, self.sems.at[1, 0])
        wait(self.half, self.sems.at[0, 0])
        self.half[...] += self.parts[core]
        for line in REST + X_PLANES + LINES:
            to_dp, to_y = chip(*line)
            send(self.half.at[4 * to_dp + to_y], self.got.at[4 * dp + y], self.sems, 1, device(*line))
        self.got[4 * dp + y] = self.half[4 * dp + y]

    def last(self):
        wait(self.got.at[pl.ds(0, 63)], self.sems.at[1, 1])
        wait(self.got.at[pl.ds(0, 63)], self.sems.at[0, 1])
        return jnp.sum(self.got[...], axis=0)


class Gather:
    def __init__(self, own, everyone, sems):
        self.own, self.all, self.sems = own, everyone, sems

    def first(self):
        dp, y, core = place()
        _, along, _ = partners()
        for o in (1, 2, 3):
            send(self.own, self.all.at[core, dp, y], self.sems, 0, along(o))
        self.all[core, dp, y] = self.own[...]

    def second(self):
        dp, y, core = place()
        across, _, _ = partners()
        wait(self.all.at[core, dp, pl.ds(0, 3)], self.sems.at[1, 0])
        wait(self.all.at[core, dp, pl.ds(0, 3)], self.sems.at[0, 0])
        line = self.all.at[core, dp]

        @pl.loop(1, 16)
        def _(o):
            send(line, line, self.sems, 1, across(o))

    def third(self):
        _, _, core = place()
        _, _, sibling = partners()
        wait(self.all.at[core, pl.ds(0, 15)], self.sems.at[1, 1])
        wait(self.all.at[core, pl.ds(0, 15)], self.sems.at[0, 1])
        send(self.all.at[core], self.all.at[core], self.sems, 2, sibling)

    def last(self):
        _, _, core = place()
        wait(self.all.at[core], self.sems.at[1, 2])
        wait(self.all.at[core], self.sems.at[0, 2])


class Reduce:
    def __init__(self, parts, half, row, line, sems):
        self.parts, self.half, self.row, self.line, self.sems = parts, half, row, line, sems

    def first(self):
        _, _, core = place()
        _, _, sibling = partners()
        send(self.parts.at[1 - core], self.half, self.sems, 0, sibling)

    def second(self):
        dp, y, core = place()
        across, _, _ = partners()
        wait(self.half, self.sems.at[1, 0])
        wait(self.half, self.sems.at[0, 0])
        self.half[...] = (self.half[...].astype(f32) + self.parts[core].astype(f32)).astype(self.half.dtype)

        @pl.loop(1, 16)
        def _(o):
            send(self.half.at[lax.rem(dp + o, 16)], self.row.at[dp], self.sems, 1, across(o))

        self.row[dp] = self.half[dp]

    def third(self):
        dp, y, core = place()
        _, along, _ = partners()
        wait(self.row.at[pl.ds(0, 15)], self.sems.at[1, 1])
        wait(self.row.at[pl.ds(0, 15)], self.sems.at[0, 1])
        mine = jnp.sum(self.row[...].astype(f32), axis=0).astype(self.row.dtype)
        self.half[0] = mine
        for o in (1, 2, 3):
            send(self.half.at[0, lax.rem(y + o, 4)], self.line.at[y], self.sems, 2, along(o))
        self.line[y] = self.half[0, y]

    def last(self):
        wait(self.line.at[pl.ds(0, 3)], self.sems.at[1, 2])
        wait(self.line.at[pl.ds(0, 3)], self.sems.at[0, 2])
        return jnp.sum(self.line[...].astype(f32), axis=0)


def rope_tables():
    freqs = np.float32(10000.0) ** (-np.arange(HD // 2, dtype=np.float32) * np.float32(2.0) / np.float32(HD))
    angle = np.arange(LEN, dtype=np.float32)[None, :] * freqs.astype(np.float32)[:, None]
    return np.cos(angle.astype(np.float64)).astype(np.float32), np.sin(angle.astype(np.float64)).astype(np.float32)


def own_tiles(w_in, w_qkv, w_out, w_gu, w_down, gains, tile_a, tile_b, wide):
    tile_a[...] = jnp.zeros_like(tile_a)
    wide[...] = jnp.zeros_like(wide)
    for name, ref in (("in", w_in), ("qkv", w_qkv), ("out", w_out), ("gu", w_gu), ("down", w_down)):
        _, chunk, _, _, which, base = SPECS[name]
        for t, at, width in lane_tiles(chunk):
            (tile_a if which == "a" else wide)[base + t, :width] = ref[pl.ds(at, width)].astype(f32)
    tile_a[0:1, 108:117] = gains[0:1, :].astype(f32)
    tile_a[0:1, 117:126] = gains[1:2, :].astype(f32)
    tile_b[...] = wide[...].astype(bf16)


def gain_columns(flat, out):
    rows = flat[pl.ds(0, 16, stride=4 * A_ROWS), :]
    r = lax.broadcasted_iota(jnp.int32, (D, 16), 0) // 9
    spread = dot((r == lax.broadcasted_iota(jnp.int32, (D, 16), 1)).astype(f32), rows)
    lane = lax.broadcasted_iota(jnp.int32, (D, 128), 1)
    e = lax.rem(lax.broadcasted_iota(jnp.int32, (D, 128), 0), 9)
    for i in (0, 1):
        out[:, i : i + 1] = jnp.sum(jnp.where(lane == e + 108 + 9 * i, spread, 0.0), axis=1, keepdims=True)


def gain_rows(partial, flat):
    pos = lax.broadcasted_iota(jnp.int32, (128, D), 0)
    r = lax.broadcasted_iota(jnp.int32, (128, D), 1) // 9
    pick = (lax.rem(pos, 64) // 4 == r).astype(f32)
    lane = lax.broadcasted_iota(jnp.int32, (D, 128), 1)
    e = lax.rem(lax.broadcasted_iota(jnp.int32, (D, 128), 0), 9)
    cols = jnp.zeros((D, 128), f32)
    for i in (0, 1):
        cols += jnp.where(lane == e + 108 + 9 * i, jnp.sum(partial[i], axis=1, keepdims=True), 0.0)
    spread = dot(pick, cols, precision=lax.Precision.HIGHEST)
    flat[pl.ds(0, 128, stride=A_ROWS), :] += spread


def series_scalars(targets, lag_mask, date_mask, freq, sets, factor, stats):
    scale = jnp.sum(jnp.abs(targets[...]), axis=1, keepdims=True) / LEN + 1e-5
    lag = lag_mask[...].astype(f32) / scale
    second = lax.broadcasted_iota(jnp.int32, (2, NDATE), 0) == 1
    start = jnp.where(second, freq[1], freq[0]) * (NDATE // 3)
    keep = jnp.where(lax.broadcasted_iota(jnp.int32, (2, NDATE), 1) >= start, date_mask[...], 0).astype(f32)
    both = jnp.concatenate([lag, keep], axis=1)
    both = jnp.concatenate([both, jnp.zeros((2, 32), f32)], axis=1)
    both = jnp.concatenate([both, jnp.zeros((6, 128), f32)], axis=0)
    factor[...] = both.T
    lane = lax.broadcasted_iota(jnp.int32, (1, 128), 1)
    row = jnp.zeros((1, 128), f32)
    for s in (0, 1):
        row += jnp.where(lane == sets[s], scale[s : s + 1], 0.0) + jnp.where(lane == sets[s] + NSET, 1.0, 0.0)
    stats[...] = row

def fold(op, a):
    return op(a.reshape(a.shape[0] // 8, 8, a.shape[1]), axis=0)


def weave(gens):
    gens = list(gens)
    while gens:
        for g in list(gens):
            try:
                next(g)
            except StopIteration:
                gens.remove(g)


VM = pl.BlockSpec(memory_space=pltpu.VMEM)
SM = pl.BlockSpec(memory_space=pltpu.SMEM)
HB = pl.BlockSpec(memory_space=pl.ANY)
NAMES = ("in", "qkv", "out", "gu", "down")


def tiled(name):
    return (-(-SPECS[name][0] // 128), ROWS[name], 128)


def heads_of(hh):
    return [hh * GROUP + u for u in range(GROUP)]


TASKS = [(u, j) for j in range(LEN // BLOCK - 1, -1, -1) for u in range(GROUP)]


def chunks(n, size):
    return [(c, min(size, n - c)) for c in range(0, n, size)]


def corners(pair, cols):
    empty = jnp.zeros((HD, BLOCK), bf16)
    return jnp.concatenate(
        [jnp.concatenate([pair[0][:, cols], empty], axis=1), jnp.concatenate([empty, pair[1][:, cols]], axis=1)], axis=0
    )


def attend(hh, q, k, v, prob, sbuf, rl, osum, mixed):
    heads = heads_of(hh)
    kts = [jnp.concatenate([k[0, h], k[1, h]], axis=0).astype(f32).T.astype(bf16) for h in heads]
    ones = (lax.broadcasted_iota(jnp.int32, (HD, LEN), 0) == 0).astype(f32).astype(bf16)
    vs = [jnp.concatenate([v[0, h], v[1, h], ones], axis=0) for h in heads]
    row = lax.broadcasted_iota(jnp.int32, (BLOCK, 2 * BLOCK), 0)
    diagonal = row <= lax.rem(lax.broadcasted_iota(jnp.int32, (BLOCK, 2 * BLOCK), 1), BLOCK)
    tops = {}

    def score(i):
        u, j = TASKS[i]
        n, best = (j + 1) * BLOCK, None
        both = corners((q[0, heads[u]], q[1, heads[u]]), slice(j * BLOCK, n))
        for c in range(0, n, CH):
            x = dot(kts[u][c : c + CH], both)
            if c + CH == n:
                x = jnp.where(diagonal, x, -1e30)
            sbuf[i % 2, c : c + CH] = x
            top = fold(jnp.max, x)
            best = top if best is None else jnp.maximum(best, top)
            yield
        tops[i] = jnp.max(best, axis=0, keepdims=True)

    def exponent(i):
        u, j = TASKS[i]
        for c in range(0, (j + 1) * BLOCK, CH):
            prob[j][heads[u], c : c + CH] = jnp.exp(sbuf[i % 2, c : c + CH] - tops[i]).astype(bf16)
            yield

    def mix(i):
        u, j = TASKS[i]
        h, n, cols = heads[u], (j + 1) * BLOCK, pl.ds(j * BLOCK, BLOCK)
        o = None
        for c, w in chunks(n, 2 * BLOCK):
            x = dot(vs[u][:, c : c + w], prob[j][h, c : c + w])
            o = x if o is None else o + x
            yield
        inv = 1.0 / o[2 * HD : 2 * HD + 1]
        for s in (0, 1):
            part = slice(s * BLOCK, s * BLOCK + BLOCK)
            own = o[s * HD : s * HD + HD, part] * inv[:, part]
            rl[s, h, :, cols] = inv[:, part]
            osum[s, h, :, cols] = own
            mixed[s, h, :, cols] = own.astype(bf16)

    last = len(TASKS)
    for i in range(last + 3):
        weave(
            ([mix(i - 3)] if 0 <= i - 3 else [])
            + ([score(i)] if i < last else [])
            + ([exponent(i - 1)] if 0 <= i - 1 < last else [])
        )


def attend_back(hh, q, k, v, prob, rl, osum, gmixed, cosr, sinr, gjoint, dsb, dq, dk, dv):
    heads = heads_of(hh)
    dos, deltas, vts, ks = [], [], [], []
    for h in heads:
        pair = [(gmixed[s, h] * rl[s, h]).astype(bf16) for s in (0, 1)]
        dos.append(pair)
        deltas.append([jnp.sum(pair[s].astype(f32) * osum[s, h], axis=0, keepdims=True) for s in (0, 1)])
        vts.append(jnp.concatenate([v[0, h], v[1, h]], axis=0).astype(f32).T.astype(bf16))
        ks.append(jnp.concatenate([k[0, h], k[1, h]], axis=0))
    dk[...] = jnp.zeros_like(dk)
    dv[...] = jnp.zeros_like(dv)

    def spread(i):
        u, j = TASKS[i]
        n = (j + 1) * BLOCK
        cols = slice(j * BLOCK, n)
        both = corners(dos[u], cols)
        delta = jnp.concatenate([deltas[u][0][:, cols], deltas[u][1][:, cols]], axis=1)
        for c, w in chunks(n, 2 * BLOCK):
            dp = dot(vts[u][c : c + w], both) - delta
            dsb[i % 2, c : c + w] = (prob[j][heads[u], c : c + w].astype(f32) * dp).astype(bf16)
            yield

    def to_query(i):
        u, j = TASKS[i]
        n = (j + 1) * BLOCK
        x = dot(ks[u][:, :n], dsb[i % 2, :n])
        for s in (0, 1):
            dq[u, s, :, j * BLOCK : n] = x[s * HD : s * HD + HD, s * BLOCK : s * BLOCK + BLOCK]
        yield

    def to_keys(i):
        u, j = TASKS[i]
        both = corners((q[0, heads[u]], q[1, heads[u]]), slice(j * BLOCK, (j + 1) * BLOCK))
        for c, w in chunks((j + 1) * BLOCK, 2 * BLOCK):
            dk[u, :, c : c + w] += dot(both, dsb[i % 2, c : c + w], 1, 1)
            yield

    def to_values(i):
        u, j = TASKS[i]
        both = corners(dos[u], slice(j * BLOCK, (j + 1) * BLOCK))
        for c, w in chunks((j + 1) * BLOCK, 2 * BLOCK):
            dv[u, :, c : c + w] += dot(both, prob[j][heads[u], c : c + w], 1, 1)
            yield

    last = len(TASKS)
    for i in range(last + 1):
        weave(([spread(i), to_values(i)] if i < last else []) + ([to_keys(i - 1), to_query(i - 1)] if i else []))
    c, sn = cosr[...], sinr[...]
    for u, h in enumerate(heads):
        for s in (0, 1):
            for which, val in ((0, dq[u, s] * 0.25), (1, dk[u, s * HD : s * HD + HD])):
                a, b = val[:8], val[8:]
                gjoint[s, which, h] = jnp.concatenate([a * c + b * sn, b * c - a * sn], axis=0).astype(bf16)
            gjoint[s, 2, h] = dv[u, s * HD : s * HD + HD].astype(bf16)


def layer_kernel(
    feats_h, targets_h, lag_h, date_h, freq_h, sets_h, w_in_h, w_qkv_h, w_out_h, w_gu_h, w_down_h, gains_h, dout_h, cos_h, sin_h,
    out_h, gfeats_h, tot_a, tot_b,
    feats, dout, targets, lag_mask, date_mask, freq, sets, w_in, w_qkv, w_out, w_gu, w_down, gains_own, cosr, sinr, out, gfeats,
    tile_a, tile_b, all_a, all_b, flat_a, flat_b, half_a, half_b, row_a, row_b, line_b,
    m_in, m_qkv, m_out, m_gu, m_down, win, wqkv, wout, wgu, wdown, winT, wqkvT, woutT, wguT, wdownT,
    gains, g_gain, factor, stats, lifted, first, inv1, normed, q, k, v, *rest,
):
    knock()
    prob = rest[: LEN // BLOCK]
    (
        sbuf, rl, osum, mixed, middle, second, hidden, both, gmid, gbranch, gmixed, gjoint, gfirst, dsb, dq, dk, dv, sem_a, sem_b, sem_c, sem_d, sem_l, sem_x, sem_z,
    ) = rest[LEN // BLOCK :]
    loads = [
        pltpu.make_async_copy(src, dst, sem_l.at[i])
        for i, (src, dst) in enumerate(
            (
                (w_in_h, w_in), (w_qkv_h, w_qkv), (w_out_h, w_out), (w_gu_h, w_gu), (w_down_h, w_down), (gains_h, gains_own),
                (feats_h, feats), (targets_h, targets), (lag_h, lag_mask), (date_h, date_mask), (freq_h, freq), (sets_h, sets),
                (cos_h, cosr), (sin_h, sinr), (dout_h, dout),
            )
        )
    ]
    for load in loads:
        load.start()

    def tiles():
        for load in loads[:6]:
            load.wait()
        own_tiles(w_in, w_qkv, w_out, w_gu, w_down, gains_own, tile_a, tile_b, flat_b.at[pl.ds(0, B_ROWS)])

    a, b = GatherDirect(tile_a, all_a, sem_a), Gather(tile_b, all_b, sem_b)

    def scalars():
        for load in loads[7:12]:
            load.wait()
        series_scalars(targets, lag_mask, date_mask, freq, sets, factor, stats)
        g_gain[...] = jnp.zeros_like(g_gain)

    def lift():
        for load in loads[6:7] + loads[12:14]:
            load.wait()
        for s in (0, 1):
            lifted[s] = (feats[s].astype(f32) * factor[:F, s : s + 1]).astype(bf16)

    enter(sem_x, sem_z, a.to, (tiles, scalars, lift))
    b.first()
    a.second()
    a.last()
    b.second()
    flat_a[...] = all_a[...].reshape(128 * A_ROWS, 128)
    gain_columns(flat_a, gains)

    def emit(name, flat, rows, mat, out, outT):
        unpack(flat, rows, name, mat)
        for t, at, width in lane_tiles(SPECS[name][0]):
            val = mat[t][:, :width]
            out[:, at : at + width] = val.astype(bf16)
            down = at if name != "gu" else 2 * at if at < FF else 2 * (at - FF) + 128
            outT[down : down + width, :] = val.T.astype(bf16)
        mat[...] = jnp.zeros_like(mat)

    emit("in", flat_a, A_ROWS, m_in, win, winT)
    emit("qkv", flat_a, A_ROWS, m_qkv, wqkv, wqkvT)

    def add_to(ref, val):
        for t, at, width in lane_tiles(val.shape[1]):
            ref[t, :, :width] += val[:, at : at + width]

    gain0 = gains[:, 0:1]
    gain1 = gains[:, 1:2]

    @pl.loop(0, 2)
    def _(s):
        @pl.loop(0, LEN // TOK_IN)
        def _(i):
            t = pl.ds(pl.multiple_of(i * TOK_IN, TOK_IN), TOK_IN)
            x = dot(winT[...], lifted[s, :, t])
            first[s, :, t] = x
            r = lax.rsqrt(jnp.mean(x * x, axis=0, keepdims=True) + EPS)
            inv1[s, :, t] = r
            n = (x * r * gain0).astype(bf16)
            normed[s, :, t] = n
            joint = dot(wqkvT[...], n).reshape(3, H, HD, TOK_IN)
            c, sn = cosr[:, t][None], sinr[:, t][None]
            for which, ref, scale in ((0, q, 0.25), (1, k, 1.0)):
                u, w = joint[which, :, :8], joint[which, :, 8:]
                ref[s, :, :, t] = (jnp.concatenate([u * c - w * sn, w * c + u * sn], axis=1) * scale).astype(bf16)
            v[s, :, :, t] = joint[2].astype(bf16)

    @pl.loop(0, H // GROUP)
    def _(hh):
        attend(hh, q, k, v, prob, sbuf, rl, osum, mixed)

        @pl.when(hh == 0)
        def _():
            b.third()

    b.last()
    flat_b[...] = all_b[...].astype(f32).reshape(128 * B_ROWS, 128)
    emit("out", flat_b, B_ROWS, m_out, wout, woutT)
    emit("gu", flat_b, B_ROWS, m_gu, wgu, wguT)
    emit("down", flat_b, B_ROWS, m_down, wdown, wdownT)
    loads[14].wait()

    @pl.loop(0, 2)
    def _(s):
        @pl.loop(0, LEN // TOK_MLP)
        def _(i):
            t = pl.ds(pl.multiple_of(i * TOK_MLP, TOK_MLP), TOK_MLP)
            mid = first[s, :, t] + dot(woutT[...], mixed[s, :, :, t].reshape(D, TOK_MLP))
            r = lax.rsqrt(jnp.mean(mid * mid, axis=0, keepdims=True) + EPS)
            sec = (mid * r * gain1).astype(bf16)
            second[:, t] = sec
            g = dout[s, :, t]
            for c in range(0, LEN, 256):
                for f in range(0, FF, 128):
                    part = slice(c, c + 256)
                    x = dot(wguT[2 * f : 2 * f + 256], sec[:, part])
                    gate, up = x[:128], x[128:]
                    gh = dot(wdown[f : f + 128], g[:, part])
                    sig = 1.0 / (1.0 + jnp.exp(-gate))
                    silu = gate * sig
                    hidden[s, f : f + 128, part] = (silu * up).astype(bf16)
                    both[FF + f : FF + f + 128, part] = (gh * silu).astype(bf16)
                    both[f : f + 128, part] = (gh * up * (sig + silu * (1.0 - sig))).astype(bf16)
            middle[s, :, t] = mid
            c = dot(wgu[...], both[:, t])
            cg = c * gain1
            inner = jnp.mean(cg * mid, axis=0, keepdims=True)
            gain_part = c * mid * r
            g_gain[1] += functools.reduce(jnp.add, [gain_part[:, x : x + 128] for x in range(0, TOK_MLP, 128)])
            gm = g.astype(f32) + r * cg - mid * (r * r * r * inner)
            gmid[s, :, t] = gm
            gb = gm.astype(bf16)
            gbranch[:, t] = gb
            gmixed[s, :, :, t] = dot(wout[...], gb).reshape(H, HD, TOK_MLP)

        add_to(m_down, dot(hidden[s], dout[s], 1, 1))
        add_to(m_gu, dot(second[...], both[...], 1, 1))
        add_to(m_out, dot(mixed[s].reshape(D, LEN), gbranch[...], 1, 1))

    flat_b[...] = jnp.zeros_like(flat_b)
    pack(m_out, "out", flat_b, B_ROWS)
    pack(m_gu, "gu", flat_b, B_ROWS)
    pack(m_down, "down", flat_b, B_ROWS)
    all_b[...] = flat_b[...].reshape(all_b.shape).astype(bf16)
    a, b = ReduceDirect(all_a, half_a, row_a, sem_c), Reduce(all_b, half_b, row_b, line_b, sem_d)
    b.first()

    @pl.loop(0, H // GROUP)
    def _(hh):
        attend_back(hh, q, k, v, prob, rl, osum, gmixed, cosr, sinr, gjoint, dsb, dq, dk, dv)

        @pl.when(hh == 0)
        def _():
            b.second()

    b.third()

    @pl.loop(0, 2)
    def _(s):
        add_to(m_qkv, dot(normed[s], gjoint[s].reshape(3 * D, LEN), 1, 1))
        @pl.loop(0, LEN // TOK_BACK)
        def _(i):
            t = pl.ds(pl.multiple_of(i * TOK_BACK, TOK_BACK), TOK_BACK)
            c = dot(wqkv[...], gjoint[s, :, :, :, t].reshape(3 * D, TOK_BACK))
            x, r = first[s, :, t], inv1[s, :, t]
            cg = c * gain0
            inner = jnp.mean(cg * x, axis=0, keepdims=True)
            gain_part = c * x * r
            g_gain[0] += functools.reduce(jnp.add, [gain_part[:, x : x + 128] for x in range(0, TOK_BACK, 128)])
            gf = (gmid[s, :, t] + r * cg - x * (r * r * r * inner)).astype(bf16)
            gfirst[s, :, t] = gf

        add_to(m_in, dot(lifted[s], gfirst[s], 1, 1))

    flat_a[...] = jnp.zeros_like(flat_a)
    pack(m_in, "in", flat_a, A_ROWS)
    pack(m_qkv, "qkv", flat_a, A_ROWS)
    gain_rows(g_gain, flat_a)
    flat_a[pl.ds(5, 128, stride=A_ROWS), :] = jnp.broadcast_to(stats[...], (128, 128))
    all_a[...] = flat_a[...].reshape(all_a.shape)
    a.first()
    tot_b[...] = b.last()
    a.second()

    for s in (0, 1):
        out[s] = (middle[s] + dot(wdownT[...], hidden[s])).astype(bf16)
        gfeats[s] = (dot(win[...], gfirst[s]) * factor[:F, s : s + 1]).astype(bf16)
    store_out = pltpu.make_async_copy(out, out_h, sem_l.at[15])
    store_out.start()
    store_gfeats = pltpu.make_async_copy(gfeats, gfeats_h, sem_l.at[16])
    store_gfeats.start()
    tot_a[...] = a.last()
    store_out.wait()
    store_gfeats.wait()


def run_layer(feats_t, targets, lag_mask, date_mask, freq_ids, dataset_ids, weights, gains, dout_t):
    cos, sin = rope_tables()
    sd, V = jax.ShapeDtypeStruct, pltpu.VMEM
    shapes = [(ROWS[n], SPECS[n][0]) for n in NAMES]
    return pl.pallas_call(
        layer_kernel,
        in_specs=[HB] * 15,
        out_specs=[HB, HB, VM, VM],
        out_shape=[sd((2, D, LEN), bf16), sd((2, F, LEN), bf16), sd((A_ROWS, 128), f32), sd((B_ROWS, 128), f32)],
        scratch_shapes=[
            V((2, F, LEN), bf16), V((2, D, LEN), bf16), V((2, LEN), f32), V((2, NLAG), jnp.int32), V((2, NDATE), jnp.int32),
            *[pltpu.SMEM((2,), jnp.int32)] * 2,
            *[V((SPECS[n][1],), bf16) for n in NAMES], V((2, 9), bf16), V((8, LEN), f32), V((8, LEN), f32),
            V((2, D, LEN), bf16), V((2, F, LEN), bf16),
            V((A_ROWS, 128), f32), V((B_ROWS, 128), bf16),
            V((2, 64, A_ROWS, 128), f32), V((2, 16, 4, B_ROWS, 128), bf16),
            V((128 * A_ROWS, 128), f32), V((128 * B_ROWS, 128), f32),
            V((64, A_ROWS, 128), f32), V((16, 4, B_ROWS, 128), bf16),
            V((64, A_ROWS, 128), f32), V((16, 4, B_ROWS, 128), bf16),
            V((4, B_ROWS, 128), bf16),
            *[V(tiled(n), f32) for n in NAMES], *[V(s, bf16) for s in shapes], *[V(s[::-1], bf16) for s in shapes],
            V((D, 2), f32), V((2, D, 128), f32), V((128, 8), f32), V((1, 128), f32),
            V((2, F, LEN), bf16), V((2, D, LEN), f32), V((2, 1, LEN), f32), V((2, D, LEN), bf16),
            V((2, H, HD, LEN), bf16), V((2, H, HD, LEN), bf16), V((2, H, HD, LEN), bf16),
            *[V((H, (j + 1) * BLOCK, 2 * BLOCK), bf16) for j in range(LEN // BLOCK)],
            V((2, LEN, 2 * BLOCK), f32), V((2, H, 1, LEN), f32), V((2, H, HD, LEN), f32), V((2, H, HD, LEN), bf16),
            V((2, D, LEN), f32), V((D, LEN), bf16), V((2, FF, LEN), bf16), V((2 * FF, LEN), bf16),
            V((2, D, LEN), f32), V((D, LEN), bf16), V((2, H, HD, LEN), f32), V((2, 3, H, HD, LEN), bf16), V((2, D, LEN), bf16),
            V((2, LEN, 2 * BLOCK), bf16), V((GROUP, 2, HD, LEN), f32), *[V((GROUP, 2 * HD, LEN), f32)] * 2,
            *[pltpu.SemaphoreType.DMA((2, 3))] * 4, pltpu.SemaphoreType.DMA((17,)), *[pltpu.SemaphoreType.REGULAR] * 2,
        ],
        compiler_params=pltpu.CompilerParams(collective_id=0, has_side_effects=True, vmem_limit_bytes=63 * 2**20),
    )(feats_t, targets, lag_mask, date_mask, freq_ids, dataset_ids, *weights, gains, dout_t, jnp.asarray(cos), jnp.asarray(sin))


def finish_kernel(out_h, gfeats_h, tot_a_h, tot_b_h, running_h, out, gfeats, o_in, o_qkv, o_out, o_gu, o_down, o_gain, o_running,
                  out_v, gfeats_v, tot_a, tot_b, running, sems):
    pairs = ((tot_a_h, tot_a), (tot_b_h, tot_b), (running_h, running), (out_h, out_v), (gfeats_h, gfeats_v))
    copies = [pltpu.make_async_copy(src, dst, sems.at[i]) for i, (src, dst) in enumerate(pairs)]
    stores = [pltpu.make_async_copy(src, dst, sems.at[5 + i]) for i, (src, dst) in enumerate(((out_v, out), (gfeats_v, gfeats)))]
    for copy in copies:
        copy.start()
    for copy in copies:
        copy.wait()
    for store in stores:
        store.start()
    for name, ref in (("in", o_in), ("qkv", o_qkv), ("out", o_out), ("gu", o_gu), ("down", o_down)):
        _, chunk, _, _, which, base = SPECS[name]
        for t, at, width in lane_tiles(chunk):
            ref[pl.ds(at, width)] = (tot_a if which == "a" else tot_b)[base + t, :width]
    o_gain[0:1, :] = tot_a[0:1, 108:117]
    o_gain[1:2, :] = tot_a[0:1, 117:126]
    sums, counts = tot_a[5, :NSET], tot_a[5, NSET : 2 * NSET]
    old = running[...]
    o_running[...] = jnp.where(counts > 0.5, 0.75 * old + 0.25 * (sums / jnp.maximum(counts, 1.0)), old)
    for store in stores:
        store.wait()


def hand_out(out, gfeats, tot_a, tot_b, running):
    sd, V = jax.ShapeDtypeStruct, pltpu.VMEM
    return pl.pallas_call(
        finish_kernel,
        in_specs=[HB] * 5,
        out_specs=[HB, HB] + [VM] * 7,
        out_shape=[sd((2, D, LEN), bf16), sd((2, F, LEN), bf16)]
        + [sd((SPECS[n][1],), f32) for n in NAMES] + [sd((2, 9), f32), sd((NSET,), f32)],
        scratch_shapes=[V((2, D, LEN), bf16), V((2, F, LEN), bf16), V((A_ROWS, 128), f32), V((B_ROWS, 128), f32), V((NSET,), f32),
                        pltpu.SemaphoreType.DMA((7,))],
        compiler_params=pltpu.CompilerParams(vmem_limit_bytes=60 * 2**20),
    )(out, gfeats, tot_a, tot_b, running)


def body(feats, targets, lag_mask, date_mask, freq_ids, dataset_ids, w_in, w_qkv, w_out, w_gu, w_down, gains, running, d_out):
    done = run_layer(
        jnp.swapaxes(feats, 1, 2), targets, lag_mask, date_mask, freq_ids, dataset_ids,
        (w_in, w_qkv, w_out, w_gu, w_down), gains, jnp.swapaxes(d_out, 1, 2),
    )
    out, gfeats, *rest = hand_out(*done, running)
    return (jnp.swapaxes(out, 1, 2), jnp.swapaxes(gfeats, 1, 2), *rest)


def solution(mesh):
    flat, rows, cube = P(BOTH), P(BOTH, None), P(BOTH, None, None)
    return jax.shard_map(
        body,
        mesh=mesh,
        in_specs=(cube, rows, rows, rows, flat, flat, flat, flat, flat, flat, flat, P(None, "dp"), P(), cube),
        out_specs=(cube, cube, flat, flat, flat, flat, flat, P(None, "dp"), P()),
        check_vma=False,
    )
```
